32 devices in a mesh: half: 2 (over x), mp: 4 (over y, core), batch: 4 (over z).
Axes of the slice: x: 2, y: 2, z: 4, core: 2. Of those that a mesh axis runs over, the one named last changes fastest.
Arguments:
- tokens: int32 [2, 4, 4, 256], replicated, may hold values from 0 to 151935
- lengths: int32 [2, 4], replicated, may hold values from 512 to 1024
- labels: int32 [2, 4], replicated, may hold values 0 or 1
- scored: int32 [2, 4, 4, 16], replicated, may hold values from 0 to 254, as said below
- qkv_weight: float32 [896, 1152], P(('half', 'mp', 'batch')), may hold values from -0.1875 to 0.1875
- out_weight: float32 [896, 896], P(('half', 'mp', 'batch')), may hold values from -0.75 to 0.75
- gu_weight: float32 [896, 9728], P(('half', 'mp', 'batch')), may hold values from -0.1875 to 0.1875
- down_weight: float32 [4864, 896], P(('half', 'mp', 'batch')), may hold values from -0.078125 to 0.078125
- embed_weight: float32 [151936, 896], P(('half', 'mp', 'batch')), may hold values from -0.25 to 0.25
- small_params: float32 [30, 128], P(None, ('half', 'mp', 'batch'))
- moment_qkv: float32 [896, 1152], P(('half', 'mp', 'batch')), may hold values from -4.5776367e-05 to 4.5776367e-05
- moment_out: float32 [896, 896], P(('half', 'mp', 'batch')), may hold values from -4.5776367e-05 to 4.5776367e-05
- moment_gu: float32 [896, 9728], P(('half', 'mp', 'batch')), may hold values from -4.5776367e-05 to 4.5776367e-05
- moment_down: float32 [4864, 896], P(('half', 'mp', 'batch')), may hold values from -4.5776367e-05 to 4.5776367e-05
- moment_embed: float32 [151936, 896], P(('half', 'mp', 'batch')), may hold values from -4.5776367e-05 to 4.5776367e-05
- moment_small: float32 [30, 128], P(None, ('half', 'mp', 'batch')), may hold values from -0.00018310547 to 0.00018310547
- square_qkv: float32 [896, 1152], P(('half', 'mp', 'batch')), may hold values from 6.5e-11 to 2.6e-10
- square_out: float32 [896, 896], P(('half', 'mp', 'batch')), may hold values from 6.5e-11 to 2.6e-10
- square_gu: float32 [896, 9728], P(('half', 'mp', 'batch')), may hold values from 6.5e-11 to 2.6e-10
- square_down: float32 [4864, 896], P(('half', 'mp', 'batch')), may hold values from 6.5e-11 to 2.6e-10
- square_embed: float32 [151936, 896], P(('half', 'mp', 'batch')), may hold values from 6.5e-11 to 2.6e-10
- square_small: float32 [30, 128], P(None, ('half', 'mp', 'batch')), may hold values from 1e-09 to 4e-09
- ref_qkv: bfloat16 [896, 1152], P(('half', 'mp', 'batch')), may hold values from -0.1875 to 0.1875
- ref_out: bfloat16 [896, 896], P(('half', 'mp', 'batch')), may hold values from -0.75 to 0.75
- ref_gu: bfloat16 [896, 9728], P(('half', 'mp', 'batch')), may hold values from -0.1875 to 0.1875
- ref_down: bfloat16 [4864, 896], P(('half', 'mp', 'batch')), may hold values from -0.078125 to 0.078125
- ref_embed: bfloat16 [151936, 896], P(('half', 'mp', 'batch')), may hold values from -0.25 to 0.25
- ref_small: bfloat16 [30, 128], P(None, ('half', 'mp', 'batch'))
Outputs:
- new_qkv: float32 [896, 1152], P(('half', 'mp', 'batch'))
- new_out: float32 [896, 896], P(('half', 'mp', 'batch'))
- new_gu: float32 [896, 9728], P(('half', 'mp', 'batch'))
- new_down: float32 [4864, 896], P(('half', 'mp', 'batch'))
- new_embed: float32 [151936, 896], P(('half', 'mp', 'batch'))
- clipped_small: float32 [30, 128], P(None, ('half', 'mp', 'batch'))
- next_moment_qkv: float32 [896, 1152], P(('half', 'mp', 'batch'))
- next_moment_out: float32 [896, 896], P(('half', 'mp', 'batch'))
- next_moment_gu: float32 [896, 9728], P(('half', 'mp', 'batch'))
- next_moment_down: float32 [4864, 896], P(('half', 'mp', 'batch'))
- next_moment_embed: float32 [151936, 896], P(('half', 'mp', 'batch'))
- next_moment_small: float32 [30, 128], P(None, ('half', 'mp', 'batch'))
- next_square_qkv: float32 [896, 1152], P(('half', 'mp', 'batch'))
- next_square_out: float32 [896, 896], P(('half', 'mp', 'batch'))
- next_square_gu: float32 [896, 9728], P(('half', 'mp', 'batch'))
- next_square_down: float32 [4864, 896], P(('half', 'mp', 'batch'))
- next_square_embed: float32 [151936, 896], P(('half', 'mp', 'batch'))
- next_square_small: float32 [30, 128], P(None, ('half', 'mp', 'batch'))
- low_qkv: bfloat16 [896, 1152], P(('half', 'mp', 'batch'))
- low_out: bfloat16 [896, 896], P(('half', 'mp', 'batch'))
- low_gu: bfloat16 [896, 9728], P(('half', 'mp', 'batch'))
- low_down: bfloat16 [4864, 896], P(('half', 'mp', 'batch'))
- low_embed: bfloat16 [151936, 896], P(('half', 'mp', 'batch'))
- grad_norm: float32 [], replicated
The draws below stay inside these ranges and needn't reach their ends.
Inputs may be any that keep to these rules, and one draw needn't show every extreme that they name: `scored`: the 16 entries of each block are distinct and increasing.
All inputs are finite; a program needn't handle non-finite values.
Results may differ from the reference program's by a relative error of at most 0.018.
Values may be sent and summed in bfloat16 or wider, within the bound.
A program may use at most 512 MiB of HBM per device.

```python
import math
import jax
import jax.numpy as jnp
import numpy as np
from jax import lax

MODEL_WIDTH = 896
QUERY_HEADS = 14
KEY_VALUE_HEADS = 2
HEAD_SIZE = 64
FF = 4864
VOC = 151936
TOK = 256
P_SIZE = 16
MICRO = 2
STEP = 5
QKV = 1152
SMALL_ROWS = 30
ROLLOUT_LENGTH = 1024
N_MP = 4
N_BATCH = 4


def draw_scored(key, part):
    noise = jax.random.randint(key, (MICRO, N_MP, N_BATCH, TOK - 1), 0, 1 << 20)
    keyed = noise * TOK + jnp.arange(TOK - 1, dtype=jnp.int32)
    order = jnp.argsort(keyed, axis=-1)
    return jnp.sort(order[..., :P_SIZE], axis=-1).astype(jnp.int32)


def small_values(key):
    gain_key = jax.random.fold_in(key, 11)
    bias_key = jax.random.fold_in(key, 12)
    gains = 1.0 + 0.1 * jax.random.normal(gain_key, (3 * MODEL_WIDTH,), jnp.float32)
    biases = 0.5 * jax.random.normal(bias_key, (QKV,), jnp.float32)
    return jnp.concatenate([gains, biases]).reshape(SMALL_ROWS, 128)


def draw_small_params(key, part):
    return small_values(jax.random.fold_in(key, 1))


def draw_ref_small(key, part):
    return small_values(jax.random.fold_in(key, 2)).astype(jnp.bfloat16)


def touch_ends(array, own_key, low, high):
    extent = array.shape
    spot = [jax.random.randint(jax.random.fold_in(own_key, axis), (), 0, extent[axis]) for axis in range(len(extent))]
    array = array.at[tuple(spot)].set(low)
    longest = extent.index(max(extent))
    spot[longest] = (spot[longest] + 1) % extent[longest]
    return array.at[tuple(spot)].set(high)


def block_levels(key, extent, split, smallest, top_value):
    loudness, own = 1.0, jax.random.fold_in(key, 6)
    for position, parts in split:
        heights = jnp.exp(jax.random.uniform(jax.random.fold_in(own, position), (parts,), jnp.float32, smallest / len(split), top_value / len(split)))
        loudness = loudness * jnp.repeat(heights, extent[position] // parts).reshape([-1 if axis == position else 1 for axis in range(len(extent))])
    return loudness


def ranked_wide(key, shape, number_of, lean):
    portions = [min(1 << octave, number_of + 1 - (1 << octave)) * (1 << 20) // math.isqrt((1 << octave) ** lean) + 1 for octave in range((number_of + 1).bit_length()) if 1 << octave <= number_of]
    scale = 1 + sum(portions) // (1 << 30)
    listing = np.cumsum(np.array([max(1, weight // scale) for weight in portions]))
    pick = jax.random.randint(jax.random.fold_in(key, 1), shape, 0, int(listing[len(portions) - 1]))
    start = jnp.left_shift(1, jnp.searchsorted(jnp.asarray(listing, jnp.int32), pick, side="right").astype(jnp.int32))
    standing = start - 1 + jax.random.randint(jax.random.fold_in(key, 4), shape, 0, 1 << 30) % jnp.minimum(start, number_of + 1 - start)
    return jax.random.permutation(jax.random.fold_in(key, 2), number_of)[standing].astype(jnp.int32)


def scatter_about(key, extent, width, bound, split=(), held_as=jnp.bfloat16):
    level = block_levels(key, extent, split, -0.22, 0.18) if split else 1.0
    array = jax.random.normal(key, extent, jnp.float32) * width * level
    return jnp.minimum(jnp.maximum(array, -bound), bound).astype(held_as)


def setup_inputs(seed: int = 0) -> dict:
    arg_keys = jax.random.split(jax.random.key(seed), 29)
    tokens = touch_ends(ranked_wide(arg_keys[0], (MICRO, N_MP, N_BATCH, TOK), VOC, 2), jax.random.fold_in(arg_keys[0], 3), 0, VOC - 1).astype(jnp.int32)
    lengths = touch_ends(jax.random.randint(arg_keys[1], (MICRO, N_BATCH), ROLLOUT_LENGTH // 2, ROLLOUT_LENGTH + 1), jax.random.fold_in(arg_keys[1], 1), ROLLOUT_LENGTH // 2, ROLLOUT_LENGTH).astype(jnp.int32)
    labels = touch_ends((jax.random.randint(arg_keys[2], (MICRO, N_BATCH), 0, 4) < 1).astype(jnp.int32), jax.random.fold_in(arg_keys[2], 1), 0, 1)
    scored = draw_scored(jax.random.fold_in(arg_keys[28], 71), 0)
    qkv_weight = scatter_about(arg_keys[4], (MODEL_WIDTH, QKV), MODEL_WIDTH ** -0.5, 0.1875, ((0, 32),), jnp.float32)
    out_weight = scatter_about(arg_keys[5], (MODEL_WIDTH, MODEL_WIDTH), (MODEL_WIDTH // 16) ** -0.5, 0.75, ((0, 32),), jnp.float32)
    gu_weight = scatter_about(arg_keys[6], (MODEL_WIDTH, 2 * FF), MODEL_WIDTH ** -0.5, 0.1875, ((0, 32),), jnp.float32)
    down_weight = scatter_about(arg_keys[7], (FF, MODEL_WIDTH), FF ** -0.5, 0.078125, ((0, 32),), jnp.float32)
    embed_weight = scatter_about(arg_keys[8], (VOC, MODEL_WIDTH), (MODEL_WIDTH // 2) ** -0.5, 0.25, ((0, 32),), jnp.float32)
    small_params = draw_small_params(jax.random.fold_in(arg_keys[28], 71), 0)
    moment_qkv = scatter_about(arg_keys[10], (MODEL_WIDTH, QKV), (8e-6), 4.57763671875e-05, ((0, 32),), jnp.float32)
    moment_out = scatter_about(arg_keys[11], (MODEL_WIDTH, MODEL_WIDTH), (8e-6), 4.57763671875e-05, ((0, 32),), jnp.float32)
    moment_gu = scatter_about(arg_keys[12], (MODEL_WIDTH, 2 * FF), (8e-6), 4.57763671875e-05, ((0, 32),), jnp.float32)
    moment_down = scatter_about(arg_keys[13], (FF, MODEL_WIDTH), (8e-6), 4.57763671875e-05, ((0, 32),), jnp.float32)
    moment_embed = scatter_about(arg_keys[14], (VOC, MODEL_WIDTH), (8e-6), 4.57763671875e-05, ((0, 32),), jnp.float32)
    moment_small = scatter_about(arg_keys[15], (SMALL_ROWS, 128), (3e-5), 0.00018310547, ((1, 32),), jnp.float32)
    square_qkv = jnp.clip(jnp.exp(math.log(2.5999999375692084e-10) - 1.3862944 * jax.random.uniform(arg_keys[16], (MODEL_WIDTH, QKV), jnp.float32) ** block_levels(arg_keys[16], (MODEL_WIDTH, QKV), ((0, 32),), -0.2, 0.2)), 6.499999843923021e-11, 2.5999999375692084e-10)
    square_out = jnp.clip(jnp.exp(math.log(2.5999999375692084e-10) - 1.3862944 * jax.random.uniform(arg_keys[17], (MODEL_WIDTH, MODEL_WIDTH), jnp.float32) ** block_levels(arg_keys[17], (MODEL_WIDTH, MODEL_WIDTH), ((0, 32),), -0.2, 0.2)), 6.499999843923021e-11, 2.5999999375692084e-10)
    square_gu = jnp.clip(jnp.exp(math.log(2.5999999375692084e-10) - 1.3862944 * jax.random.uniform(arg_keys[18], (MODEL_WIDTH, 2 * FF), jnp.float32) ** block_levels(arg_keys[18], (MODEL_WIDTH, 2 * FF), ((0, 32),), -0.2, 0.2)), 6.499999843923021e-11, 2.5999999375692084e-10)
    square_down = jnp.clip(jnp.exp(math.log(2.5999999375692084e-10) - 1.3862944 * jax.random.uniform(arg_keys[19], (FF, MODEL_WIDTH), jnp.float32) ** block_levels(arg_keys[19], (FF, MODEL_WIDTH), ((0, 32),), -0.2, 0.2)), 6.499999843923021e-11, 2.5999999375692084e-10)
    square_embed = jnp.clip(jnp.exp(math.log(2.5999999375692084e-10) - 1.3862944 * jax.random.uniform(arg_keys[20], (VOC, MODEL_WIDTH), jnp.float32) ** block_levels(arg_keys[20], (VOC, MODEL_WIDTH), ((0, 32),), -0.2, 0.2)), 6.499999843923021e-11, 2.5999999375692084e-10)
    square_small = jnp.clip(jnp.exp(math.log(3.999999886872274e-09) - 1.3862944 * jax.random.uniform(arg_keys[21], (SMALL_ROWS, 128), jnp.float32) ** block_levels(arg_keys[21], (SMALL_ROWS, 128), ((1, 32),), -0.2, 0.2)), 9.999999717180685e-10, 3.999999886872274e-09)
    ref_qkv = scatter_about(arg_keys[22], (MODEL_WIDTH, QKV), MODEL_WIDTH ** -0.5, 0.1875, ((0, 32),))
    ref_out = scatter_about(arg_keys[23], (MODEL_WIDTH, MODEL_WIDTH), (MODEL_WIDTH // 16) ** -0.5, 0.75, ((0, 32),))
    ref_gu = scatter_about(arg_keys[24], (MODEL_WIDTH, 2 * FF), MODEL_WIDTH ** -0.5, 0.1875, ((0, 32),))
    ref_down = scatter_about(arg_keys[25], (FF, MODEL_WIDTH), FF ** -0.5, 0.078125, ((0, 32),))
    ref_embed = scatter_about(arg_keys[26], (VOC, MODEL_WIDTH), (MODEL_WIDTH // 2) ** -0.5, 0.25, ((0, 32),))
    ref_small = draw_ref_small(jax.random.fold_in(arg_keys[28], 71), 0)
    return {"tokens": tokens, "lengths": lengths, "labels": labels, "scored": scored, "qkv_weight": qkv_weight, "out_weight": out_weight, "gu_weight": gu_weight, "down_weight": down_weight, "embed_weight": embed_weight, "small_params": small_params, "moment_qkv": moment_qkv, "moment_out": moment_out, "moment_gu": moment_gu, "moment_down": moment_down, "moment_embed": moment_embed, "moment_small": moment_small, "square_qkv": square_qkv, "square_out": square_out, "square_gu": square_gu, "square_down": square_down, "square_embed": square_embed, "square_small": square_small, "ref_qkv": ref_qkv, "ref_out": ref_out, "ref_gu": ref_gu, "ref_down": ref_down, "ref_embed": ref_embed, "ref_small": ref_small}


EPS_NORM = 1e-06
THETA = 1000000.0
BETA = 0.05
CLIP = 0.1
RATE = 0.03
DECAY = 0.01
MOM1 = 0.5
MOM2 = 0.5
EPS_ADAM = 1e-08
HIGH = lax.Precision.HIGHEST

@jax.custom_vjp
def lowered_input(v):
    return lax.optimization_barrier(v.astype(jnp.bfloat16)).astype(jnp.float32)

@jax.custom_vjp
def low_back(v):
    return v

def low_keep(v):
    return (lowered_input(v), None)

def low_pass(kept, grad):
    return (grad,)

def back_keep(v):
    return (v, None)

def back_low(kept, grad):
    return (lowered_input(grad),)
lowered_input.defvjp(low_keep, low_pass)
low_back.defvjp(back_keep, back_low)

def mat(left, right):
    return jnp.dot(left, right, precision=HIGH, preferred_element_type=jnp.float32)

def rms_norm(x, gain):
    return x * lax.rsqrt(lax.optimization_barrier(jnp.mean(x * x, axis=-1, keepdims=True)) + EPS_NORM) * gain

def apply_rotary(x, token_positions):
    half_size = x.shape[-1] // 2
    freq = THETA ** (-(jnp.arange(half_size, dtype=jnp.float32) * 2.0) / x.shape[-1])
    angle = token_positions.astype(jnp.float32)[:, None] * freq[None, :]
    cosine_table = jnp.cos(angle)[:, None, :]
    sine_table = jnp.sin(angle)[:, None, :]
    first = x[..., :half_size]
    second = x[..., half_size:]
    return jnp.concatenate([first * cosine_table - second * sine_table, second * cosine_table + first * sine_table], axis=-1)

def attend(query_rows, key_rows, value_rows, length):
    query_group = QUERY_HEADS // KEY_VALUE_HEADS
    rows_per_block = min(512, ROLLOUT_LENGTH)
    places = jnp.arange(ROLLOUT_LENGTH)

    def block(block_start):
        expand_query = lax.dynamic_slice_in_dim(query_rows, block_start, rows_per_block, 0).reshape(rows_per_block, KEY_VALUE_HEADS, query_group, HEAD_SIZE)
        query_pos = block_start + jnp.arange(rows_per_block)
        scores = low_back(jnp.einsum('tkgd,skd->kgts', expand_query, key_rows, precision=HIGH) * HEAD_SIZE ** (-0.5))
        allowed = (places[None, :] <= query_pos[:, None]) & (places[None, :] < length)
        scores = jnp.where(allowed, scores, -1e+30)
        probs = lowered_input(jax.nn.softmax(scores, axis=-1))
        out = jnp.einsum('kgts,skd->tkgd', probs, value_rows, precision=HIGH)
        return out.reshape(rows_per_block, QUERY_HEADS * HEAD_SIZE)
    starts = jnp.arange(ROLLOUT_LENGTH // rows_per_block) * rows_per_block
    return lax.map(jax.checkpoint(block), starts).reshape(ROLLOUT_LENGTH, QUERY_HEADS * HEAD_SIZE)

def rollout_logprobs(params, ids, picks, length):
    qkv_w, out_w, gu_w, down_w, table, small = params
    flat = small.reshape(-1)
    gain_attn = flat[:MODEL_WIDTH]
    gain_mlp = flat[MODEL_WIDTH:2 * MODEL_WIDTH]
    gain_final = flat[2 * MODEL_WIDTH:3 * MODEL_WIDTH]
    bias = flat[3 * MODEL_WIDTH:]
    token_positions = jnp.arange(ROLLOUT_LENGTH)
    x = table[ids]
    normed = lowered_input(rms_norm(x, gain_attn))
    mixed_heads = low_back(mat(normed, qkv_w) + bias)
    query_rows = lowered_input(apply_rotary(mixed_heads[:, :MODEL_WIDTH].reshape(ROLLOUT_LENGTH, QUERY_HEADS, HEAD_SIZE), token_positions))
    key_rows = lowered_input(apply_rotary(mixed_heads[:, MODEL_WIDTH:MODEL_WIDTH + KEY_VALUE_HEADS * HEAD_SIZE].reshape(ROLLOUT_LENGTH, KEY_VALUE_HEADS, HEAD_SIZE), token_positions))
    value_rows = lowered_input(mixed_heads[:, MODEL_WIDTH + KEY_VALUE_HEADS * HEAD_SIZE:].reshape(ROLLOUT_LENGTH, KEY_VALUE_HEADS, HEAD_SIZE))
    attended = lowered_input(low_back(attend(query_rows, key_rows, value_rows, length)))
    x = x + low_back(mat(attended, out_w))
    normed = lowered_input(rms_norm(x, gain_mlp))
    gate_up = low_back(mat(normed, gu_w))
    hidden = lowered_input(jax.nn.silu(gate_up[:, :FF]) * gate_up[:, FF:])
    x = x + low_back(mat(hidden, down_w))
    final = lowered_input(rms_norm(x, gain_final))
    row_count = final[picks]
    logits = low_back(jnp.dot(row_count, table.T, precision=HIGH, preferred_element_type=jnp.float32))
    lse = jax.nn.logsumexp(logits, axis=-1)
    target = jnp.take_along_axis(logits, ids[picks + 1][:, None], axis=-1)[:, 0]
    return target - lse

def layout(tokens, scored, lengths):
    ids = tokens.transpose(0, 2, 1, 3).reshape(MICRO * N_BATCH, ROLLOUT_LENGTH)
    places = scored + (jnp.arange(N_MP, dtype=jnp.int32) * TOK)[None, :, None, None]
    live = (places + 1 < lengths[:, None, :, None]).astype(jnp.float32)
    picks = places.transpose(0, 2, 1, 3).reshape(MICRO * N_BATCH, N_MP * P_SIZE).astype(jnp.int32)
    valid = live.transpose(0, 2, 1, 3).reshape(MICRO * N_BATCH, N_MP * P_SIZE)
    return (ids, picks, valid, lengths.reshape(-1))

def all_logprobs(params, ids, picks, lens):
    run = jax.checkpoint(lambda args: rollout_logprobs(params, args[0], args[1], args[2]))

    def step(carry, args):
        return (carry, run(args))
    _, out = lax.scan(step, jnp.zeros((), jnp.float32), (ids, picks, lens))
    return out

def reference(tokens, lengths, labels, scored, qkv_weight, out_weight, gu_weight, down_weight, embed_weight, small_params, moment_qkv, moment_out, moment_gu, moment_down, moment_embed, moment_small, square_qkv, square_out, square_gu, square_down, square_embed, square_small, ref_qkv, ref_out, ref_gu, ref_down, ref_embed, ref_small):
    masters = (qkv_weight, out_weight, gu_weight, down_weight, embed_weight, small_params)
    firsts = (moment_qkv, moment_out, moment_gu, moment_down, moment_embed, moment_small)
    seconds = (square_qkv, square_out, square_gu, square_down, square_embed, square_small)
    frozen = tuple((w.astype(jnp.float32) for w in (ref_qkv, ref_out, ref_gu, ref_down, ref_embed, ref_small)))
    ids, picks, valid, lens = layout(tokens, scored, lengths)
    ref_lp = all_logprobs(frozen, ids, picks, lens)
    count = jnp.sum(valid)
    total = MICRO * N_MP * N_BATCH * P_SIZE
    outcome = labels.reshape(-1).astype(jnp.float32)

    def objective(params):
        rounded = tuple((lowered_input(w) for w in params))
        lp = all_logprobs(rounded, ids, picks, lens)
        reward = BETA * total / count * lax.optimization_barrier(jnp.sum(valid * (lp - ref_lp), axis=-1))
        return jnp.mean(jax.nn.softplus(reward) - outcome * reward)
    loss, pull = jax.vjp(objective, masters)
    grads = pull(jnp.ones((), jnp.float32))[0]
    norm = jnp.sqrt(sum((jnp.sum(g * g) for g in grads)))
    factor = jnp.minimum(1.0, CLIP / (norm + 1e-06))
    weights, moments, squares, lows, clips = ([], [], [], [], [])
    for w, g, m, v in zip(masters, grads, firsts, seconds):
        g = g * factor
        m_new = MOM1 * m + (1.0 - MOM1) * g
        v_new = MOM2 * v + (1.0 - MOM2) * g * g
        update = m_new / (1.0 - MOM1 ** STEP) / (jnp.sqrt(v_new / (1.0 - MOM2 ** STEP)) + EPS_ADAM)
        w_new = w - RATE * (update + DECAY * w)
        weights.append(w_new)
        moments.append(m_new)
        squares.append(v_new)
        clips.append(g)
        lows.append(w_new.astype(jnp.bfloat16))
    return (weights[0], weights[1], weights[2], weights[3], weights[4], clips[5], moments[0], moments[1], moments[2], moments[3], moments[4], moments[5], squares[0], squares[1], squares[2], squares[3], squares[4], squares[5], lows[0], lows[1], lows[2], lows[3], lows[4], norm)
```

```python
import functools

import jax
import jax.numpy as jnp
from jax import lax
from jax.experimental import pallas as pl
from jax.experimental.pallas import tpu as pltpu
from jax.sharding import PartitionSpec as P

MODEL_WIDTH = 896
QUERY_HEADS = 14
KEY_VALUE_HEADS = 2
HEAD_SIZE = 64
FF = 4864
QKV = 1152
TOK = 256
P_SIZE = 16
MICRO = 2
STEP = 5

EPS_NORM = 1e-06
THETA = 1000000.0
BETA = 0.05
CLIP = 0.1
RATE = 0.03
DECAY = 0.01
MOM1 = 0.5
MOM2 = 0.5
EPS_ADAM = 1e-08

MESH = pl.DeviceIdType.MESH

def places():
    n_mp, n_batch = lax.axis_size("mp"), lax.axis_size("batch")
    return 2, n_mp // 2, n_batch


def coords():
    mp = lax.axis_index("mp")
    return lax.axis_index("half"), mp // 2, lax.rem(mp, 2), lax.axis_index("batch")


def comm_index():
    _, n_y, n_batch = places()
    half, y, core, batch = coords()
    return ((core * 2 + half) * n_y + y) * n_batch + batch


def peers():
    _, n_y, n_batch = places()
    half, y, core, batch = coords()
    line = []
    for k in range(1, n_batch):
        to, frm = lax.rem(batch + k, n_batch), lax.rem(batch + n_batch - k, n_batch)
        line.append(({"half": half, "mp": y * 2 + core, "batch": to}, to, frm))
    plane = []
    n_plane = 2 * n_y
    spot = half * n_y + y
    for k in range(1, n_plane):
        to, frm = lax.rem(spot + k, n_plane), lax.rem(spot + n_plane - k, n_plane)
        plane.append(
            ({"half": to // n_y, "mp": lax.rem(to, n_y) * 2 + core, "batch": batch}, to, frm)
        )
    other = ({"half": half, "mp": y * 2 + (1 - core), "batch": batch}, 1 - core, 1 - core)
    return line, plane, other


def greet(line, plane, other):
    barrier = pltpu.get_barrier_semaphore()
    everyone = line + plane + [other]
    for who, _, _ in everyone:
        pl.semaphore_signal(barrier, inc=1, device_id=who, device_id_type=MESH)
    pl.semaphore_wait(barrier, len(everyone))


def push(src, dst, send_sem, recv_sem, who):
    copy = pltpu.make_async_remote_copy(
        src_ref=src,
        dst_ref=dst,
        send_sem=send_sem,
        recv_sem=recv_sem,
        device_id=who,
        device_id_type=MESH,
    )
    copy.start()
    return copy


def gather_kernel(n_arr, *refs):
    ins, outs = refs[:n_arr], refs[n_arr : 2 * n_arr]
    send_sems, recv_sems, own_sem = refs[2 * n_arr :]
    _, n_y, n_batch = places()
    half, y, core, batch = coords()
    n_plane = 2 * n_y
    spot = half * n_y + y
    line, plane, other = peers()
    greet(line, plane, other)

    def rows(i, first, count):
        size = ins[i].shape[1]
        return outs[i].at[:, pl.ds(pl.multiple_of(first * size, size), count * size), :]

    mine = (core * n_plane + spot) * n_batch + batch
    block = (core * n_plane + spot) * n_batch
    local = []
    for i in range(n_arr):
        copy = pltpu.make_async_copy(ins[i], rows(i, mine, 1), own_sem.at[i])
        copy.start()
        local.append(copy)
    pending = []
    slot = 0
    for i in range(n_arr):
        for who, _, _ in line:
            pending.append(push(ins[i], rows(i, mine, 1), send_sems.at[slot], recv_sems.at[slot], who))
            slot += 1
    for copy in local:
        copy.wait()
    for copy in pending:
        copy.wait()
    pending = []
    for i in range(n_arr):
        for who, _, _ in plane:
            pending.append(
                push(rows(i, block, n_batch), rows(i, block, n_batch), send_sems.at[slot], recv_sems.at[slot], who)
            )
            slot += 1
    last = []
    for i in range(n_arr):
        last.append(
            push(rows(i, block, n_batch), rows(i, block, n_batch), send_sems.at[slot], recv_sems.at[slot], other[0])
        )
        slot += 1
    at = 0
    for i in range(n_arr):
        for _, _, frm in plane:
            pending[at].wait_recv()
            at += 1
            first = (core * n_plane + frm) * n_batch
            last.append(
                push(rows(i, first, n_batch), rows(i, first, n_batch), send_sems.at[slot], recv_sems.at[slot], other[0])
            )
            slot += 1
    for copy in pending:
        copy.wait_send()
    for copy in last:
        copy.wait()


def gather(arrays, cid, vmem=48):
    _, n_y, n_batch = places()
    n_plane = 2 * n_y
    total = 2 * n_plane * n_batch
    n = len(arrays)
    copies = n * ((n_batch - 1) + (n_plane - 1) + n_plane)
    return pl.pallas_call(
        functools.partial(gather_kernel, n),
        out_shape=[jax.ShapeDtypeStruct((a.shape[0], a.shape[1] * total, a.shape[2]), a.dtype) for a in arrays],
        in_specs=[pl.BlockSpec(memory_space=pltpu.VMEM)] * n,
        out_specs=[pl.BlockSpec(memory_space=pltpu.VMEM)] * n,
        scratch_shapes=[
            pltpu.SemaphoreType.DMA((copies,)),
            pltpu.SemaphoreType.DMA((copies,)),
            pltpu.SemaphoreType.DMA((n,)),
        ],
        compiler_params=pltpu.CompilerParams(
            collective_id=cid, has_side_effects=True, vmem_limit_bytes=vmem * 2**20
        ),
        name=f"gather_{cid}",
    )(*arrays)


def reduce_kernel(n_arr, *refs):
    ins, outs = refs[:n_arr], refs[n_arr : 2 * n_arr]
    scr = refs[2 * n_arr : 7 * n_arr]
    send_sems, recv_sems = refs[7 * n_arr :]
    _, n_y, n_batch = places()
    half, y, core, batch = coords()
    n_plane = 2 * n_y
    spot = half * n_y + y
    line, plane, other = peers()
    greet(line, plane, other)
    f32 = jnp.float32
    slot = 0
    first = []
    for i in range(n_arr):
        core_in = scr[5 * i]
        size = core_in.shape[1]
        src = ins[i].at[:, pl.ds(pl.multiple_of((1 - core) * size, size), size), :]
        first.append(push(src, core_in, send_sems.at[slot], recv_sems.at[slot], other[0]))
        slot += 1
    pending = []
    for i in range(n_arr):
        core_in, core_sum, plane_in, plane_sum, line_in = scr[5 * i : 5 * i + 5]
        size = core_in.shape[1]
        part = plane_sum.shape[1]
        first[i].wait_recv()
        for k, (who, to, _) in enumerate(plane):
            at = pl.multiple_of(to * part, part)
            here = pl.multiple_of(core * size + to * part, part)
            core_sum[:, pl.ds(at, part), :] = (
                ins[i][:, pl.ds(here, part), :].astype(f32) + core_in[:, pl.ds(at, part), :].astype(f32)
            ).astype(core_sum.dtype)
            pending.append(
                push(core_sum.at[:, pl.ds(at, part), :], plane_in.at[k], send_sems.at[slot], recv_sems.at[slot], who)
            )
            slot += 1
    second = []
    at_copy = 0
    for i in range(n_arr):
        core_in, core_sum, plane_in, plane_sum, line_in = scr[5 * i : 5 * i + 5]
        size = core_in.shape[1]
        part = plane_sum.shape[1]
        row = line_in.shape[2]
        at = pl.multiple_of(spot * part, part)
        here = pl.multiple_of(core * size + spot * part, part)
        total = ins[i][:, pl.ds(here, part), :].astype(f32) + core_in[:, pl.ds(at, part), :].astype(f32)
        for k in range(len(plane)):
            pending[at_copy].wait_recv()
            at_copy += 1
            total = total + plane_in[k].astype(f32)
        plane_sum[...] = total.astype(plane_sum.dtype)
        for k, (who, to, _) in enumerate(line):
            src = plane_sum.at[:, pl.ds(pl.multiple_of(to * row, row), row), :]
            second.append(push(src, line_in.at[k], send_sems.at[slot], recv_sems.at[slot], who))
            slot += 1
    at_copy = 0
    for i in range(n_arr):
        core_in, core_sum, plane_in, plane_sum, line_in = scr[5 * i : 5 * i + 5]
        row = line_in.shape[2]
        total = plane_sum[:, pl.ds(pl.multiple_of(batch * row, row), row), :].astype(f32)
        for k in range(len(line)):
            second[at_copy].wait_recv()
            at_copy += 1
            total = total + line_in[k].astype(f32)
        outs[i][...] = total
    for copy in first + pending + second:
        copy.wait_send()


def reduce(arrays, cid, vmem=48):
    _, n_y, n_batch = places()
    n_plane = 2 * n_y
    total = 2 * n_plane * n_batch
    n = len(arrays)
    copies = n * (1 + (n_plane - 1) + (n_batch - 1))
    scratch = []
    for a in arrays:
        m, rows, w = a.shape
        scratch += [
            pltpu.VMEM((m, rows // 2, w), a.dtype),
            pltpu.VMEM((m, rows // 2, w), a.dtype),
            pltpu.VMEM((n_plane - 1, m, rows // (2 * n_plane), w), a.dtype),
            pltpu.VMEM((m, rows // (2 * n_plane), w), a.dtype),
            pltpu.VMEM((n_batch - 1, m, rows // total, w), a.dtype),
        ]
    return pl.pallas_call(
        functools.partial(reduce_kernel, n),
        out_shape=[jax.ShapeDtypeStruct((a.shape[0], a.shape[1] // total, a.shape[2]), jnp.float32) for a in arrays],
        in_specs=[pl.BlockSpec(memory_space=pltpu.VMEM)] * n,
        out_specs=[pl.BlockSpec(memory_space=pltpu.VMEM)] * n,
        scratch_shapes=scratch
        + [pltpu.SemaphoreType.DMA((copies,)), pltpu.SemaphoreType.DMA((copies,))],
        compiler_params=pltpu.CompilerParams(
            collective_id=cid, has_side_effects=True, vmem_limit_bytes=vmem * 2**20
        ),
        name=f"reduce_{cid}",
    )(*arrays)


HEAD_SLOTS = (0, 2, 4, 6, 1, 3, 5, 8, 10, 12, 7, 9, 11, 13)
COMBOS = ((0, 4, 0), (0, 3, 4), (4, 7, 7), (3, 7, 10))
PAIRS = QUERY_HEADS // 2
TILE = 128


def column(vector):
    return jnp.transpose(jnp.broadcast_to(vector.astype(jnp.float32), (128, 128)))


def last_last(a, b):
    return lax.dot_general(a, b, (((1,), (1,)), ((), ())), preferred_element_type=jnp.float32)


def first_first(a, b):
    return lax.dot_general(a, b, (((0,), (0,)), ((), ())), preferred_element_type=jnp.float32)


def straight(a, b):
    return jnp.dot(a, b, preferred_element_type=jnp.float32)


def lookup_kernel(
    block, span, n_ref, table_ref, frozen_ref, rows_ref, flat_ref, frow_ref,
    low_ref, picked_ref, x_ref, held, staged, sem,
):
    step = pl.program_id(0)
    f32, bf16 = jnp.float32, jnp.bfloat16
    inside = step * span + lax.broadcasted_iota(jnp.int32, (span, 1), 0) < block
    low = jnp.where(inside, table_ref[...], 0.0).astype(bf16)
    low_ref[...] = low
    at = pl.multiple_of(step * span, span)
    held[0, pl.ds(at, span), :] = low
    held[1, pl.ds(at, span), :] = jnp.where(inside, frozen_ref[...].astype(f32), 0.0).astype(bf16)

    @pl.when(step == pl.num_programs(0) - 1)
    def _():
        picked_ref[...] = jnp.zeros_like(picked_ref)
        n_rows = frow_ref.shape[0]
        n_span = held.shape[1] // span

        def tile(i, _):
            wanted = column(rows_ref[pl.ds(i, 1), :])
            match = (
                frow_ref[...].astype(f32) == jnp.broadcast_to(flat_ref[pl.ds(i, 1), :].astype(f32), (n_rows, TILE))
            )
            match = jnp.where(match, 1.0, 0.0).astype(bf16)
            wide = jnp.concatenate([wanted] * (span // 128), axis=1)
            lanes = lax.broadcasted_iota(jnp.int32, (TILE, span), 1).astype(f32)
            for model in range(2):

                def part(k, total):
                    first = pl.multiple_of(k * span, span)
                    hot = jnp.where(wide == lanes + (k * span).astype(f32), 1.0, 0.0).astype(bf16)
                    return total + straight(hot, held[model, pl.ds(first, span), :])

                found = lax.fori_loop(0, n_span, part, jnp.zeros((TILE, table_ref.shape[1]), f32)).astype(bf16)
                staged[model] = found
                picked_ref[model] = picked_ref[model] + straight(match, found).astype(bf16)
            copy = pltpu.make_async_copy(staged, x_ref.at[:, pl.ds(pl.multiple_of(i * TILE, TILE), TILE), :], sem)
            copy.start()
            copy.wait()
            return 0

        lax.fori_loop(0, (n_ref[0] + TILE - 1) // TILE, tile, 0)


def lookup(n_local, table, frozen, rows, flat, frow):
    block, width = table.shape
    span = 512
    steps = pl.cdiv(block, span)
    cap = rows.shape[0] * 128
    n_rows = frow.shape[0]
    bf16 = jnp.bfloat16
    whole = lambda shape: pl.BlockSpec(shape, lambda i: (0,) * len(shape))
    return pl.pallas_call(
        functools.partial(lookup_kernel, block, span),
        grid=(steps,),
        out_shape=[
            jax.ShapeDtypeStruct((block, width), bf16),
            jax.ShapeDtypeStruct((2, n_rows, width), bf16),
            jax.ShapeDtypeStruct((2, cap, width), bf16),
        ],
        in_specs=[
            pl.BlockSpec(memory_space=pltpu.SMEM),
            pl.BlockSpec((span, width), lambda i: (i, 0)),
            pl.BlockSpec((span, width), lambda i: (i, 0)),
            whole(rows.shape),
            whole(flat.shape),
            whole(frow.shape),
        ],
        out_specs=[
            pl.BlockSpec((span, width), lambda i: (i, 0)),
            whole((2, n_rows, width)),
            pl.BlockSpec(memory_space=pl.ANY),
        ],
        scratch_shapes=[
            pltpu.VMEM((2, steps * span, width), bf16),
            pltpu.VMEM((2, TILE, width), bf16),
            pltpu.SemaphoreType.DMA,
        ],
        compiler_params=pltpu.CompilerParams(vmem_limit_bytes=56 * 2**20),
        name="lookup",
    )(n_local, table, frozen, rows, flat, frow)


def head_pieces(both, lane):
    turned = pltpu.roll(both, 64, 1)
    low, high = lane < 64, lane >= 64
    bf16 = jnp.bfloat16
    zero = jnp.zeros_like(both)
    return (
        jnp.where(low, both, zero).astype(bf16),
        jnp.where(high, turned, zero).astype(bf16),
        jnp.where(low, turned, zero).astype(bf16),
        jnp.where(high, both, zero).astype(bf16),
    )


def turn(values, positions, freq, lane, sign):
    angle = positions * freq
    cosine, sine = jnp.cos(angle), jnp.sin(angle)
    first = lax.rem(lane, 64) < 32
    mixed = jnp.where(first, -sign * pltpu.roll(values, 96, 1), sign * pltpu.roll(values, 32, 1))
    return values * cosine + mixed * sine


def allowed_of(frow, flat, r, length):
    flat = jnp.broadcast_to(flat, frow.shape)
    return jnp.where((flat <= frow) & (flat >= r * length), 1.0, 0.0)


def attend_kernel(
    length, rp, n_ref, lo_ref, hi_ref, q_ref, x_ref, w_ref, gain_ref, bias_ref, freq_ref, frow_ref, flat_ref, pos_ref,
    o_ref, m_ref, l_ref, kv_ref, xbuf, kvbuf, m_scr, l_scr, o_scr, sem,
):
    model = pl.program_id(0)
    f32, bf16 = jnp.float32, jnp.bfloat16
    lane = lax.broadcasted_iota(jnp.int32, (TILE, 128), 1)
    lane_r = lax.broadcasted_iota(jnp.int32, (rp, 128), 1)
    m_scr[...] = jnp.full(m_scr.shape, -1e30, f32)
    l_scr[...] = jnp.zeros_like(l_scr)
    o_scr[...] = jnp.zeros_like(o_scr)

    def tile(i, _):
        at = pl.ds(pl.multiple_of(i * TILE, TILE), TILE)
        copy = pltpu.make_async_copy(x_ref.at[model, at, :], xbuf, sem.at[0])
        copy.start()
        copy.wait()
        x = xbuf[...].astype(f32)
        scale = lax.rsqrt(jnp.mean(x * x, axis=-1, keepdims=True) + EPS_NORM)
        normed = (x * scale * gain_ref[0]).astype(bf16)
        mixed = straight(normed, w_ref[0]) + bias_ref[0]
        key = turn(mixed[:, :128], column(pos_ref[pl.ds(i, 1), :]), freq_ref[...], lane, 1.0)
        key = key.astype(bf16)
        value = mixed[:, 128:].astype(bf16)
        kvbuf[...] = jnp.concatenate([key, value], axis=1)
        out = pltpu.make_async_copy(kvbuf, kv_ref.at[model, at, :], sem.at[1])
        out.start()
        keys = head_pieces(key.astype(f32), lane)
        values = head_pieces(value.astype(f32), lane)
        flat = flat_ref[pl.ds(i, 1), :]

        def rollout(r, _):
            rows = pl.ds(pl.multiple_of(r * rp, rp), rp)
            ok = allowed_of(frow_ref[rows, :], flat, r, length)[None]
            shift = (ok - 1.0) * 1e30
            alphas, adds = {}, {}
            for c, (p0, p1, s0) in enumerate(COMBOS):
                n = p1 - p0
                query = q_ref[p0:p1, rows, :].reshape(n * rp, 128)
                score = last_last(query, keys[c]).reshape(n, rp, TILE) * HEAD_SIZE ** (-0.5)
                score = score * ok + shift
                old = m_scr[s0 : s0 + n, rows, :]
                new = jnp.maximum(old, jnp.max(score, axis=-1, keepdims=True))
                m_scr[s0 : s0 + n, rows, :] = new
                alpha = jnp.exp(old - new)
                prob = jnp.exp(score - new) * ok
                l_scr[s0 : s0 + n, rows, :] = l_scr[s0 : s0 + n, rows, :] * alpha + jnp.sum(prob, axis=-1, keepdims=True)
                add = straight(prob.astype(bf16).reshape(n * rp, TILE), values[c]).reshape(n, rp, 128)
                for k in range(n):
                    alphas[p0 + k, c % 2] = alpha[k]
                    adds[p0 + k, c % 2] = add[k]
            for p in range(PAIRS):
                both = jnp.where(lane_r < 64, alphas[p, 0], alphas[p, 1])
                o_scr[p, rows, :] = o_scr[p, rows, :] * both + adds[p, 0] + adds[p, 1]
            return 0

        lax.fori_loop(lo_ref[i], hi_ref[i] + 1, rollout, 0)
        out.wait()
        return 0

    lax.fori_loop(0, (n_ref[0] + TILE - 1) // TILE, tile, 0)
    o_ref[...] = o_scr[...].astype(bf16)
    n_rows = m_scr.shape[1]
    lanes = lax.broadcasted_iota(jnp.int32, (n_rows, 128), 1)
    tops = jnp.full((n_rows, 128), -1e30, f32)
    totals = jnp.zeros((n_rows, 128), f32)
    for slot, head in enumerate(HEAD_SLOTS):
        tops = jnp.where(lanes == head, m_scr[slot], tops)
        totals = jnp.where(lanes == head, l_scr[slot], totals)
    m_ref[0] = tops
    l_ref[0] = totals


def attend(n_local, lo, hi, q, x, w, gain, bias, freq, frow, flat, pos, length, rp):
    n_rows = q.shape[1]
    width = x.shape[2]
    cap = x.shape[1]
    bf16 = jnp.bfloat16
    whole = lambda shape: pl.BlockSpec(shape, lambda i: (0,) * len(shape))
    smem = pl.BlockSpec(memory_space=pltpu.SMEM)
    anyw = pl.BlockSpec(memory_space=pl.ANY)
    model = lambda shape: pl.BlockSpec(shape, lambda i: (i, 0, 0))
    return pl.pallas_call(
        functools.partial(attend_kernel, length, rp),
        grid=(2,),
        out_shape=[
            jax.ShapeDtypeStruct((2 * PAIRS, n_rows, 128), bf16),
            jax.ShapeDtypeStruct((2, n_rows, 128), jnp.float32),
            jax.ShapeDtypeStruct((2, n_rows, 128), jnp.float32),
            jax.ShapeDtypeStruct((2, cap, 256), bf16),
        ],
        in_specs=[
            smem, smem, smem, model((PAIRS, n_rows, 128)), anyw, model((1, width, 256)), model((1, 1, width)),
            model((1, 1, 256)), whole((1, 128)), whole(frow.shape), whole(flat.shape), whole(pos.shape),
        ],
        out_specs=[model((PAIRS, n_rows, 128)), model((1, n_rows, 128)), model((1, n_rows, 128)), anyw],
        scratch_shapes=[
            pltpu.VMEM((TILE, width), bf16),
            pltpu.VMEM((TILE, 256), bf16),
            pltpu.VMEM((QUERY_HEADS, n_rows, 128), jnp.float32),
            pltpu.VMEM((QUERY_HEADS, n_rows, 128), jnp.float32),
            pltpu.VMEM((PAIRS, n_rows, 128), jnp.float32),
            pltpu.SemaphoreType.DMA((2,)),
        ],
        compiler_params=pltpu.CompilerParams(vmem_limit_bytes=60 * 2**20),
        name="attend",
    )(n_local, lo, hi, q, x, w, gain, bias, freq, frow, flat, pos)


def attend_back_kernel(
    length, rp, n_ref, lo_ref, hi_ref, q_ref, do_ref, st_ref, x_ref, kv_ref, w_ref, gain_ref, freq_ref, frow_ref, flat_ref,
    pos_ref, dq_ref, gkv_ref, gs_ref, gb_ref, dx_ref, xbuf, kvbuf, dxbuf, dq_scr, dk_scr, dv_scr, sem,
):
    f32, bf16 = jnp.float32, jnp.bfloat16
    lane = lax.broadcasted_iota(jnp.int32, (TILE, 128), 1)
    dq_scr[...] = jnp.zeros_like(dq_scr)
    gkv_ref[...] = jnp.zeros_like(gkv_ref)
    gs_ref[...] = jnp.zeros_like(gs_ref)
    gb_ref[...] = jnp.zeros_like(gb_ref)

    def tile(i, _):
        at = pl.ds(pl.multiple_of(i * TILE, TILE), TILE)
        one = pltpu.make_async_copy(x_ref.at[0, at, :], xbuf, sem.at[0])
        one.start()
        two = pltpu.make_async_copy(kv_ref.at[0, at, :], kvbuf, sem.at[1])
        two.start()
        one.wait()
        two.wait()
        keys = head_pieces(kvbuf[:, :128].astype(f32), lane)
        values = head_pieces(kvbuf[:, 128:].astype(f32), lane)
        flat = flat_ref[pl.ds(i, 1), :]
        dk_scr[...] = jnp.zeros_like(dk_scr)
        dv_scr[...] = jnp.zeros_like(dv_scr)

        def rollout(r, _):
            rows = pl.ds(pl.multiple_of(r * rp, rp), rp)
            ok = allowed_of(frow_ref[rows, :], flat, r, length)[None]
            shift = (ok - 1.0) * 1e30
            stats = st_ref[rows, :]
            adds = {}
            for c, (p0, p1, s0) in enumerate(COMBOS):
                n = p1 - p0
                heads = HEAD_SLOTS[s0 : s0 + n]
                query = q_ref[p0:p1, rows, :].reshape(n * rp, 128)
                back = do_ref[p0:p1, rows, :].reshape(n * rp, 128)
                lse = jnp.stack([stats[:, h : h + 1] for h in heads])
                delta = jnp.stack([stats[:, 16 + h : 17 + h] for h in heads])
                score = last_last(query, keys[c]).reshape(n, rp, TILE) * HEAD_SIZE ** (-0.5)
                prob = jnp.exp(score * ok + shift - lse)
                d_prob = last_last(back, values[c]).reshape(n, rp, TILE)
                d_score = (prob * (d_prob - delta)).astype(bf16).reshape(n * rp, TILE)
                add = straight(d_score, keys[c]).reshape(n, rp, 128)
                dk_scr[c] += first_first(d_score, query)
                dv_scr[c] += first_first(prob.astype(bf16).reshape(n * rp, TILE), back)
                for k in range(n):
                    adds[p0 + k, c % 2] = add[k]
            for p in range(PAIRS):
                dq_scr[p, rows, :] = dq_scr[p, rows, :] + adds[p, 0] + adds[p, 1]
            return 0

        lax.fori_loop(lo_ref[i], hi_ref[i] + 1, rollout, 0)

        def joined(scr):
            return jnp.where(lane < 64, scr[0] + pltpu.roll(scr[1], 64, 1), scr[3] + pltpu.roll(scr[2], 64, 1))

        d_key = turn(joined(dk_scr) * HEAD_SIZE ** (-0.5), column(pos_ref[pl.ds(i, 1), :]), freq_ref[...], lane, -1.0)
        d_mixed = jnp.concatenate([d_key, joined(dv_scr)], axis=1).astype(bf16)
        x = xbuf[...].astype(f32)
        scale = lax.rsqrt(jnp.mean(x * x, axis=-1, keepdims=True) + EPS_NORM)
        gain = gain_ref[0]
        normed = (x * scale * gain).astype(bf16)
        gkv_ref[...] += first_first(normed, d_mixed)
        gb_ref[...] += jnp.sum(d_mixed.astype(f32).reshape(TILE // 8, 8, 256), axis=0)
        d_normed = last_last(d_mixed, w_ref[0])
        gs_ref[...] += jnp.sum((d_normed * x * scale).reshape(TILE // 8, 8, x.shape[1]), axis=0)
        d_hat = d_normed * gain
        d_x = scale * (d_hat - x * scale * scale * jnp.mean(d_hat * x, axis=-1, keepdims=True))
        dxbuf[...] = d_x.astype(bf16)
        out = pltpu.make_async_copy(dxbuf, dx_ref.at[at, :], sem.at[2])
        out.start()
        out.wait()
        return 0

    lax.fori_loop(0, (n_ref[0] + TILE - 1) // TILE, tile, 0)
    dq_ref[...] = (dq_scr[...] * HEAD_SIZE ** (-0.5)).astype(bf16)


def attend_back(n_local, lo, hi, q, do, stats, x, kv, w, gain, freq, frow, flat, pos, length, rp):
    n_rows = q.shape[1]
    width = x.shape[2]
    cap = x.shape[1]
    bf16, f32 = jnp.bfloat16, jnp.float32
    whole = lambda shape: pl.BlockSpec(shape, lambda i: (0,) * len(shape))
    smem = pl.BlockSpec(memory_space=pltpu.SMEM)
    anyw = pl.BlockSpec(memory_space=pl.ANY)
    return pl.pallas_call(
        functools.partial(attend_back_kernel, length, rp),
        grid=(1,),
        out_shape=[
            jax.ShapeDtypeStruct((PAIRS, n_rows, 128), bf16),
            jax.ShapeDtypeStruct((width, 256), f32),
            jax.ShapeDtypeStruct((8, width), f32),
            jax.ShapeDtypeStruct((8, 256), f32),
            jax.ShapeDtypeStruct((cap, width), bf16),
        ],
        in_specs=[
            smem, smem, smem, whole((PAIRS, n_rows, 128)), whole((PAIRS, n_rows, 128)), whole((n_rows, 128)), anyw, anyw,
            whole((1, width, 256)), whole((1, 1, width)), whole((1, 128)), whole(frow.shape), whole(flat.shape),
            whole(pos.shape),
        ],
        out_specs=[
            whole((PAIRS, n_rows, 128)), whole((width, 256)), whole((8, width)), whole((8, 256)), anyw,
        ],
        scratch_shapes=[
            pltpu.VMEM((TILE, width), bf16),
            pltpu.VMEM((TILE, 256), bf16),
            pltpu.VMEM((TILE, width), bf16),
            pltpu.VMEM((PAIRS, n_rows, 128), f32),
            pltpu.VMEM((4, TILE, 128), f32),
            pltpu.VMEM((4, TILE, 128), f32),
            pltpu.SemaphoreType.DMA((3,)),
        ],
        compiler_params=pltpu.CompilerParams(vmem_limit_bytes=60 * 2**20),
        name="attend_back",
    )(n_local, lo, hi, q, do, stats, x, kv, w, gain, freq, frow, flat, pos)


def table_grad_kernel(
    block, span, kept, n_ref, dl_ref, af_ref, dxs_ref, srow_ref, rows_ref, dx_ref, g_ref, sq_ref, cache, extra, sem,
):
    step = pl.program_id(0)
    f32, bf16 = jnp.float32, jnp.bfloat16
    tiles = (n_ref[0] + TILE - 1) // TILE

    @pl.when(step == 0)
    def _():
        sq_ref[...] = jnp.zeros_like(sq_ref)

        def load(i, _):
            at = pl.ds(pl.multiple_of(i * TILE, TILE), TILE)
            copy = pltpu.make_async_copy(dx_ref.at[at, :], cache.at[at, :], sem)
            copy.start()
            copy.wait()
            return 0

        lax.fori_loop(0, jnp.minimum(tiles, kept), load, 0)

    inside = step * span + lax.broadcasted_iota(jnp.int32, (span, 1), 0) < block
    row = step * span + lax.broadcasted_iota(jnp.int32, (span, dxs_ref.shape[0]), 0)
    total = straight(jnp.where(inside, dl_ref[...].astype(f32), 0.0).astype(bf16), af_ref[...])
    hot = jnp.where(row == srow_ref[...], 1.0, 0.0).astype(bf16)
    total = total + straight(hot, dxs_ref[...])
    g_ref[...] = total
    near = step * span + lax.broadcasted_iota(jnp.int32, (span, TILE), 0)

    def tile(i, _):
        at = pl.ds(pl.multiple_of(i * TILE, TILE), TILE)
        hit = jnp.where(near == rows_ref[pl.ds(i, 1), :], 1.0, 0.0).astype(bf16)
        g_ref[...] += straight(hit, cache[at, :])
        return 0

    lax.fori_loop(0, jnp.minimum(tiles, kept), tile, 0)

    def far(i, _):
        at = pl.ds(pl.multiple_of(i * TILE, TILE), TILE)
        copy = pltpu.make_async_copy(dx_ref.at[at, :], extra, sem)
        copy.start()
        copy.wait()
        hit = jnp.where(near == rows_ref[pl.ds(i, 1), :], 1.0, 0.0).astype(bf16)
        g_ref[...] += straight(hit, extra[...])
        return 0

    lax.fori_loop(kept, tiles, far, 0)
    square = g_ref[...] * g_ref[...]
    sq_ref[...] += jnp.sum(square.reshape(span // 8, 8, square.shape[1]), axis=0)


def table_grad(n_local, dl, af, dxs, srow, rows, dx, block):
    width = af.shape[1]
    n_rows = af.shape[0]
    span = 512
    kept = min(rows.shape[0], 64)
    whole = lambda shape: pl.BlockSpec(shape, lambda i: (0,) * len(shape))
    return pl.pallas_call(
        functools.partial(table_grad_kernel, block, span, kept),
        grid=(pl.cdiv(block, span),),
        out_shape=[
            jax.ShapeDtypeStruct((block, width), jnp.float32),
            jax.ShapeDtypeStruct((8, width), jnp.float32),
        ],
        in_specs=[
            pl.BlockSpec(memory_space=pltpu.SMEM),
            pl.BlockSpec((span, n_rows), lambda i: (i, 0)),
            whole(af.shape), whole(dxs.shape), whole(srow.shape), whole(rows.shape),
            pl.BlockSpec(memory_space=pl.ANY),
        ],
        out_specs=[pl.BlockSpec((span, width), lambda i: (i, 0)), whole((8, width))],
        scratch_shapes=[
            pltpu.VMEM((kept * TILE, width), jnp.bfloat16),
            pltpu.VMEM((TILE, width), jnp.bfloat16),
            pltpu.SemaphoreType.DMA,
        ],
        compiler_params=pltpu.CompilerParams(vmem_limit_bytes=56 * 2**20),
        name="table_grad",
    )(n_local, dl, af, dxs, srow, rows, dx)


def blend(parts, lane):
    f32 = jnp.float32
    top = parts[0][1]
    for p in parts[1:]:
        top = jnp.maximum(top, p[1])
    weights = [jnp.exp(p[1] - top) for p in parts]
    total = sum(p[2] * w for p, w in zip(parts, weights))
    n_models = top.shape[0]
    planes = []
    for model in range(n_models):
        for pair in range(PAIRS):
            acc = None
            for p, w in zip(parts, weights):
                each = jnp.where(
                    lane < 64, w[model][:, 2 * pair : 2 * pair + 1], w[model][:, 2 * pair + 1 : 2 * pair + 2]
                )
                term = p[0][model * PAIRS + pair].astype(f32) * each
                acc = term if acc is None else acc + term
            planes.append(acc)
    return planes, top, total


def mix_kernel(o_ref, m_ref, l_ref, oo_ref, mo_ref, lo_ref, *rest):
    core_o, core_s, sum_o, sum_s, plane_o, plane_s, keep_o, keep_s, line_o, line_s, send_sems, recv_sems = rest
    _, n_y, n_batch = places()
    half, y, core, batch = coords()
    n_plane = 2 * n_y
    spot = half * n_y + y
    line, plane, other = peers()
    greet(line, plane, other)
    size = core_o.shape[1]
    part = keep_o.shape[1]
    row = line_o.shape[2]
    lane = lax.broadcasted_iota(jnp.int32, (part, 128), 1)
    lane_row = lax.broadcasted_iota(jnp.int32, (row, 128), 1)
    away = pl.ds(pl.multiple_of((1 - core) * size, size), size)
    slot = 0
    first = []
    for src, dst in ((o_ref.at[:, away, :], core_o), (m_ref.at[:, away, :], core_s.at[0]), (l_ref.at[:, away, :], core_s.at[1])):
        first.append(push(src, dst, send_sems.at[slot], recv_sems.at[slot], other[0]))
        slot += 1
    for copy in first:
        copy.wait_recv()

    def core_blend(to):
        at = pl.ds(pl.multiple_of(to * part, part), part)
        here = pl.ds(pl.multiple_of(core * size + to * part, part), part)
        return blend(
            [
                (o_ref[:, here, :], m_ref[:, here, :], l_ref[:, here, :]),
                (core_o[:, at, :], core_s[0, :, at, :], core_s[1, :, at, :]),
            ],
            lane,
        )

    second = []
    for k, (who, to, _) in enumerate(plane):
        planes, top, total = core_blend(to)
        for j, value in enumerate(planes):
            sum_o[k, j] = value.astype(sum_o.dtype)
        sum_s[k, 0] = top
        sum_s[k, 1] = total
        second.append(push(sum_o.at[k], plane_o.at[k], send_sems.at[slot], recv_sems.at[slot], who))
        slot += 1
        second.append(push(sum_s.at[k], plane_s.at[k], send_sems.at[slot], recv_sems.at[slot], who))
        slot += 1
    planes, top, total = core_blend(spot)
    parts = [(planes, top, total)]
    for k in range(len(plane)):
        second[2 * k].wait_recv()
        second[2 * k + 1].wait_recv()
        parts.append((plane_o[k], plane_s[k, 0], plane_s[k, 1]))
    planes, top, total = blend(parts, lane)
    for j, value in enumerate(planes):
        keep_o[j] = value.astype(keep_o.dtype)
    keep_s[0] = top
    keep_s[1] = total
    third = []
    for k, (who, to, _) in enumerate(line):
        at = pl.ds(pl.multiple_of(to * row, row), row)
        third.append(push(keep_o.at[:, at, :], line_o.at[k], send_sems.at[slot], recv_sems.at[slot], who))
        slot += 1
        third.append(push(keep_s.at[:, :, at, :], line_s.at[k], send_sems.at[slot], recv_sems.at[slot], who))
        slot += 1
    at = pl.ds(pl.multiple_of(batch * row, row), row)
    parts = [(keep_o[:, at, :], keep_s[0, :, at, :], keep_s[1, :, at, :])]
    for k in range(len(line)):
        third[2 * k].wait_recv()
        third[2 * k + 1].wait_recv()
        parts.append((line_o[k], line_s[k, 0], line_s[k, 1]))
    planes, top, total = blend(parts, lane_row)
    for j, value in enumerate(planes):
        oo_ref[j] = value
    mo_ref[...] = top
    lo_ref[...] = total
    for copy in first + second + third:
        copy.wait_send()


def mix(o, m, l, cid):
    _, n_y, n_batch = places()
    n_plane = 2 * n_y
    total = 2 * n_plane * n_batch
    planes, rows, _ = o.shape
    nm = m.shape[0]
    bf16, f32 = jnp.bfloat16, jnp.float32
    copies = 3 + 2 * (n_plane - 1) + 2 * (n_batch - 1)
    part, row = rows // (2 * n_plane), rows // total
    vm = pl.BlockSpec(memory_space=pltpu.VMEM)
    return pl.pallas_call(
        mix_kernel,
        out_shape=[
            jax.ShapeDtypeStruct((planes, row, 128), f32),
            jax.ShapeDtypeStruct((nm, row, 128), f32),
            jax.ShapeDtypeStruct((nm, row, 128), f32),
        ],
        in_specs=[vm] * 3,
        out_specs=[vm] * 3,
        scratch_shapes=[
            pltpu.VMEM((planes, rows // 2, 128), bf16),
            pltpu.VMEM((2, nm, rows // 2, 128), f32),
            pltpu.VMEM((n_plane - 1, planes, part, 128), bf16),
            pltpu.VMEM((n_plane - 1, 2, nm, part, 128), f32),
            pltpu.VMEM((n_plane - 1, planes, part, 128), bf16),
            pltpu.VMEM((n_plane - 1, 2, nm, part, 128), f32),
            pltpu.VMEM((planes, part, 128), bf16),
            pltpu.VMEM((2, nm, part, 128), f32),
            pltpu.VMEM((n_batch - 1, planes, row, 128), bf16),
            pltpu.VMEM((n_batch - 1, 2, nm, row, 128), f32),
            pltpu.SemaphoreType.DMA((copies,)),
            pltpu.SemaphoreType.DMA((copies,)),
        ],
        compiler_params=pltpu.CompilerParams(collective_id=cid, has_side_effects=True, vmem_limit_bytes=56 * 2**20),
        name="mix",
    )(o, m, l)


AXES = ("half", "mp", "batch")


def norm_forward(x, gain):
    scale = lax.rsqrt(jnp.mean(x * x, axis=-1, keepdims=True) + EPS_NORM)
    return (x * scale * gain, scale)


def norm_backward(d_out, x, scale, gain):
    d_gain = d_out * x * scale
    d_hat = d_out * gain
    d_x = scale * (d_hat - x * scale * scale * jnp.mean(d_hat * x, axis=-1, keepdims=True))
    return (d_x, d_gain)


def frequencies():
    half_size = HEAD_SIZE // 2
    return THETA ** (-(jnp.arange(half_size, dtype=jnp.float32) * 2.0) / HEAD_SIZE)


def rotate(x, cosine, sine, sign):
    half_size = HEAD_SIZE // 2
    first, second = x[..., :half_size], x[..., half_size:]
    return jnp.concatenate(
        [first * cosine - sign * second * sine, second * cosine + sign * first * sine], axis=-1
    )


def to_pairs(x):
    lead, rows = x.shape[:-2], x.shape[-2]
    x = x.reshape(lead + (rows, PAIRS, 128))
    x = jnp.moveaxis(x, -2, -3)
    return x.reshape((-1, rows, 128))


def from_pairs(x, models):
    rows = x.shape[1]
    x = x.reshape(models, PAIRS, rows, 128)
    return jnp.moveaxis(x, 1, 2).reshape(models, rows, MODEL_WIDTH)


def bmm(x, w):
    return jnp.stack([jnp.dot(x[i], w[i], preferred_element_type=jnp.float32) for i in range(2)])


def body(
    tokens, lengths, labels, scored, qkv_weight, out_weight, gu_weight, down_weight, embed_weight, small_params,
    moment_qkv, moment_out, moment_gu, moment_down, moment_embed, moment_small,
    square_qkv, square_out, square_gu, square_down, square_embed, square_small,
    ref_qkv, ref_out, ref_gu, ref_down, ref_embed, ref_small,
):
    masters = (qkv_weight, out_weight, gu_weight, down_weight, embed_weight, small_params)
    firsts = (moment_qkv, moment_out, moment_gu, moment_down, moment_embed, moment_small)
    seconds = (square_qkv, square_out, square_gu, square_down, square_embed, square_small)
    bf16, f32, i32 = jnp.bfloat16, jnp.float32, jnp.int32
    n_mp, n_batch = lax.axis_size("mp"), lax.axis_size("batch")
    devices = 2 * n_mp * n_batch
    n_y = n_mp // 2
    block = embed_weight.shape[0]
    feats = qkv_weight.shape[0]
    units = down_weight.shape[0]
    rollouts = MICRO * n_batch
    length = n_mp * TOK
    rp = n_mp * P_SIZE
    n_rows = rollouts * rp
    own_rows = n_rows // devices
    lin = lax.axis_index(AXES)
    com = comm_index()
    base = lin * block

    smalls = jnp.stack([small_params.astype(bf16).reshape(-1), ref_small.reshape(-1)])
    extra = jnp.zeros((feats, 128), bf16).at[:2, : smalls.shape[1]].set(smalls) if smalls.shape[1] <= 128 else None
    w_cat = jnp.concatenate([qkv_weight.astype(bf16), out_weight.astype(bf16), ref_qkv, ref_out, extra], axis=1)
    w_all = lax.all_gather(w_cat, AXES, axis=0, tiled=True)
    gu_both = jnp.stack([gu_weight.astype(bf16), ref_gu]).reshape(2, feats, 2, devices, units)
    gu_send = gu_both.transpose(3, 0, 1, 2, 4).reshape(devices, 2, feats, 2 * units)
    gu_cols = lax.all_to_all(gu_send, AXES, split_axis=0, concat_axis=0, tiled=True)
    gu_cols = gu_cols.transpose(1, 0, 2, 3).reshape(2, MODEL_WIDTH, 2 * units)
    w_gate, w_up = gu_cols[:, :, :units], gu_cols[:, :, units:]
    down_low = jnp.stack([down_weight.astype(bf16), ref_down])

    ids = tokens.transpose(0, 2, 1, 3).reshape(rollouts, length)
    lens = lengths.reshape(rollouts)
    spots = jnp.arange(length, dtype=i32)
    flat_ids = jnp.arange(rollouts * length, dtype=i32).reshape(rollouts, length)
    bits = max(1, (block - 1).bit_length())
    local = (ids >= base) & (ids < base + block) & (spots[None, :] < lens[:, None])
    key = jnp.where(local, (flat_ids << bits) + (ids - base), jnp.int32(2**31 - 1)).reshape(-1)
    key = lax.sort(key)
    n_local = jnp.sum(local.astype(i32))
    live = jnp.arange(rollouts * length, dtype=i32) < n_local
    row_of = jnp.where(live, key & ((1 << bits) - 1), -1).reshape(-1, TILE)
    flat_of = jnp.where(live, key >> bits, 1 << 22).reshape(-1, TILE)
    pos_of = jnp.where(live, (key >> bits) % length, 0).reshape(-1, TILE).astype(f32)
    tile_lo = flat_of[:, 0] // length
    tile_hi = jnp.max(jnp.where(live, (key >> bits) // length, -1).reshape(-1, TILE), axis=1)
    n_one = n_local.reshape(1)

    picks = scored.transpose(0, 2, 1, 3) + (jnp.arange(n_mp, dtype=i32) * TOK)[None, None, :, None]
    picks = picks.reshape(rollouts, rp)
    valid = (picks + 1 < lens[:, None]).astype(f32)
    count = jnp.sum(valid)
    here = picks[:, :, None] == spots[None, None, :]
    after = picks[:, :, None] + 1 == spots[None, None, :]
    own_ids = jnp.sum(jnp.where(here, ids[:, None, :], 0), axis=2).reshape(-1)
    targets = jnp.sum(jnp.where(after, ids[:, None, :], 0), axis=2).reshape(-1)
    owned = (own_ids >= base) & (own_ids < base + block) & (picks < lens[:, None]).reshape(-1)
    own_row = jnp.where(owned, own_ids - base, -1)
    frow = (picks + (jnp.arange(rollouts, dtype=i32) * length)[:, None]).reshape(-1)
    frow_wide = jnp.broadcast_to(frow[:, None], (n_rows, 128))

    low_table, picked, x_tok = lookup(n_one, embed_weight, ref_embed, row_of, flat_of, frow_wide)
    (x0,) = reduce([picked], 1)

    w_all3 = w_all.reshape(devices, feats, -1)
    w_qkv = jnp.stack([w_all[:, :QKV], w_all[:, QKV + MODEL_WIDTH : 2 * QKV + MODEL_WIDTH]])
    w_q, w_kv = w_qkv[:, :, :MODEL_WIDTH], w_qkv[:, :, MODEL_WIDTH:]
    w_out = jnp.stack(
        [w_all[:, QKV : QKV + MODEL_WIDTH], w_all[:, 2 * QKV + MODEL_WIDTH : 2 * QKV + 2 * MODEL_WIDTH]]
    )
    flat_small = w_all3[:, :2, 2 * QKV + 2 * MODEL_WIDTH :][:, :, : smalls.shape[1]]
    small_rows = small_params.shape[0]
    flat_small = flat_small.reshape(devices, 2, small_rows, -1).transpose(1, 2, 0, 3).reshape(2, -1).astype(f32)
    gain_attn = flat_small[:, None, :MODEL_WIDTH]
    gain_mlp = flat_small[:, None, MODEL_WIDTH : 2 * MODEL_WIDTH]
    gain_final = flat_small[:, None, 2 * MODEL_WIDTH : 3 * MODEL_WIDTH]
    bias = flat_small[:, None, 3 * MODEL_WIDTH :]

    freq = frequencies()
    my_pos = lax.dynamic_slice_in_dim(picks.reshape(-1), com * own_rows, own_rows)
    angle = my_pos.astype(f32)[:, None] * freq[None, :]
    cosine, sine = jnp.cos(angle)[:, None, :], jnp.sin(angle)[:, None, :]
    a1, scale_one = norm_forward(x0, gain_attn)
    a1 = a1.astype(bf16)
    mixed = bmm(a1, w_q) + bias[:, :, :MODEL_WIDTH]
    q = rotate(mixed.reshape(2, own_rows, QUERY_HEADS, HEAD_SIZE), cosine, sine, 1.0)
    q = to_pairs(q.reshape(2, own_rows, MODEL_WIDTH).astype(bf16))
    q_all, a1_all = gather([q, a1[:1]], 2)

    freq_wide = jnp.tile(freq, 4).reshape(1, 128)
    o_part, m_part, l_part, kv_tok = attend(
        n_one, tile_lo, tile_hi, q_all, x_tok, w_kv, gain_attn, bias[:, :, MODEL_WIDTH:], freq_wide, frow_wide, flat_of,
        pos_of, length, rp,
    )
    o_sum, top, total = mix(o_part, m_part, l_part, 3)
    lse = (top + jnp.log(total))[0]
    share = (1.0 / total)[:, :, :QUERY_HEADS]
    o = from_pairs(o_sum, 2).reshape(2, own_rows, QUERY_HEADS, HEAD_SIZE) * share[..., None]
    o = o.reshape(2, own_rows, MODEL_WIDTH).astype(bf16)
    x1 = x0 + bmm(o, w_out)
    a2, scale_two = norm_forward(x1, gain_mlp)
    a2_all, o_all = gather([a2.astype(bf16), o[:1]], 4)
    gate, up = bmm(a2_all, w_gate), bmm(a2_all, w_up)
    hidden = (jax.nn.silu(gate) * up).astype(bf16)
    (branch,) = reduce([bmm(hidden, down_low).astype(bf16)], 5)
    x2 = x1 + branch
    af, scale_final = norm_forward(x2, gain_final)
    (af_all,) = gather([af.astype(bf16)], 6)

    vocab = base + jnp.arange(block, dtype=i32)
    hit = vocab[:, None] == targets[None, :]
    tables = (low_table, ref_embed)
    logits = [
        lax.dot_general(tables[i], af_all[i], (((1,), (1,)), ((), ())), preferred_element_type=f32) for i in range(2)
    ]
    stats = []
    for i in range(2):
        peak = jnp.max(logits[i], axis=0)
        stats.append(
            jnp.stack(
                [
                    peak,
                    jnp.sum(jnp.exp(logits[i] - peak[None, :]), axis=0),
                    jnp.sum(jnp.where(hit, logits[i], 0.0), axis=0),
                ]
            )
        )
    stats = jnp.concatenate(stats, axis=0)
    stats = jnp.concatenate([stats, jnp.zeros((2, n_rows), f32)], axis=0)
    (stats_all,) = gather([stats[None]], 7)
    stats_all = stats_all.reshape(devices, 8, n_rows)
    lps, lses = [], []
    for i in range(2):
        peaks = stats_all[:, 3 * i]
        peak = jnp.max(peaks, axis=0)
        sums = jnp.sum(stats_all[:, 3 * i + 1] * jnp.exp(peaks - peak[None]), axis=0)
        lses.append(peak + jnp.log(sums))
        lps.append(jnp.sum(stats_all[:, 3 * i + 2], axis=0) - lses[i])
    ratio = (lps[0] - lps[1]).reshape(rollouts, rp)
    factor = BETA * n_rows / count
    reward = factor * jnp.sum(valid * ratio, axis=1)
    d_reward = (jax.nn.sigmoid(reward) - labels.reshape(rollouts).astype(f32)) / rollouts
    d_lp = (valid * (d_reward * factor)[:, None]).reshape(-1)

    probs = jnp.exp(logits[0] - lses[0][None, :])
    d_logits = (d_lp[None, :] * (hit.astype(f32) - probs)).astype(bf16)
    d_af = lax.dot_general(d_logits, low_table, (((0,), (0,)), ((), ())), preferred_element_type=f32)
    (d_final,) = reduce([d_af.astype(bf16)[None]], 8)
    d_out, g_gain_final = norm_backward(d_final[0], x2[0], scale_final[0], gain_final[0])
    (d_branch,) = gather([d_out.astype(bf16)[None]], 9)
    d_branch = d_branch[0]
    g_down = lax.dot_general(hidden[0], d_branch, (((0,), (0,)), ((), ())), preferred_element_type=f32)
    d_hidden = lax.dot_general(d_branch, down_low[0], (((1,), (1,)), ((), ())), preferred_element_type=f32)
    sigma = jax.nn.sigmoid(gate[0])
    d_gate = (d_hidden * up[0] * sigma * (1.0 + gate[0] * (1.0 - sigma))).astype(bf16)
    d_up = (d_hidden * gate[0] * sigma).astype(bf16)
    d_a2 = lax.dot_general(d_gate, w_gate[0], (((1,), (1,)), ((), ())), preferred_element_type=f32)
    d_a2 = d_a2 + lax.dot_general(d_up, w_up[0], (((1,), (1,)), ((), ())), preferred_element_type=f32)
    (d_normed,) = reduce([d_a2.astype(bf16)[None]], 10)
    d_mid, g_gain_mlp = norm_backward(d_normed[0], x1[0], scale_two[0], gain_mlp[0])
    d_mid = d_mid + d_out
    d_attn = d_mid.astype(bf16)
    d_o = lax.dot_general(d_attn, w_out[0], (((1,), (1,)), ((), ())), preferred_element_type=f32).astype(bf16)
    delta = jnp.sum(
        (d_o.astype(f32) * o[0].astype(f32)).reshape(own_rows, QUERY_HEADS, HEAD_SIZE), axis=-1
    )
    row_stats = jnp.concatenate(
        [lse[:, :16], delta, jnp.zeros((own_rows, 128 - 16 - QUERY_HEADS), f32)], axis=1
    )
    d_attn_all, d_o_all, row_stats_all = gather([d_attn[None], to_pairs(d_o), row_stats[None]], 11)
    d_attn_all = d_attn_all[0]

    g_gate = lax.dot_general(a2_all[0], d_gate, (((0,), (0,)), ((), ())), preferred_element_type=f32)
    g_up = lax.dot_general(a2_all[0], d_up, (((0,), (0,)), ((), ())), preferred_element_type=f32)
    g_gu = jnp.concatenate([g_gate, g_up], axis=1)
    gu_square = jnp.sum(g_gu * g_gu)
    g_gu = lax.all_to_all(
        g_gu.astype(bf16).reshape(devices, feats, 2 * units), AXES, split_axis=0, concat_axis=0, tiled=True
    )
    g_gu = g_gu.reshape(devices, feats, 2, units).transpose(1, 2, 0, 3).reshape(feats, 2 * FF).astype(f32)

    dq_part, g_kv_part, g_gain_kv, g_bias_kv, dx_tok = attend_back(
        n_one, tile_lo, tile_hi, q_all[:PAIRS], d_o_all, row_stats_all[0], x_tok, kv_tok, w_kv[:1], gain_attn[:1],
        freq_wide, frow_wide, flat_of, pos_of, length, rp,
    )
    padded = -(-feats // 16) * 16
    g_kv_part = g_kv_part.reshape(2, n_y, 2, n_batch, feats, 256).transpose(2, 0, 1, 3, 4, 5)
    g_kv_part = jnp.pad(g_kv_part.reshape(devices, feats, 256), ((0, 0), (0, padded - feats), (0, 0)))
    dq, g_kv = reduce([dq_part, g_kv_part.reshape(1, devices * padded, 256)], 12)
    g_kv = g_kv[0, :feats]
    dq = rotate(from_pairs(dq, 1).reshape(own_rows, QUERY_HEADS, HEAD_SIZE), cosine, sine, -1.0)
    dq = dq.reshape(own_rows, MODEL_WIDTH).astype(bf16)
    (dq_all,) = gather([dq[None]], 13)
    dq_all = dq_all[0]
    d_a1 = lax.dot_general(dq_all, w_q[0], (((1,), (1,)), ((), ())), preferred_element_type=f32)
    x_row = picked[0].astype(f32)
    scale_row = lax.rsqrt(jnp.mean(x_row * x_row, axis=-1, keepdims=True) + EPS_NORM)
    d_row, g_gain_row = norm_backward(d_a1, x_row, scale_row, gain_attn[0])
    d_row = jnp.where(owned[:, None], d_row + d_attn_all.astype(f32), 0.0).astype(bf16)
    g_gain_row = jnp.sum(jnp.where(owned[:, None], g_gain_row, 0.0), axis=0)

    embed_grad, embed_square = table_grad(
        n_one, d_logits, af_all[0], d_row, own_row.reshape(1, -1), row_of, dx_tok, block
    )

    def mine(rows, grads):
        cols = lax.dynamic_slice_in_dim(rows, lin * feats, feats, 1)
        return lax.dot_general(cols, grads, (((0,), (0,)), ((), ())), preferred_element_type=f32)

    g_out = mine(o_all[0], d_attn_all)
    g_q = mine(a1_all[0], dq_all)
    g_qkv = jnp.concatenate([g_q, g_kv], axis=1)

    small_part = jnp.concatenate(
        [
            jnp.sum(g_gain_kv, axis=0) + g_gain_row,
            jnp.sum(g_gain_mlp, axis=0),
            jnp.sum(g_gain_final, axis=0),
            jnp.sum(dq.astype(f32), axis=0),
            jnp.sum(g_bias_kv, axis=0),
        ]
    )
    square_part = (
        jnp.sum(g_qkv * g_qkv) + jnp.sum(g_out * g_out) + gu_square + jnp.sum(g_down * g_down) + jnp.sum(embed_square)
    )
    last = jnp.concatenate([small_part, jnp.full((128,), square_part, f32), jnp.zeros((128,), f32)]).reshape(1, -1, 128)
    (last_all,) = gather([last], 14)
    last_all = jnp.sum(last_all.reshape(devices, -1, 128), axis=0)
    g_small = last_all[:small_rows]
    norm = jnp.sqrt(jnp.sum(g_small * g_small) + last_all[small_rows, 0])
    g_small = lax.dynamic_slice_in_dim(g_small, lin * small_params.shape[1], small_params.shape[1], 1)

    owned_grads = (g_qkv, g_out, g_gu, g_down, embed_grad, g_small)
    clip = jnp.minimum(1.0, CLIP / (norm + 1e-06))
    new_weights, new_firsts, new_seconds, new_lows, clipped_list = ([], [], [], [], [])
    for w, g, m, v in zip(masters, owned_grads, firsts, seconds):
        g = g * clip
        m_new = MOM1 * m + (1.0 - MOM1) * g
        v_new = MOM2 * v + (1.0 - MOM2) * g * g
        update = m_new / (1.0 - MOM1**STEP) / (jnp.sqrt(v_new / (1.0 - MOM2**STEP)) + EPS_ADAM)
        w_new = w - RATE * (update + DECAY * w)
        new_weights.append(w_new)
        new_firsts.append(m_new)
        new_seconds.append(v_new)
        clipped_list.append(g)
        new_lows.append(w_new.astype(bf16))
    return (
        *new_weights[:5], clipped_list[5], *new_firsts, *new_seconds, *new_lows[:5], norm,
    )


def solution(mesh):
    rows, cols = P(AXES, None), P(None, AXES)
    six = (rows, rows, rows, rows, rows, cols)
    in_specs = (P(), P(), P(), P()) + six * 4
    out_specs = six * 3 + (rows,) * 5 + (P(),)
    return jax.shard_map(body, mesh=mesh, in_specs=in_specs, out_specs=out_specs, check_vma=False)
```

```python
import functools

import jax
import jax.numpy as jnp
from jax import lax
from jax.experimental import pallas as pl
from jax.experimental.pallas import tpu as pltpu
from jax.sharding import PartitionSpec as P

MODEL_WIDTH = 896
QUERY_HEADS = 14
KEY_VALUE_HEADS = 2
HEAD_SIZE = 64
FF = 4864
QKV = 1152
TOK = 256
P_SIZE = 16
MICRO = 2
STEP = 5

EPS_NORM = 1e-06
THETA = 1000000.0
BETA = 0.05
CLIP = 0.1
RATE = 0.03
DECAY = 0.01
MOM1 = 0.5
MOM2 = 0.5
EPS_ADAM = 1e-08

MESH = pl.DeviceIdType.MESH

def places():
    n_mp, n_batch = lax.axis_size("mp"), lax.axis_size("batch")
    return 2, n_mp // 2, n_batch


def coords():
    mp = lax.axis_index("mp")
    return lax.axis_index("half"), mp // 2, lax.rem(mp, 2), lax.axis_index("batch")


def comm_index():
    _, n_y, n_batch = places()
    half, y, core, batch = coords()
    return ((core * 2 + half) * n_y + y) * n_batch + batch


def peers():
    _, n_y, n_batch = places()
    half, y, core, batch = coords()
    line = []
    for k in range(1, n_batch):
        to, frm = lax.rem(batch + k, n_batch), lax.rem(batch + n_batch - k, n_batch)
        line.append(({"half": half, "mp": y * 2 + core, "batch": to}, to, frm))
    plane = []
    n_plane = 2 * n_y
    spot = half * n_y + y
    for k in range(1, n_plane):
        to, frm = lax.rem(spot + k, n_plane), lax.rem(spot + n_plane - k, n_plane)
        plane.append(
            ({"half": to // n_y, "mp": lax.rem(to, n_y) * 2 + core, "batch": batch}, to, frm)
        )
    other = ({"half": half, "mp": y * 2 + (1 - core), "batch": batch}, 1 - core, 1 - core)
    return line, plane, other


def greet(line, plane, other):
    barrier = pltpu.get_barrier_semaphore()
    everyone = line + plane + [other]
    for who, _, _ in everyone:
        pl.semaphore_signal(barrier, inc=1, device_id=who, device_id_type=MESH)
    pl.semaphore_wait(barrier, len(everyone))


def push(src, dst, send_sem, recv_sem, who):
    copy = pltpu.make_async_remote_copy(
        src_ref=src,
        dst_ref=dst,
        send_sem=send_sem,
        recv_sem=recv_sem,
        device_id=who,
        device_id_type=MESH,
    )
    copy.start()
    return copy


def gather_kernel(n_arr, *refs):
    ins, outs = refs[:n_arr], refs[n_arr : 2 * n_arr]
    send_sems, recv_sems, own_sem = refs[2 * n_arr :]
    _, n_y, n_batch = places()
    half, y, core, batch = coords()
    n_plane = 2 * n_y
    spot = half * n_y + y
    line, plane, other = peers()
    greet(line, plane, other)
    slots = iter(range(n_arr * (n_batch - 1 + n_plane * n_batch + (n_plane - 1) * n_batch)))

    def rows(i, where, j):
        size = ins[i].shape[1]
        at = (core * n_plane + where) * n_batch + lax.rem(batch + n_batch - j, n_batch)
        return outs[i].at[:, pl.ds(pl.multiple_of(at * size, size), size), :]

    def send(src, dst, who):
        slot = next(slots)
        return push(src, dst, send_sems.at[slot], recv_sems.at[slot], who)

    local, by_line, by_plane, by_core = [], [], [], []
    for i in range(n_arr):
        by_line.append([send(ins[i], rows(i, spot, 0), who) for who, _, _ in line])
    for i in range(n_arr):
        by_plane.append([[send(ins[i], rows(i, spot, 0), who) for who, _, _ in plane]])
        by_core.append(send(ins[i], rows(i, spot, 0), other[0]))
        copy = pltpu.make_async_copy(ins[i], rows(i, spot, 0), own_sem.at[i])
        copy.start()
        local.append(copy)
    for j in range(1, n_batch):
        for i in range(n_arr):
            by_line[i][j - 1].wait_recv()
            by_plane[i].append([send(rows(i, spot, j), rows(i, spot, j), who) for who, _, _ in plane])
            by_core.append(send(rows(i, spot, j), rows(i, spot, j), other[0]))
    for j in range(n_batch):
        for i in range(n_arr):
            for k, (_, _, frm) in enumerate(plane):
                by_plane[i][j][k].wait_recv()
                by_core.append(send(rows(i, frm, j), rows(i, frm, j), other[0]))
    for copy in local:
        copy.wait()
    for copy in by_core:
        copy.wait_recv()
    for i in range(n_arr):
        for copy in by_line[i] + sum(by_plane[i], []):
            copy.wait_send()
    for copy in by_core:
        copy.wait_send()


def gather(arrays, cid, vmem=48):
    _, n_y, n_batch = places()
    n_plane = 2 * n_y
    total = 2 * n_plane * n_batch
    n = len(arrays)
    copies = n * ((n_batch - 1) + (n_plane - 1) * n_batch + n_plane * n_batch)
    return pl.pallas_call(
        functools.partial(gather_kernel, n),
        out_shape=[jax.ShapeDtypeStruct((a.shape[0], a.shape[1] * total, a.shape[2]), a.dtype) for a in arrays],
        in_specs=[pl.BlockSpec(memory_space=pltpu.VMEM)] * n,
        out_specs=[pl.BlockSpec(memory_space=pltpu.VMEM)] * n,
        scratch_shapes=[
            pltpu.SemaphoreType.DMA((copies,)),
            pltpu.SemaphoreType.DMA((copies,)),
            pltpu.SemaphoreType.DMA((n,)),
        ],
        compiler_params=pltpu.CompilerParams(
            collective_id=cid, has_side_effects=True, vmem_limit_bytes=vmem * 2**20
        ),
        name=f"gather_{cid}",
    )(*arrays)


def reduce_kernel(n_arr, *refs):
    ins, outs = refs[:n_arr], refs[n_arr : 2 * n_arr]
    scr = refs[2 * n_arr : 7 * n_arr]
    send_sems, recv_sems = refs[7 * n_arr :]
    _, n_y, n_batch = places()
    half, y, core, batch = coords()
    n_plane = 2 * n_y
    spot = half * n_y + y
    line, plane, other = peers()
    greet(line, plane, other)
    f32 = jnp.float32
    slots = iter(range(n_arr * (n_plane * n_batch + (n_plane - 1) * n_batch + n_batch - 1)))
    order = list(range(1, n_batch)) + [0]
    spots = [to for _, to, _ in plane] + [spot]

    def send(src, dst, who):
        slot = next(slots)
        return push(src, dst, send_sems.at[slot], recv_sems.at[slot], who)

    def rows(i, side, where, j):
        size = outs[i].shape[1]
        at = (side * n_plane + where) * n_batch + lax.rem(batch + j, n_batch)
        return pl.ds(pl.multiple_of(at * size, size), size)

    by_core, by_plane, by_line = {}, {}, {}
    for j in order:
        for p in range(n_plane):
            for i in range(n_arr):
                src = ins[i].at[:, rows(i, 1 - core, spots[p], j), :]
                by_core[i, p, j] = send(src, scr[5 * i].at[p, j], other[0])

    def mine(i, p, j):
        by_core[i, p, j].wait_recv()
        return ins[i][:, rows(i, core, spots[p], j), :].astype(f32) + scr[5 * i][p, j].astype(f32)

    for j in order:
        for p in range(n_plane - 1):
            for i in range(n_arr):
                out = scr[5 * i + 1]
                out[p, j] = mine(i, p, j).astype(out.dtype)
                by_plane[i, p, j] = send(out.at[p, j], scr[5 * i + 2].at[p, j], plane[p][0])
    totals = {}
    for j in order:
        for i in range(n_arr):
            total = mine(i, n_plane - 1, j)
            for p in range(n_plane - 1):
                by_plane[i, p, j].wait_recv()
                total = total + scr[5 * i + 2][p, j].astype(f32)
            if j:
                out = scr[5 * i + 3]
                out[j - 1] = total.astype(out.dtype)
                by_line[i, j] = send(out.at[j - 1], scr[5 * i + 4].at[j - 1], line[j - 1][0])
            else:
                outs[i][...] = total
    for i in range(n_arr):
        for j in range(1, n_batch):
            by_line[i, j].wait_recv()
            outs[i][...] += scr[5 * i + 4][j - 1].astype(f32)
    for group in (by_core, by_plane, by_line):
        for copy in group.values():
            copy.wait_send()


def reduce(arrays, cid, vmem=48):
    _, n_y, n_batch = places()
    n_plane = 2 * n_y
    total = 2 * n_plane * n_batch
    n = len(arrays)
    copies = n * (n_plane * n_batch + (n_plane - 1) * n_batch + n_batch - 1)
    scratch = []
    for a in arrays:
        m, rows, w = a.shape
        size = rows // total
        scratch += [
            pltpu.VMEM((n_plane, n_batch, m, size, w), a.dtype),
            pltpu.VMEM((n_plane - 1, n_batch, m, size, w), a.dtype),
            pltpu.VMEM((n_plane - 1, n_batch, m, size, w), a.dtype),
            pltpu.VMEM((n_batch - 1, m, size, w), a.dtype),
            pltpu.VMEM((n_batch - 1, m, size, w), a.dtype),
        ]
    return pl.pallas_call(
        functools.partial(reduce_kernel, n),
        out_shape=[jax.ShapeDtypeStruct((a.shape[0], a.shape[1] // total, a.shape[2]), jnp.float32) for a in arrays],
        in_specs=[pl.BlockSpec(memory_space=pltpu.VMEM)] * n,
        out_specs=[pl.BlockSpec(memory_space=pltpu.VMEM)] * n,
        scratch_shapes=scratch
        + [pltpu.SemaphoreType.DMA((copies,)), pltpu.SemaphoreType.DMA((copies,))],
        compiler_params=pltpu.CompilerParams(
            collective_id=cid, has_side_effects=True, vmem_limit_bytes=vmem * 2**20
        ),
        name=f"reduce_{cid}",
    )(*arrays)


HEAD_SLOTS = (0, 2, 4, 6, 1, 3, 5, 8, 10, 12, 7, 9, 11, 13)
COMBOS = ((0, 4, 0), (0, 3, 4), (4, 7, 7), (3, 7, 10))
PAIRS = QUERY_HEADS // 2
TILE = 128


def column(vector):
    return jnp.transpose(jnp.broadcast_to(vector.astype(jnp.float32), (128, 128)))


def last_last(a, b):
    return lax.dot_general(a, b, (((1,), (1,)), ((), ())), preferred_element_type=jnp.float32)


def first_first(a, b):
    return lax.dot_general(a, b, (((0,), (0,)), ((), ())), preferred_element_type=jnp.float32)


def straight(a, b):
    return jnp.dot(a, b, preferred_element_type=jnp.float32)


def lookup_kernel(
    block, span, n_ref, rows_ref, table_ref, frozen_ref, flat_ref, frow_ref,
    low_ref, picked_ref, x_ref, held, rough, staged, sem,
):
    step = pl.program_id(0)
    f32, bf16 = jnp.float32, jnp.bfloat16
    low = table_ref[...].astype(bf16)
    low_ref[...] = low
    at = pl.multiple_of(step * span, span)
    held[0, pl.ds(at, span), :] = low.astype(f32)
    held[1, pl.ds(at, span), :] = frozen_ref[...].astype(f32)

    @pl.when(step == pl.num_programs(0) - 1)
    def _():
        picked_ref[...] = jnp.zeros_like(picked_ref)
        n_rows = frow_ref.shape[0]

        def tile(i, _):
            def eight(k, _):
                for j in range(8):
                    place = k * 8 + j
                    row = rows_ref[i * TILE + place]
                    for model in range(2):
                        rough[model, pl.ds(place, 1), :] = held[model, pl.ds(row, 1), :]
                return 0

            lax.fori_loop(0, TILE // 8, eight, 0)
            staged[...] = rough[...].astype(bf16)
            copy = pltpu.make_async_copy(staged, x_ref.at[:, pl.ds(pl.multiple_of(i * TILE, TILE), TILE), :], sem)
            copy.start()
            match = frow_ref[...] == jnp.broadcast_to(flat_ref[pl.ds(i, 1), :], (n_rows, TILE))
            match = jnp.where(match, 1.0, 0.0).astype(bf16)
            for model in range(2):
                picked_ref[model] = picked_ref[model] + straight(match, staged[model]).astype(bf16)
            copy.wait()
            return 0

        lax.fori_loop(0, (n_ref[0] + TILE - 1) // TILE, tile, 0)


def lookup(n_local, rows, table, frozen, flat, frow):
    block, width = table.shape
    span = 512
    steps = pl.cdiv(block, span)
    cap = flat.shape[0] * TILE
    n_rows = frow.shape[0]
    bf16 = jnp.bfloat16
    whole = lambda shape: pl.BlockSpec(shape, lambda i: (0,) * len(shape))
    smem = pl.BlockSpec(memory_space=pltpu.SMEM)
    return pl.pallas_call(
        functools.partial(lookup_kernel, block, span),
        grid=(steps,),
        out_shape=[
            jax.ShapeDtypeStruct((block, width), bf16),
            jax.ShapeDtypeStruct((2, n_rows, width), bf16),
            jax.ShapeDtypeStruct((2, cap, width), bf16),
        ],
        in_specs=[
            smem,
            smem,
            pl.BlockSpec((span, width), lambda i: (i, 0)),
            pl.BlockSpec((span, width), lambda i: (i, 0)),
            whole(flat.shape),
            whole(frow.shape),
        ],
        out_specs=[
            pl.BlockSpec((span, width), lambda i: (i, 0)),
            whole((2, n_rows, width)),
            pl.BlockSpec(memory_space=pl.ANY),
        ],
        scratch_shapes=[
            pltpu.VMEM((2, steps * span, width), jnp.float32),
            pltpu.VMEM((2, TILE, width), jnp.float32),
            pltpu.VMEM((2, TILE, width), bf16),
            pltpu.SemaphoreType.DMA,
        ],
        compiler_params=pltpu.CompilerParams(vmem_limit_bytes=60 * 2**20),
        name="lookup",
    )(n_local, rows, table, frozen, flat, frow)


def head_pieces(both, lane):
    turned = pltpu.roll(both, 64, 1)
    low, high = lane < 64, lane >= 64
    bf16 = jnp.bfloat16
    zero = jnp.zeros_like(both)
    return (
        jnp.where(low, both, zero).astype(bf16),
        jnp.where(high, turned, zero).astype(bf16),
        jnp.where(low, turned, zero).astype(bf16),
        jnp.where(high, both, zero).astype(bf16),
    )


def turn(values, positions, freq, lane, sign):
    angle = positions * freq
    cosine, sine = jnp.cos(angle), jnp.sin(angle)
    first = lax.rem(lane, 64) < 32
    mixed = jnp.where(first, -sign * pltpu.roll(values, 96, 1), sign * pltpu.roll(values, 32, 1))
    return values * cosine + mixed * sine


def allowed_of(frow, flat, r, length):
    flat = jnp.broadcast_to(flat, frow.shape)
    return jnp.where((flat <= frow) & (flat >= r * length), 1.0, 0.0)


def attend_kernel(
    length, rp, n_ref, lo_ref, hi_ref, q_ref, x_ref, w_ref, gain_ref, bias_ref, freq_ref, frow_ref, flat_ref, pos_ref,
    o_ref, st_ref, kv_ref, xbuf, kvbuf, m_scr, l_scr, o_scr, sem,
):
    model = pl.program_id(0)
    f32, bf16 = jnp.float32, jnp.bfloat16
    lane = lax.broadcasted_iota(jnp.int32, (TILE, 128), 1)
    lane_r = lax.broadcasted_iota(jnp.int32, (rp, 128), 1)
    m_scr[...] = jnp.full(m_scr.shape, -1e30, f32)
    l_scr[...] = jnp.zeros_like(l_scr)
    o_scr[...] = jnp.zeros_like(o_scr)

    tiles = (n_ref[0] + TILE - 1) // TILE

    def fetch(i):
        slot = lax.rem(i, 2)
        at = pl.ds(pl.multiple_of(i * TILE, TILE), TILE)
        return pltpu.make_async_copy(x_ref.at[model, at, :], xbuf.at[slot], sem.at[slot])

    @pl.when(tiles > 0)
    def _():
        fetch(0).start()

    def tile(i, _):
        at = pl.ds(pl.multiple_of(i * TILE, TILE), TILE)

        @pl.when(i + 1 < tiles)
        def _():
            fetch(i + 1).start()

        fetch(i).wait()
        x = xbuf[lax.rem(i, 2)].astype(f32)
        scale = lax.rsqrt(jnp.mean(x * x, axis=-1, keepdims=True) + EPS_NORM)
        normed = (x * scale * gain_ref[0]).astype(bf16)
        mixed = straight(normed, w_ref[...]) + bias_ref[0]
        key = turn(mixed[:, :128], column(pos_ref[pl.ds(i, 1), :]), freq_ref[...], lane, 1.0)
        key = key.astype(bf16)
        value = mixed[:, 128:].astype(bf16)
        kvbuf[...] = jnp.concatenate([key, value], axis=1)
        out = pltpu.make_async_copy(kvbuf, kv_ref.at[model, at, :], sem.at[2])
        out.start()
        keys = head_pieces(key.astype(f32), lane)
        values = head_pieces(value.astype(f32), lane)
        one = jnp.ones((TILE, 128), bf16)
        values = tuple(jnp.where((lane < 64) == (c % 2 == 0), v, one) for c, v in enumerate(values))
        flat = flat_ref[pl.ds(i, 1), :]

        def rollout(r, _):
            rows = pl.ds(pl.multiple_of(r * rp, rp), rp)
            ok = allowed_of(frow_ref[rows, :], flat, r, length)[None]
            shift = (ok - 1.0) * 1e30
            falls, adds = {}, {}
            for c, (p0, p1, s0) in enumerate(COMBOS):
                n = p1 - p0
                query = q_ref[p0:p1, rows, :].reshape(n * rp, 128)
                score = last_last(query, keys[c]).reshape(n, rp, TILE) * HEAD_SIZE ** (-0.5)
                score = score * ok + shift
                old = m_scr[s0 : s0 + n, rows, :]
                new = jnp.maximum(old, jnp.max(score, axis=-1, keepdims=True))
                m_scr[s0 : s0 + n, rows, :] = new
                fall = old - new
                prob = jnp.exp(score - new) * ok
                add = straight(prob.astype(bf16).reshape(n * rp, TILE), values[c]).reshape(n, rp, 128)
                for k in range(n):
                    falls[p0 + k, c % 2] = fall[k]
                    adds[p0 + k, c % 2] = add[k]
            for p in range(PAIRS):
                alpha = jnp.exp(jnp.where(lane_r < 64, falls[p, 0], falls[p, 1]))
                turned = pltpu.roll(alpha, 64, 1)
                o_scr[p, rows, :] = o_scr[p, rows, :] * alpha + jnp.where(lane_r < 64, adds[p, 0], adds[p, 1])
                l_scr[p, rows, :] = l_scr[p, rows, :] * turned + jnp.where(lane_r < 64, adds[p, 1], adds[p, 0])
            return 0

        lax.fori_loop(lo_ref[i], hi_ref[i] + 1, rollout, 0)
        out.wait()
        return 0

    lax.fori_loop(0, tiles, tile, 0)

    def leave(r, _):
        rows = pl.ds(pl.multiple_of(r * rp, rp), rp)
        o_ref[:, rows, :] = o_scr[:, rows, :].astype(bf16)
        tops = jnp.full((rp, 128), -1e30, f32)
        totals = jnp.zeros((rp, 128), f32)
        for slot, head in enumerate(HEAD_SLOTS):
            tops = jnp.where(lane_r == head, m_scr[slot, rows, :], tops)
            held = l_scr[head // 2, rows, :]
            held = held[:, 64:65] if head % 2 == 0 else held[:, 0:1]
            totals = jnp.where(lane_r == head, held, totals)
        st_ref[0, rows, :] = tops
        st_ref[1, rows, :] = totals
        return 0

    lax.fori_loop(0, m_scr.shape[1] // rp, leave, 0)


def attend(n_local, lo, hi, q, x, w, gain, bias, freq, frow, flat, pos, length, rp):
    n_rows = q.shape[1]
    width = x.shape[2]
    cap = x.shape[1]
    bf16 = jnp.bfloat16
    whole = lambda shape: pl.BlockSpec(shape, lambda i: (0,) * len(shape))
    smem = pl.BlockSpec(memory_space=pltpu.SMEM)
    anyw = pl.BlockSpec(memory_space=pl.ANY)
    model = lambda shape: pl.BlockSpec(shape, lambda i: (i, 0, 0))
    return pl.pallas_call(
        functools.partial(attend_kernel, length, rp),
        grid=(2,),
        out_shape=[
            jax.ShapeDtypeStruct((2 * PAIRS, n_rows, 128), bf16),
            jax.ShapeDtypeStruct((4, n_rows, 128), jnp.float32),
            jax.ShapeDtypeStruct((2, cap, 256), bf16),
        ],
        in_specs=[
            smem, smem, smem, model((PAIRS, n_rows, 128)), anyw, pl.BlockSpec((width, 256), lambda i: (0, i)), model((1, 1, width)),
            model((1, 1, 256)), whole((1, 128)), whole(frow.shape), whole(flat.shape), whole(pos.shape),
        ],
        out_specs=[model((PAIRS, n_rows, 128)), model((2, n_rows, 128)), anyw],
        scratch_shapes=[
            pltpu.VMEM((2, TILE, width), bf16),
            pltpu.VMEM((TILE, 256), bf16),
            pltpu.VMEM((QUERY_HEADS, n_rows, 128), jnp.float32),
            pltpu.VMEM((PAIRS, n_rows, 128), jnp.float32),
            pltpu.VMEM((PAIRS, n_rows, 128), jnp.float32),
            pltpu.SemaphoreType.DMA((3,)),
        ],
        compiler_params=pltpu.CompilerParams(vmem_limit_bytes=62 * 2**20),
        name="attend",
    )(n_local, lo, hi, q, x, w, gain, bias, freq, frow, flat, pos)


def attend_back_kernel(
    length, rp, n_ref, lo_ref, hi_ref, q_ref, do_ref, st_ref, x_ref, kv_ref, w_ref, gain_ref, freq_ref, frow_ref, flat_ref,
    pos_ref, dq_ref, gkv_ref, gs_ref, gb_ref, dx_ref, xbuf, kvbuf, dxbuf, dq_scr, dk_scr, dv_scr, sem,
):
    f32, bf16 = jnp.float32, jnp.bfloat16
    lane = lax.broadcasted_iota(jnp.int32, (TILE, 128), 1)
    dq_scr[...] = jnp.zeros_like(dq_scr)
    gkv_ref[...] = jnp.zeros_like(gkv_ref)
    gs_ref[...] = jnp.zeros_like(gs_ref)
    gb_ref[...] = jnp.zeros_like(gb_ref)

    def tile(i, _):
        at = pl.ds(pl.multiple_of(i * TILE, TILE), TILE)
        one = pltpu.make_async_copy(x_ref.at[0, at, :], xbuf, sem.at[0])
        one.start()
        two = pltpu.make_async_copy(kv_ref.at[0, at, :], kvbuf, sem.at[1])
        two.start()
        one.wait()
        two.wait()
        keys = head_pieces(kvbuf[:, :128].astype(f32), lane)
        values = head_pieces(kvbuf[:, 128:].astype(f32), lane)
        flat = flat_ref[pl.ds(i, 1), :]
        dk_scr[...] = jnp.zeros_like(dk_scr)
        dv_scr[...] = jnp.zeros_like(dv_scr)

        def rollout(r, _):
            rows = pl.ds(pl.multiple_of(r * rp, rp), rp)
            ok = allowed_of(frow_ref[rows, :], flat, r, length)[None]
            shift = (ok - 1.0) * 1e30
            stats = st_ref[rows, :]
            adds = {}
            for c, (p0, p1, s0) in enumerate(COMBOS):
                n = p1 - p0
                heads = HEAD_SLOTS[s0 : s0 + n]
                query = q_ref[p0:p1, rows, :].reshape(n * rp, 128)
                back = do_ref[p0:p1, rows, :].reshape(n * rp, 128)
                lse = jnp.stack([stats[:, h : h + 1] for h in heads])
                delta = jnp.stack([stats[:, 16 + h : 17 + h] for h in heads])
                score = last_last(query, keys[c]).reshape(n, rp, TILE) * HEAD_SIZE ** (-0.5)
                prob = jnp.exp(score * ok + shift - lse)
                d_prob = last_last(back, values[c]).reshape(n, rp, TILE)
                d_score = (prob * (d_prob - delta)).astype(bf16).reshape(n * rp, TILE)
                add = straight(d_score, keys[c]).reshape(n, rp, 128)
                dk_scr[c] += first_first(d_score, query)
                dv_scr[c] += first_first(prob.astype(bf16).reshape(n * rp, TILE), back)
                for k in range(n):
                    adds[p0 + k, c % 2] = add[k]
            for p in range(PAIRS):
                dq_scr[p, rows, :] = dq_scr[p, rows, :] + adds[p, 0] + adds[p, 1]
            return 0

        lax.fori_loop(lo_ref[i], hi_ref[i] + 1, rollout, 0)

        def joined(scr):
            return jnp.where(lane < 64, scr[0] + pltpu.roll(scr[1], 64, 1), scr[3] + pltpu.roll(scr[2], 64, 1))

        d_key = turn(joined(dk_scr) * HEAD_SIZE ** (-0.5), column(pos_ref[pl.ds(i, 1), :]), freq_ref[...], lane, -1.0)
        d_mixed = jnp.concatenate([d_key, joined(dv_scr)], axis=1).astype(bf16)
        x = xbuf[...].astype(f32)
        scale = lax.rsqrt(jnp.mean(x * x, axis=-1, keepdims=True) + EPS_NORM)
        gain = gain_ref[0]
        normed = (x * scale * gain).astype(bf16)
        gkv_ref[...] += first_first(normed, d_mixed)
        gb_ref[...] += jnp.sum(d_mixed.astype(f32).reshape(TILE // 8, 8, 256), axis=0)
        d_normed = last_last(d_mixed, w_ref[...])
        gs_ref[...] += jnp.sum((d_normed * x * scale).reshape(TILE // 8, 8, x.shape[1]), axis=0)
        d_hat = d_normed * gain
        d_x = scale * (d_hat - x * scale * scale * jnp.mean(d_hat * x, axis=-1, keepdims=True))
        dxbuf[...] = d_x.astype(bf16)
        out = pltpu.make_async_copy(dxbuf, dx_ref.at[at, :], sem.at[2])
        out.start()
        out.wait()
        return 0

    lax.fori_loop(0, (n_ref[0] + TILE - 1) // TILE, tile, 0)
    dq_ref[...] = (dq_scr[...] * HEAD_SIZE ** (-0.5)).astype(bf16)


def attend_back(n_local, lo, hi, q, do, stats, x, kv, w, gain, freq, frow, flat, pos, length, rp):
    n_rows = q.shape[1]
    width = x.shape[2]
    cap = x.shape[1]
    bf16, f32 = jnp.bfloat16, jnp.float32
    whole = lambda shape: pl.BlockSpec(shape, lambda i: (0,) * len(shape))
    smem = pl.BlockSpec(memory_space=pltpu.SMEM)
    anyw = pl.BlockSpec(memory_space=pl.ANY)
    return pl.pallas_call(
        functools.partial(attend_back_kernel, length, rp),
        grid=(1,),
        out_shape=[
            jax.ShapeDtypeStruct((PAIRS, n_rows, 128), bf16),
            jax.ShapeDtypeStruct((width, 256), f32),
            jax.ShapeDtypeStruct((8, width), f32),
            jax.ShapeDtypeStruct((8, 256), f32),
            jax.ShapeDtypeStruct((cap, width), bf16),
        ],
        in_specs=[
            smem, smem, smem, whole((PAIRS, n_rows, 128)), whole((PAIRS, n_rows, 128)), whole((n_rows, 128)), anyw, anyw,
            whole((width, 256)), whole((1, 1, width)), whole((1, 128)), whole(frow.shape), whole(flat.shape),
            whole(pos.shape),
        ],
        out_specs=[
            whole((PAIRS, n_rows, 128)), whole((width, 256)), whole((8, width)), whole((8, 256)), anyw,
        ],
        scratch_shapes=[
            pltpu.VMEM((TILE, width), bf16),
            pltpu.VMEM((TILE, 256), bf16),
            pltpu.VMEM((TILE, width), bf16),
            pltpu.VMEM((PAIRS, n_rows, 128), f32),
            pltpu.VMEM((4, TILE, 128), f32),
            pltpu.VMEM((4, TILE, 128), f32),
            pltpu.SemaphoreType.DMA((3,)),
        ],
        compiler_params=pltpu.CompilerParams(vmem_limit_bytes=60 * 2**20),
        name="attend_back",
    )(n_local, lo, hi, q, do, stats, x, kv, w, gain, freq, frow, flat, pos)


def table_grad_kernel(
    block, span, n_ref, rows_ref, dl_ref, af_ref, drow_ref, frow_ref, flat_ref, dx_ref,
    g_ref, sq_ref, added, moved, rough, sem,
):
    step = pl.program_id(0)
    f32, bf16 = jnp.float32, jnp.bfloat16

    @pl.when(step == 0)
    def _():
        sq_ref[...] = jnp.zeros_like(sq_ref)
        added[...] = jnp.zeros_like(added)
        n_rows = drow_ref.shape[0]

        def tile(i, _):
            copy = pltpu.make_async_copy(dx_ref.at[pl.ds(pl.multiple_of(i * TILE, TILE), TILE), :], moved, sem)
            copy.start()
            token = column(flat_ref[pl.ds(i, 1), :])
            token = jnp.concatenate([token] * (n_rows // 128), axis=1)
            match = jnp.where(token == jnp.broadcast_to(frow_ref[...], (TILE, n_rows)), 1.0, 0.0).astype(bf16)
            own = straight(match, drow_ref[...])
            copy.wait()
            rough[...] = own + moved[...].astype(f32)

            def eight(k, _):
                for j in range(8):
                    place = k * 8 + j
                    row = pl.ds(rows_ref[i * TILE + place], 1)
                    added[row, :] = added[row, :] + rough[pl.ds(place, 1), :]
                return 0

            lax.fori_loop(0, TILE // 8, eight, 0)
            return 0

        lax.fori_loop(0, (n_ref[0] + TILE - 1) // TILE, tile, 0)

    inside = step * span + lax.broadcasted_iota(jnp.int32, (span, 1), 0) < block
    logit = jnp.where(inside, dl_ref[...].astype(f32), 0.0).astype(bf16)
    total = straight(logit, af_ref[...]) + added[pl.ds(pl.multiple_of(step * span, span), span), :]
    g_ref[...] = total.astype(bf16)
    square = total * total
    sq_ref[...] += jnp.sum(square.reshape(span // 8, 8, square.shape[1]), axis=0)


def table_grad(n_local, rows, dl, af, drow, frow, flat, dx, block):
    n_rows, width = af.shape
    span = 512
    steps = pl.cdiv(block, span)
    whole = lambda shape: pl.BlockSpec(shape, lambda i: (0,) * len(shape))
    smem = pl.BlockSpec(memory_space=pltpu.SMEM)
    return pl.pallas_call(
        functools.partial(table_grad_kernel, block, span),
        grid=(steps,),
        out_shape=[
            jax.ShapeDtypeStruct((block, width), jnp.bfloat16),
            jax.ShapeDtypeStruct((8, width), jnp.float32),
        ],
        in_specs=[
            smem, smem,
            pl.BlockSpec((span, n_rows), lambda i: (i, 0)),
            whole(af.shape), whole(drow.shape), whole(frow.shape), whole(flat.shape),
            pl.BlockSpec(memory_space=pl.ANY),
        ],
        out_specs=[pl.BlockSpec((span, width), lambda i: (i, 0)), whole((8, width))],
        scratch_shapes=[
            pltpu.VMEM((steps * span, width), jnp.float32),
            pltpu.VMEM((TILE, width), jnp.bfloat16),
            pltpu.VMEM((TILE, width), jnp.float32),
            pltpu.SemaphoreType.DMA,
        ],
        compiler_params=pltpu.CompilerParams(vmem_limit_bytes=56 * 2**20),
        name="table_grad",
    )(n_local, rows, dl, af, drow, frow, flat, dx)


def spread_kernel(own_ref, frozen_ref, out_ref):
    devices, _, _, wide = out_ref.shape
    units, rows = wide // 2, own_ref.shape[0]
    bf16 = jnp.bfloat16
    out_ref[...] = jnp.zeros_like(out_ref)
    for side in range(2):
        for d in range(devices):
            at = (side * devices + d) * units
            out_ref[d, 0, :rows, side * units : (side + 1) * units] = own_ref[:, at : at + units].astype(bf16)
            out_ref[d, 1, :rows, side * units : (side + 1) * units] = frozen_ref[:, at : at + units]


def spread(own, frozen, devices, units, rows_up):
    vm = pl.BlockSpec(memory_space=pltpu.VMEM)
    return pl.pallas_call(
        spread_kernel,
        out_shape=jax.ShapeDtypeStruct((devices, 2, rows_up, 2 * units), jnp.bfloat16),
        in_specs=[vm, vm],
        out_specs=vm,
        compiler_params=pltpu.CompilerParams(vmem_limit_bytes=48 * 2**20),
        name="spread",
    )(own, frozen)


def join_kernel(g_ref, out_ref):
    devices, _, wide = g_ref.shape
    units, rows = wide // 2, out_ref.shape[0]
    for side in range(2):
        for d in range(devices):
            at = (side * devices + d) * units
            out_ref[:, at : at + units] = g_ref[d, :rows, side * units : (side + 1) * units].astype(jnp.float32)


def join(g, rows, units):
    vm = pl.BlockSpec(memory_space=pltpu.VMEM)
    return pl.pallas_call(
        join_kernel,
        out_shape=jax.ShapeDtypeStruct((rows, 2 * units * g.shape[0]), jnp.float32),
        in_specs=[vm],
        out_specs=vm,
        compiler_params=pltpu.CompilerParams(vmem_limit_bytes=48 * 2**20),
        name="join",
    )(g)


def blend(parts, lane):
    f32 = jnp.float32
    n_models = len(parts[0][1]) // 2
    planes, stats = [], []
    for model in range(n_models):
        tops = [p[1][2 * model] for p in parts]
        top = tops[0]
        for t in tops[1:]:
            top = jnp.maximum(top, t)
        weights = [jnp.exp(t - top) for t in tops]
        stats += [top, sum(p[1][2 * model + 1] * w for p, w in zip(parts, weights))]
        for pair in range(PAIRS):
            acc = None
            for p, w in zip(parts, weights):
                each = jnp.where(lane < 64, w[:, 2 * pair : 2 * pair + 1], w[:, 2 * pair + 1 : 2 * pair + 2])
                term = p[0][model * PAIRS + pair].astype(f32) * each
                acc = term if acc is None else acc + term
            planes.append(acc)
    return planes, stats


def mix_kernel(o_ref, st_ref, oo_ref, so_ref, *rest):
    core_o, core_s, sum_o, sum_s, plane_o, plane_s, keep_o, keep_s, line_o, line_s, send_sems, recv_sems = rest
    _, n_y, n_batch = places()
    half, y, core, batch = coords()
    n_plane = 2 * n_y
    spot = half * n_y + y
    line, plane, other = peers()
    greet(line, plane, other)
    size = oo_ref.shape[1]
    lane = lax.broadcasted_iota(jnp.int32, (size, 128), 1)
    order = list(range(1, n_batch)) + [0]
    spots = [to for _, to, _ in plane] + [spot]
    slots = iter(range(2 * (n_plane * n_batch + (n_plane - 1) * n_batch + n_batch - 1)))

    def send(src, dst, who):
        slot = next(slots)
        return push(src, dst, send_sems.at[slot], recv_sems.at[slot], who)

    def rows(side, where, j):
        at = (side * n_plane + where) * n_batch + lax.rem(batch + j, n_batch)
        return pl.ds(pl.multiple_of(at * size, size), size)

    def store(o, s, merged):
        for k, value in enumerate(merged[0]):
            o[k] = value.astype(o.dtype)
        for k, value in enumerate(merged[1]):
            s[k] = value

    by_core, by_plane, by_line = {}, {}, {}
    for j in order:
        for p in range(n_plane):
            at = rows(1 - core, spots[p], j)
            by_core[p, j] = (
                send(o_ref.at[:, at, :], core_o.at[p, j], other[0]), send(st_ref.at[:, at, :], core_s.at[p, j], other[0])
            )

    def mine(p, j):
        at = rows(core, spots[p], j)
        for copy in by_core[p, j]:
            copy.wait_recv()
        return blend([(o_ref[:, at, :], st_ref[:, at, :]), (core_o[p, j], core_s[p, j])], lane)

    for j in order:
        for p in range(n_plane - 1):
            store(sum_o.at[p, j], sum_s.at[p, j], mine(p, j))
            by_plane[p, j] = (
                send(sum_o.at[p, j], plane_o.at[p, j], plane[p][0]), send(sum_s.at[p, j], plane_s.at[p, j], plane[p][0])
            )
    for j in order:
        parts = [mine(n_plane - 1, j)]
        for p in range(n_plane - 1):
            for copy in by_plane[p, j]:
                copy.wait_recv()
            parts.append((plane_o[p, j], plane_s[p, j]))
        store(keep_o.at[j], keep_s.at[j], blend(parts, lane))
        if j:
            by_line[j] = (
                send(keep_o.at[j], line_o.at[j - 1], line[j - 1][0]), send(keep_s.at[j], line_s.at[j - 1], line[j - 1][0])
            )
    parts = [(keep_o[0], keep_s[0])]
    for j in range(1, n_batch):
        for copy in by_line[j]:
            copy.wait_recv()
        parts.append((line_o[j - 1], line_s[j - 1]))
    store(oo_ref, so_ref, blend(parts, lane))
    for group in (by_core, by_plane, by_line):
        for pair in group.values():
            for copy in pair:
                copy.wait_send()


def mix(o, stats, cid):
    _, n_y, n_batch = places()
    n_plane = 2 * n_y
    planes, all_rows, _ = o.shape
    ns = stats.shape[0]
    bf16, f32 = jnp.bfloat16, jnp.float32
    copies = 2 * (n_plane * n_batch + (n_plane - 1) * n_batch + n_batch - 1)
    row = all_rows // (2 * n_plane * n_batch)
    vm = pl.BlockSpec(memory_space=pltpu.VMEM)
    scratch = []
    for lead in ((n_plane, n_batch), (n_plane - 1, n_batch), (n_plane - 1, n_batch), (n_batch,), (n_batch - 1,)):
        scratch += [pltpu.VMEM(lead + (planes, row, 128), bf16), pltpu.VMEM(lead + (ns, row, 128), f32)]
    return pl.pallas_call(
        mix_kernel,
        out_shape=[
            jax.ShapeDtypeStruct((planes, row, 128), f32),
            jax.ShapeDtypeStruct((ns, row, 128), f32),
        ],
        in_specs=[vm] * 2,
        out_specs=[vm] * 2,
        scratch_shapes=scratch + [pltpu.SemaphoreType.DMA((copies,)), pltpu.SemaphoreType.DMA((copies,))],
        compiler_params=pltpu.CompilerParams(collective_id=cid, has_side_effects=True, vmem_limit_bytes=56 * 2**20),
        name="mix",
    )(o, stats)


AXES = ("half", "mp", "batch")


def norm_forward(x, gain):
    scale = lax.rsqrt(jnp.mean(x * x, axis=-1, keepdims=True) + EPS_NORM)
    return (x * scale * gain, scale)


def norm_backward(d_out, x, scale, gain):
    d_gain = d_out * x * scale
    d_hat = d_out * gain
    d_x = scale * (d_hat - x * scale * scale * jnp.mean(d_hat * x, axis=-1, keepdims=True))
    return (d_x, d_gain)


def frequencies():
    half_size = HEAD_SIZE // 2
    return THETA ** (-(jnp.arange(half_size, dtype=jnp.float32) * 2.0) / HEAD_SIZE)


def rotate(x, cosine, sine, sign):
    half_size = HEAD_SIZE // 2
    first, second = x[..., :half_size], x[..., half_size:]
    return jnp.concatenate(
        [first * cosine - sign * second * sine, second * cosine + sign * first * sine], axis=-1
    )


def to_pairs(x):
    lead, rows = x.shape[:-2], x.shape[-2]
    x = x.reshape(lead + (rows, PAIRS, 128))
    x = jnp.moveaxis(x, -2, -3)
    return x.reshape((-1, rows, 128))


def from_pairs(x, models):
    rows = x.shape[1]
    x = x.reshape(models, PAIRS, rows, 128)
    return jnp.moveaxis(x, 1, 2).reshape(models, rows, MODEL_WIDTH)


def bmm(x, w):
    return jnp.stack([jnp.dot(x[i], w[i], preferred_element_type=jnp.float32) for i in range(2)])


def body(
    tokens, lengths, labels, scored, qkv_weight, out_weight, gu_weight, down_weight, embed_weight, small_params,
    moment_qkv, moment_out, moment_gu, moment_down, moment_embed, moment_small,
    square_qkv, square_out, square_gu, square_down, square_embed, square_small,
    ref_qkv, ref_out, ref_gu, ref_down, ref_embed, ref_small,
):
    masters = (qkv_weight, out_weight, gu_weight, down_weight, embed_weight, small_params)
    firsts = (moment_qkv, moment_out, moment_gu, moment_down, moment_embed, moment_small)
    seconds = (square_qkv, square_out, square_gu, square_down, square_embed, square_small)
    bf16, f32, i32 = jnp.bfloat16, jnp.float32, jnp.int32
    n_mp, n_batch = lax.axis_size("mp"), lax.axis_size("batch")
    devices = 2 * n_mp * n_batch
    n_y = n_mp // 2
    block = embed_weight.shape[0]
    feats = qkv_weight.shape[0]
    units = down_weight.shape[0]
    rollouts = MICRO * n_batch
    length = n_mp * TOK
    rp = n_mp * P_SIZE
    n_rows = rollouts * rp
    own_rows = n_rows // devices
    lin = lax.axis_index(AXES)
    com = comm_index()
    base = lin * block

    feats_up = -(-feats // 16) * 16

    def to_up(x):
        return jnp.pad(x, ((0, feats_up - feats), (0, 0)))

    feat = jnp.arange(MODEL_WIDTH, dtype=i32)
    padded = jnp.arange(devices * feats_up, dtype=i32)
    to_order = (padded[None, :] == (feat // feats * feats_up + feat % feats)[:, None]).astype(bf16)
    from_order = (padded[:, None] == (feat // feats * feats_up + feat % feats)[None, :]).astype(bf16)

    def pad_feats(x):
        return jnp.dot(x, to_order, preferred_element_type=f32).astype(bf16)

    def cut_feats(x):
        high = x.astype(bf16)
        both = jnp.concatenate([high, (x - high.astype(f32)).astype(bf16)], axis=0)
        both = jnp.dot(both, from_order, preferred_element_type=f32)
        return both[: x.shape[0]] + both[x.shape[0] :]

    def placed(x):
        x = jnp.pad(x.astype(bf16), ((0, 0), (0, 128 - x.shape[1])))
        x = jnp.roll(x, lin * small_params.shape[1], axis=1)
        return jnp.pad(x, ((0, -x.shape[0] % feats_up), (0, 0)))

    qkv_low = qkv_weight.astype(bf16)
    early = to_up(
        jnp.concatenate(
            [qkv_low[:, :MODEL_WIDTH], ref_qkv[:, :MODEL_WIDTH], qkv_low[:, MODEL_WIDTH:], ref_qkv[:, MODEL_WIDTH:]], axis=1
        )
    )
    smalls = [placed(small_params), placed(ref_small)]
    tall = smalls[0].shape[0] // feats_up
    smalls = [x.reshape(tall, feats_up, 128)[k] for x in smalls for k in range(tall)]
    early = lax.all_gather(jnp.concatenate([early] + smalls, axis=1), AXES, axis=0, tiled=True)
    at_small = 2 * QKV
    w_q = (early[:, :MODEL_WIDTH], early[:, MODEL_WIDTH : 2 * MODEL_WIDTH])
    down_low = jnp.stack([down_weight.astype(bf16), ref_down])

    ids = tokens.transpose(0, 2, 1, 3).reshape(rollouts, length)
    lens = lengths.reshape(rollouts)
    spots = jnp.arange(length, dtype=i32)
    flat_ids = jnp.arange(rollouts * length, dtype=i32).reshape(rollouts, length)
    bits = max(1, (block - 1).bit_length())
    local = (ids >= base) & (ids < base + block) & (spots[None, :] < lens[:, None])
    key = jnp.where(local, (flat_ids << bits) + (ids - base), jnp.int32(2**31 - 1)).reshape(-1)
    key = lax.sort(key)
    n_local = jnp.sum(local.astype(i32))
    live = jnp.arange(rollouts * length, dtype=i32) < n_local
    row_of = jnp.where(live, key & ((1 << bits) - 1), 0)
    flat_of = jnp.where(live, key >> bits, 1 << 22).reshape(-1, TILE)
    pos_of = jnp.where(live, (key >> bits) % length, 0).reshape(-1, TILE).astype(f32)
    tile_lo = flat_of[:, 0] // length
    tile_hi = jnp.max(jnp.where(live, (key >> bits) // length, -1).reshape(-1, TILE), axis=1)
    n_one = n_local.reshape(1)

    picks = scored.transpose(0, 2, 1, 3) + (jnp.arange(n_mp, dtype=i32) * TOK)[None, None, :, None]
    picks = picks.reshape(rollouts, rp)
    valid = (picks + 1 < lens[:, None]).astype(f32)
    count = jnp.sum(valid)
    after = picks[:, :, None] + 1 == spots[None, None, :]
    targets = jnp.sum(jnp.where(after, ids[:, None, :], 0), axis=2).reshape(-1)
    frow = (picks + (jnp.arange(rollouts, dtype=i32) * length)[:, None]).reshape(-1)
    frow_wide = jnp.broadcast_to(frow[:, None], (n_rows, 128))

    low_table, picked, x_tok = lookup(n_one, row_of, embed_weight, ref_embed, flat_of, frow_wide)
    out_both = to_up(jnp.concatenate([out_weight.astype(bf16), ref_out], axis=1))
    picked, out_both = lax.optimization_barrier((picked, out_both))
    late = lax.all_gather(out_both, AXES, axis=0, tiled=True)
    w_out = (late[:, :MODEL_WIDTH], late[:, MODEL_WIDTH:])
    (x0,) = reduce([picked], 1)

    w_kv = jnp.dot(to_order, early[:, 2 * MODEL_WIDTH : at_small], preferred_element_type=f32).astype(bf16)
    small_rows = small_params.shape[0]
    flat_small = jnp.sum(early[:, at_small:].astype(f32).reshape(devices, feats_up, -1), axis=0)
    flat_small = flat_small.reshape(feats_up, 2, tall, 128).transpose(1, 2, 0, 3).reshape(2, tall * feats_up, 128)
    flat_small = flat_small[:, :small_rows].reshape(2, -1)
    gain_attn = flat_small[:, None, :MODEL_WIDTH]
    gain_mlp = flat_small[:, None, MODEL_WIDTH : 2 * MODEL_WIDTH]
    gain_final = flat_small[:, None, 2 * MODEL_WIDTH : 3 * MODEL_WIDTH]
    bias = flat_small[:, None, 3 * MODEL_WIDTH :]

    freq = frequencies()
    my_pos = lax.dynamic_slice_in_dim(picks.reshape(-1), com * own_rows, own_rows)
    angle = my_pos.astype(f32)[:, None] * freq[None, :]
    cosine, sine = jnp.cos(angle)[:, None, :], jnp.sin(angle)[:, None, :]
    a1, scale_one = norm_forward(x0, gain_attn)
    a1 = a1.astype(bf16)
    mixed = bmm(pad_feats(a1), w_q) + bias[:, :, :MODEL_WIDTH]
    q = rotate(mixed.reshape(2, own_rows, QUERY_HEADS, HEAD_SIZE), cosine, sine, 1.0)
    q = to_pairs(q.reshape(2, own_rows, MODEL_WIDTH).astype(bf16))
    q_all, a1_all = gather([q, a1[:1]], 2)
    q_all, gu_sent = lax.optimization_barrier((q_all, spread(gu_weight, ref_gu, devices, units, feats_up)))
    gu_cols = lax.all_to_all(gu_sent, AXES, split_axis=0, concat_axis=0, tiled=True)
    w_gu = tuple(gu_cols[:, model].reshape(devices * feats_up, 2 * units) for model in range(2))

    freq_wide = jnp.tile(freq, 4).reshape(1, 128)
    o_part, st_part, kv_tok = attend(
        n_one, tile_lo, tile_hi, q_all, x_tok, w_kv, gain_attn, bias[:, :, MODEL_WIDTH:], freq_wide, frow_wide, flat_of,
        pos_of, length, rp,
    )
    o_sum, st_sum = mix(o_part, st_part, 3)
    lse = st_sum[0] + jnp.log(st_sum[1])
    share = (1.0 / st_sum[1::2])[:, :, :QUERY_HEADS]
    o = from_pairs(o_sum, 2).reshape(2, own_rows, QUERY_HEADS, HEAD_SIZE) * share[..., None]
    o = o.reshape(2, own_rows, MODEL_WIDTH).astype(bf16)
    x1 = x0 + bmm(pad_feats(o), w_out)
    a2, scale_two = norm_forward(x1, gain_mlp)
    a2_all, o_all = gather([pad_feats(a2.astype(bf16)), o[:1]], 4)
    gate_up = bmm(a2_all, w_gu)
    gate, up = gate_up[:, :, :units], gate_up[:, :, units:]
    hidden = (jax.nn.silu(gate) * up).astype(bf16)
    (branch,) = reduce([bmm(hidden, down_low).astype(bf16)], 5)
    x2 = x1 + branch
    af, scale_final = norm_forward(x2, gain_final)
    (af_all,) = gather([af.astype(bf16)], 6)

    vocab = base + jnp.arange(block, dtype=i32)
    hit = vocab[:, None] == targets[None, :]
    tables = (low_table, ref_embed)
    logits = [
        lax.dot_general(tables[i], af_all[i], (((1,), (1,)), ((), ())), preferred_element_type=f32) for i in range(2)
    ]
    stats = []
    for i in range(2):
        peak = jnp.max(logits[i], axis=0)
        stats.append(
            jnp.stack(
                [
                    peak,
                    jnp.sum(jnp.exp(logits[i] - peak[None, :]), axis=0),
                    jnp.sum(jnp.where(hit, logits[i], 0.0), axis=0),
                ]
            )
        )
    stats = jnp.concatenate(stats, axis=0)
    stats = jnp.concatenate([stats, jnp.zeros((2, n_rows), f32)], axis=0)
    (stats_all,) = gather([stats[None]], 7)
    stats_all = stats_all.reshape(devices, 8, n_rows)
    lps, lses = [], []
    for i in range(2):
        peaks = stats_all[:, 3 * i]
        peak = jnp.max(peaks, axis=0)
        sums = jnp.sum(stats_all[:, 3 * i + 1] * jnp.exp(peaks - peak[None]), axis=0)
        lses.append(peak + jnp.log(sums))
        lps.append(jnp.sum(stats_all[:, 3 * i + 2], axis=0) - lses[i])
    ratio = (lps[0] - lps[1]).reshape(rollouts, rp)
    factor = BETA * n_rows / count
    reward = factor * jnp.sum(valid * ratio, axis=1)
    d_reward = (jax.nn.sigmoid(reward) - labels.reshape(rollouts).astype(f32)) / rollouts
    d_lp = (valid * (d_reward * factor)[:, None]).reshape(-1)

    probs = jnp.exp(logits[0] - lses[0][None, :])
    d_logits = (d_lp[None, :] * (hit.astype(f32) - probs)).astype(bf16)
    d_af = lax.dot_general(d_logits, low_table, (((0,), (0,)), ((), ())), preferred_element_type=f32)
    (d_final,) = reduce([d_af.astype(bf16)[None]], 8)
    d_out, g_gain_final = norm_backward(d_final[0], x2[0], scale_final[0], gain_final[0])
    (d_branch,) = gather([d_out.astype(bf16)[None]], 9)
    d_branch = d_branch[0]
    g_down = lax.dot_general(hidden[0], d_branch, (((0,), (0,)), ((), ())), preferred_element_type=f32)
    d_hidden = lax.dot_general(d_branch, down_low[0], (((1,), (1,)), ((), ())), preferred_element_type=f32)
    sigma = jax.nn.sigmoid(gate[0])
    d_gate = d_hidden * up[0] * sigma * (1.0 + gate[0] * (1.0 - sigma))
    d_up = d_hidden * gate[0] * sigma
    d_gate_up = jnp.concatenate([d_gate, d_up], axis=1).astype(bf16)
    d_a2 = lax.dot_general(d_gate_up, w_gu[0], (((1,), (1,)), ((), ())), preferred_element_type=f32)
    (d_normed,) = reduce([d_a2.astype(bf16)[None]], 10)
    d_mid, g_gain_mlp = norm_backward(cut_feats(d_normed[0]), x1[0], scale_two[0], gain_mlp[0])
    d_mid = d_mid + d_out
    d_attn = d_mid.astype(bf16)
    d_o = lax.dot_general(d_attn, w_out[0], (((1,), (1,)), ((), ())), preferred_element_type=f32)
    d_o = cut_feats(d_o).astype(bf16)
    delta = jnp.sum(
        (d_o.astype(f32) * o[0].astype(f32)).reshape(own_rows, QUERY_HEADS, HEAD_SIZE), axis=-1
    )
    row_stats = jnp.concatenate(
        [lse[:, :16], delta, jnp.zeros((own_rows, 128 - 16 - QUERY_HEADS), f32)], axis=1
    )
    d_attn_all, d_o_all, row_stats_all = gather([d_attn[None], to_pairs(d_o), row_stats[None]], 11)
    d_attn_all = d_attn_all[0]

    g_gu = lax.dot_general(a2_all[0], d_gate_up, (((0,), (0,)), ((), ())), preferred_element_type=f32)
    gu_square = jnp.sum(g_gu * g_gu)
    g_gu = g_gu.astype(bf16).reshape(devices, feats_up, 2 * units)
    g_gu, d_o_all = lax.optimization_barrier((g_gu, d_o_all))
    g_gu = lax.all_to_all(g_gu, AXES, split_axis=0, concat_axis=0, tiled=True)
    dq_part, g_kv_part, g_gain_kv, g_bias_kv, dx_tok = attend_back(
        n_one, tile_lo, tile_hi, q_all[:PAIRS], d_o_all, row_stats_all[0], x_tok, kv_tok, w_kv, gain_attn[:1],
        freq_wide, frow_wide, flat_of, pos_of, length, rp,
    )
    dq_part, g_gu = lax.optimization_barrier((dq_part, g_gu))
    g_kv_part = g_kv_part.reshape(2, n_y, 2, n_batch, feats, 256).transpose(2, 0, 1, 3, 4, 5)
    g_kv_part = jnp.pad(g_kv_part.reshape(devices, feats, 256), ((0, 0), (0, feats_up - feats), (0, 0)))
    dq, g_kv = reduce([dq_part, g_kv_part.reshape(1, devices * feats_up, 256)], 12)
    g_kv = g_kv[0, :feats]
    dq = rotate(from_pairs(dq, 1).reshape(own_rows, QUERY_HEADS, HEAD_SIZE), cosine, sine, -1.0)
    dq = dq.reshape(own_rows, MODEL_WIDTH).astype(bf16)
    d_a1 = cut_feats(lax.dot_general(dq, w_q[0], (((1,), (1,)), ((), ())), preferred_element_type=f32))
    d_row, g_gain_row = norm_backward(d_a1, x0[0], scale_one[0], gain_attn[0])
    dq_all, d_row_all = gather([dq[None], (d_row + d_mid).astype(bf16)[None]], 13)
    dq_all = dq_all[0]

    embed_grad, embed_square = table_grad(
        n_one, row_of, d_logits, af_all[0], d_row_all[0], frow.reshape(1, -1).astype(f32), flat_of, dx_tok, block
    )

    def mine(rows, grads):
        cols = lax.dynamic_slice_in_dim(rows, lin * feats, feats, 1)
        return lax.dot_general(cols, grads, (((0,), (0,)), ((), ())), preferred_element_type=f32)

    g_out = mine(o_all[0], d_attn_all)
    g_q = mine(a1_all[0], dq_all)
    g_qkv = jnp.concatenate([g_q, g_kv], axis=1)

    small_part = jnp.concatenate(
        [
            jnp.sum(g_gain_kv, axis=0) + jnp.sum(g_gain_row, axis=0),
            jnp.sum(g_gain_mlp, axis=0),
            jnp.sum(g_gain_final, axis=0),
            jnp.sum(dq.astype(f32), axis=0),
            jnp.sum(g_bias_kv, axis=0),
        ]
    )
    square_part = (
        jnp.sum(g_qkv * g_qkv) + jnp.sum(g_out * g_out) + gu_square + jnp.sum(g_down * g_down) + jnp.sum(embed_square)
    )
    last = jnp.concatenate([small_part, jnp.full((128,), square_part, f32), jnp.zeros((128,), f32)]).reshape(1, -1, 128)
    (last_all,) = gather([last], 14)
    last_all = jnp.sum(last_all.reshape(devices, -1, 128), axis=0)
    g_small = last_all[:small_rows]
    norm = jnp.sqrt(jnp.sum(g_small * g_small) + last_all[small_rows, 0])
    g_small = lax.dynamic_slice_in_dim(g_small, lin * small_params.shape[1], small_params.shape[1], 1)

    g_gu = join(g_gu, feats, units)
    owned_grads = (g_qkv, g_out, g_gu, g_down, embed_grad, g_small)
    clip = jnp.minimum(1.0, CLIP / (norm + 1e-06))
    new_weights, new_firsts, new_seconds, new_lows, clipped_list = ([], [], [], [], [])
    for w, g, m, v in zip(masters, owned_grads, firsts, seconds):
        g = g.astype(f32) * clip
        m_new = MOM1 * m + (1.0 - MOM1) * g
        v_new = MOM2 * v + (1.0 - MOM2) * g * g
        update = m_new / (1.0 - MOM1**STEP) / (jnp.sqrt(v_new / (1.0 - MOM2**STEP)) + EPS_ADAM)
        w_new = w - RATE * (update + DECAY * w)
        new_weights.append(w_new)
        new_firsts.append(m_new)
        new_seconds.append(v_new)
        clipped_list.append(g)
        new_lows.append(w_new.astype(bf16))
    return (
        *new_weights[:5], clipped_list[5], *new_firsts, *new_seconds, *new_lows[:5], norm,
    )


def solution(mesh):
    rows, cols = P(AXES, None), P(None, AXES)
    six = (rows, rows, rows, rows, rows, cols)
    in_specs = (P(), P(), P(), P()) + six * 4
    out_specs = six * 3 + (rows,) * 5 + (P(),)
    return jax.shard_map(body, mesh=mesh, in_specs=in_specs, out_specs=out_specs, check_vma=False)
```

```python
import functools

import jax
import jax.numpy as jnp
from jax import lax
from jax.experimental import pallas as pl
from jax.experimental.pallas import tpu as pltpu
from jax.sharding import PartitionSpec as P

MODEL_WIDTH = 896
QUERY_HEADS = 14
KEY_VALUE_HEADS = 2
HEAD_SIZE = 64
FF = 4864
QKV = 1152
TOK = 256
P_SIZE = 16
MICRO = 2
STEP = 5

EPS_NORM = 1e-06
THETA = 1000000.0
BETA = 0.05
CLIP = 0.1
RATE = 0.03
DECAY = 0.01
MOM1 = 0.5
MOM2 = 0.5
EPS_ADAM = 1e-08

MESH = pl.DeviceIdType.MESH

def places():
    n_mp, n_batch = lax.axis_size("mp"), lax.axis_size("batch")
    return 2, n_mp // 2, n_batch


def coords():
    mp = lax.axis_index("mp")
    return lax.axis_index("half"), mp // 2, lax.rem(mp, 2), lax.axis_index("batch")


def comm_index():
    _, n_y, n_batch = places()
    half, y, core, batch = coords()
    return ((core * 2 + half) * n_y + y) * n_batch + batch


def peers():
    _, n_y, n_batch = places()
    half, y, core, batch = coords()
    line = []
    for k in range(1, n_batch):
        to, frm = lax.rem(batch + k, n_batch), lax.rem(batch + n_batch - k, n_batch)
        line.append(({"half": half, "mp": y * 2 + core, "batch": to}, to, frm))
    plane = []
    n_plane = 2 * n_y
    spot = half * n_y + y
    for k in range(1, n_plane):
        to, frm = lax.rem(spot + k, n_plane), lax.rem(spot + n_plane - k, n_plane)
        plane.append(
            ({"half": to // n_y, "mp": lax.rem(to, n_y) * 2 + core, "batch": batch}, to, frm)
        )
    other = ({"half": half, "mp": y * 2 + (1 - core), "batch": batch}, 1 - core, 1 - core)
    return line, plane, other


def greet(line, plane, other):
    barrier = pltpu.get_barrier_semaphore()
    everyone = line + plane + [other]
    for who, _, _ in everyone:
        pl.semaphore_signal(barrier, inc=1, device_id=who, device_id_type=MESH)
    pl.semaphore_wait(barrier, len(everyone))


def push(src, dst, send_sem, recv_sem, who):
    copy = pltpu.make_async_remote_copy(
        src_ref=src,
        dst_ref=dst,
        send_sem=send_sem,
        recv_sem=recv_sem,
        device_id=who,
        device_id_type=MESH,
    )
    copy.start()
    return copy


def gather_phase(ins, outs, send_sems, recv_sems, own_sem, line, plane, other):
    n_arr = len(ins)
    _, n_y, n_batch = places()
    half, y, core, batch = coords()
    n_plane = 2 * n_y
    spot = half * n_y + y
    slots = iter(range(n_arr * (n_batch - 1 + n_plane * n_batch + (n_plane - 1) * n_batch)))

    def rows(i, where, j):
        size = ins[i].shape[1]
        at = (core * n_plane + where) * n_batch + lax.rem(batch + n_batch - j, n_batch)
        return outs[i].at[:, pl.ds(pl.multiple_of(at * size, size), size), :]

    def send(src, dst, who):
        slot = next(slots)
        return push(src, dst, send_sems.at[slot], recv_sems.at[slot], who)

    local, by_line, by_plane, by_core = [], [], [], []
    for i in range(n_arr):
        by_line.append([send(ins[i], rows(i, spot, 0), who) for who, _, _ in line])
    for i in range(n_arr):
        by_plane.append([[send(ins[i], rows(i, spot, 0), who) for who, _, _ in plane]])
        by_core.append(send(ins[i], rows(i, spot, 0), other[0]))
        copy = pltpu.make_async_copy(ins[i], rows(i, spot, 0), own_sem.at[i])
        copy.start()
        local.append(copy)
    for j in range(1, n_batch):
        for i in range(n_arr):
            by_line[i][j - 1].wait_recv()
            by_plane[i].append([send(rows(i, spot, j), rows(i, spot, j), who) for who, _, _ in plane])
            by_core.append(send(rows(i, spot, j), rows(i, spot, j), other[0]))
    for j in range(n_batch):
        for i in range(n_arr):
            for k, (_, _, frm) in enumerate(plane):
                by_plane[i][j][k].wait_recv()
                by_core.append(send(rows(i, frm, j), rows(i, frm, j), other[0]))
    for copy in local:
        copy.wait()
    for copy in by_core:
        copy.wait_recv()
    for i in range(n_arr):
        for copy in by_line[i] + sum(by_plane[i], []):
            copy.wait_send()
    for copy in by_core:
        copy.wait_send()


def gather_kernel(n_arr, *refs):
    ins, outs = refs[:n_arr], refs[n_arr : 2 * n_arr]
    line, plane, other = peers()
    greet(line, plane, other)
    gather_phase(ins, outs, *refs[2 * n_arr :], line, plane, other)


def gather(arrays, cid, vmem=48):
    _, n_y, n_batch = places()
    n_plane = 2 * n_y
    total = 2 * n_plane * n_batch
    n = len(arrays)
    copies = n * ((n_batch - 1) + (n_plane - 1) * n_batch + n_plane * n_batch)
    return pl.pallas_call(
        functools.partial(gather_kernel, n),
        out_shape=[jax.ShapeDtypeStruct((a.shape[0], a.shape[1] * total, a.shape[2]), a.dtype) for a in arrays],
        in_specs=[pl.BlockSpec(memory_space=pltpu.VMEM)] * n,
        out_specs=[pl.BlockSpec(memory_space=pltpu.VMEM)] * n,
        scratch_shapes=[
            pltpu.SemaphoreType.DMA((copies,)),
            pltpu.SemaphoreType.DMA((copies,)),
            pltpu.SemaphoreType.DMA((n,)),
        ],
        compiler_params=pltpu.CompilerParams(
            collective_id=cid, has_side_effects=True, vmem_limit_bytes=vmem * 2**20
        ),
        name=f"gather_{cid}",
    )(*arrays)


def reduce_phase(ins, outs, scr, send_sems, recv_sems, line, plane, other):
    n_arr = len(ins)
    _, n_y, n_batch = places()
    half, y, core, batch = coords()
    n_plane = 2 * n_y
    spot = half * n_y + y
    f32 = jnp.float32
    slots = iter(range(n_arr * (n_plane * n_batch + (n_plane - 1) * n_batch + n_batch - 1)))
    order = list(range(1, n_batch)) + [0]
    spots = [to for _, to, _ in plane] + [spot]

    def send(src, dst, who):
        slot = next(slots)
        return push(src, dst, send_sems.at[slot], recv_sems.at[slot], who)

    def rows(i, side, where, j):
        size = outs[i].shape[1]
        at = (side * n_plane + where) * n_batch + lax.rem(batch + j, n_batch)
        return pl.ds(pl.multiple_of(at * size, size), size)

    by_core, by_plane, by_line = {}, {}, {}
    for j in order:
        for p in range(n_plane):
            for i in range(n_arr):
                src = ins[i].at[:, rows(i, 1 - core, spots[p], j), :]
                by_core[i, p, j] = send(src, scr[5 * i].at[p, j], other[0])

    def mine(i, p, j):
        by_core[i, p, j].wait_recv()
        return ins[i][:, rows(i, core, spots[p], j), :].astype(f32) + scr[5 * i][p, j].astype(f32)

    for j in order:
        for p in range(n_plane - 1):
            for i in range(n_arr):
                out = scr[5 * i + 1]
                out[p, j] = mine(i, p, j).astype(out.dtype)
                by_plane[i, p, j] = send(out.at[p, j], scr[5 * i + 2].at[p, j], plane[p][0])
    totals = {}
    for j in order:
        for i in range(n_arr):
            total = mine(i, n_plane - 1, j)
            for p in range(n_plane - 1):
                by_plane[i, p, j].wait_recv()
                total = total + scr[5 * i + 2][p, j].astype(f32)
            if j:
                out = scr[5 * i + 3]
                out[j - 1] = total.astype(out.dtype)
                by_line[i, j] = send(out.at[j - 1], scr[5 * i + 4].at[j - 1], line[j - 1][0])
            else:
                outs[i][...] = total
    for i in range(n_arr):
        for j in range(1, n_batch):
            by_line[i, j].wait_recv()
            outs[i][...] += scr[5 * i + 4][j - 1].astype(f32)
    for group in (by_core, by_plane, by_line):
        for copy in group.values():
            copy.wait_send()


def reduce_scratch(arrays):
    _, n_y, n_batch = places()
    n_plane = 2 * n_y
    scratch = []
    for a in arrays:
        m, rows, w = a.shape
        size = rows // (2 * n_plane * n_batch)
        for lead in ((n_plane, n_batch), (n_plane - 1, n_batch), (n_plane - 1, n_batch), (n_batch - 1,), (n_batch - 1,)):
            scratch.append(pltpu.VMEM(lead + (m, size, w), a.dtype))
    return scratch


def exchange_kernel(n_in, columns, n_const, n_out, n_extra, reducer, compute, *refs):
    refs = list(refs)

    def take(n):
        part = refs[:n]
        del refs[:n]
        return part

    n_fetch = len(columns)
    ins, sources, consts, outs, extras = take(n_in), take(n_fetch), take(n_const), take(n_out), take(n_extra)
    totals, staged, fetched = take(n_in), take(n_out), take(n_fetch)
    send_one, recv_one, send_two, recv_two, own_sem, fetch_sem = refs[-6:]
    line, plane, other = peers()
    copies = []
    for k, (first, width) in enumerate(columns):
        copy = pltpu.make_async_copy(sources[k].at[:, pl.ds(first, width)], fetched[k], fetch_sem.at[k])
        copy.start()
        copies.append(copy)
    greet(line, plane, other)
    if ins:
        reducer(ins, totals, refs[:-6], send_one, recv_one, line, plane, other)
    for copy in copies:
        copy.wait()
    compute(totals, fetched + consts, staged, extras)
    if outs:
        gather_phase(staged, outs, send_two, recv_two, own_sem, line, plane, other)


def exchange(name, cid, arrays, fetches, consts, compute, gathered, extras, reducer=reduce_phase):
    _, n_y, n_batch = places()
    n_plane = 2 * n_y
    total = 2 * n_plane * n_batch
    f32 = jnp.float32
    n_in, n_out = len(arrays), len(gathered)
    one = max(1, n_in) * (n_plane * n_batch + (n_plane - 1) * n_batch + n_batch - 1)
    two = max(1, n_out) * (n_batch - 1 + (n_plane - 1) * n_batch + n_plane * n_batch)
    vm = pl.BlockSpec(memory_space=pltpu.VMEM)
    dma = pltpu.SemaphoreType.DMA
    columns = tuple((first, width) for _, first, width in fetches)
    return pl.pallas_call(
        functools.partial(
            exchange_kernel, n_in, columns, len(consts), n_out, len(extras), reducer, compute
        ),
        out_shape=[jax.ShapeDtypeStruct((m, rows * total, w), t) for m, rows, w, t in gathered]
        + [jax.ShapeDtypeStruct(shape, t) for shape, t in extras],
        in_specs=[vm] * n_in + [pl.BlockSpec(memory_space=pl.ANY)] * len(fetches) + [vm] * len(consts),
        out_specs=[vm] * (n_out + len(extras)),
        scratch_shapes=[pltpu.VMEM((a.shape[0], a.shape[1] // total, a.shape[2]), f32) for a in arrays]
        + [pltpu.VMEM((m, rows, w), t) for m, rows, w, t in gathered]
        + [pltpu.VMEM((a.shape[0], width), a.dtype) for a, _, width in fetches]
        + reduce_scratch(arrays)
        + [dma((one,)), dma((one,)), dma((two,)), dma((two,)), dma((max(1, n_out),)), dma((max(1, len(fetches)),))],
        compiler_params=pltpu.CompilerParams(collective_id=cid, has_side_effects=True, vmem_limit_bytes=60 * 2**20),
        name=name,
    )(*arrays, *[a for a, _, _ in fetches], *consts)


def norm_forward(x, gain):
    scale = lax.rsqrt(jnp.mean(x * x, axis=-1, keepdims=True) + EPS_NORM)
    return (x * scale * gain, scale)


def norm_backward(d_out, x, scale, gain):
    d_gain = d_out * x * scale
    d_hat = d_out * gain
    d_x = scale * (d_hat - x * scale * scale * jnp.mean(d_hat * x, axis=-1, keepdims=True))
    return (d_x, d_gain)


HEAD_SLOTS = (0, 2, 4, 6, 1, 3, 5, 8, 10, 12, 7, 9, 11, 13)
COMBOS = ((0, 4, 0), (0, 3, 4), (4, 7, 7), (3, 7, 10))
PAIRS = QUERY_HEADS // 2
TILE = 128


def column(vector):
    return jnp.transpose(jnp.broadcast_to(vector.astype(jnp.float32), (128, 128)))


def last_last(a, b):
    return lax.dot_general(a, b, (((1,), (1,)), ((), ())), preferred_element_type=jnp.float32)


def first_first(a, b):
    return lax.dot_general(a, b, (((0,), (0,)), ((), ())), preferred_element_type=jnp.float32)


def straight(a, b):
    return jnp.dot(a, b, preferred_element_type=jnp.float32)


def lookup_kernel(
    block, span, n_ref, rows_ref, table_ref, frozen_ref, flat_ref, frow_ref,
    low_ref, picked_ref, x_ref, held, rough, staged, sem,
):
    step = pl.program_id(0)
    f32, bf16 = jnp.float32, jnp.bfloat16
    low = table_ref[...].astype(bf16)
    low_ref[...] = low
    at = pl.multiple_of(step * span, span)
    held[0, pl.ds(at, span), :] = low.astype(f32)
    held[1, pl.ds(at, span), :] = frozen_ref[...].astype(f32)

    @pl.when(step == pl.num_programs(0) - 1)
    def _():
        picked_ref[...] = jnp.zeros_like(picked_ref)
        n_rows = frow_ref.shape[0]

        def tile(i, _):
            def eight(k, _):
                for j in range(8):
                    place = k * 8 + j
                    row = rows_ref[i * TILE + place]
                    for model in range(2):
                        rough[model, pl.ds(place, 1), :] = held[model, pl.ds(row, 1), :]
                return 0

            lax.fori_loop(0, TILE // 8, eight, 0)
            slot = lax.rem(i, 2)
            where = pl.ds(pl.multiple_of(i * TILE, TILE), TILE)
            copy = pltpu.make_async_copy(staged.at[slot], x_ref.at[:, where, :], sem.at[slot])

            @pl.when(i >= 2)
            def _():
                copy.wait()

            staged[slot] = rough[...].astype(bf16)
            copy.start()
            match = frow_ref[...] == jnp.broadcast_to(flat_ref[pl.ds(i, 1), :], (n_rows, TILE))
            match = jnp.where(match, 1.0, 0.0).astype(bf16)
            for model in range(2):
                picked_ref[model] = picked_ref[model] + straight(match, staged[slot, model]).astype(bf16)
            return 0

        tiles = (n_ref[0] + TILE - 1) // TILE
        lax.fori_loop(0, tiles, tile, 0)
        for k in range(2):

            @pl.when(tiles > k)
            def _():
                where = pl.ds(0, TILE)
                pltpu.make_async_copy(staged.at[k], x_ref.at[:, where, :], sem.at[k]).wait()


def lookup(n_local, rows, table, frozen, flat, frow):
    block, width = table.shape
    span = 512
    steps = pl.cdiv(block, span)
    cap = flat.shape[0] * TILE
    n_rows = frow.shape[0]
    bf16 = jnp.bfloat16
    whole = lambda shape: pl.BlockSpec(shape, lambda i: (0,) * len(shape))
    smem = pl.BlockSpec(memory_space=pltpu.SMEM)
    return pl.pallas_call(
        functools.partial(lookup_kernel, block, span),
        grid=(steps,),
        out_shape=[
            jax.ShapeDtypeStruct((block, width), bf16),
            jax.ShapeDtypeStruct((2, n_rows, width), bf16),
            jax.ShapeDtypeStruct((2, cap, width), bf16),
        ],
        in_specs=[
            smem,
            smem,
            pl.BlockSpec((span, width), lambda i: (i, 0)),
            pl.BlockSpec((span, width), lambda i: (i, 0)),
            whole(flat.shape),
            whole(frow.shape),
        ],
        out_specs=[
            pl.BlockSpec((span, width), lambda i: (i, 0)),
            whole((2, n_rows, width)),
            pl.BlockSpec(memory_space=pl.ANY),
        ],
        scratch_shapes=[
            pltpu.VMEM((2, steps * span, width), jnp.float32),
            pltpu.VMEM((2, TILE, width), jnp.float32),
            pltpu.VMEM((2, 2, TILE, width), bf16),
            pltpu.SemaphoreType.DMA((2,)),
        ],
        compiler_params=pltpu.CompilerParams(vmem_limit_bytes=60 * 2**20),
        name="lookup",
    )(n_local, rows, table, frozen, flat, frow)


def head_pieces(both, lane):
    turned = pltpu.roll(both, 64, 1)
    low, high = lane < 64, lane >= 64
    bf16 = jnp.bfloat16
    zero = jnp.zeros_like(both)
    return (
        jnp.where(low, both, zero).astype(bf16),
        jnp.where(high, turned, zero).astype(bf16),
        jnp.where(low, turned, zero).astype(bf16),
        jnp.where(high, both, zero).astype(bf16),
    )


def turn(values, positions, freq, lane, sign):
    angle = positions * freq
    cosine, sine = jnp.cos(angle), jnp.sin(angle)
    first = lax.rem(lane, 64) < 32
    mixed = jnp.where(first, -sign * pltpu.roll(values, 96, 1), sign * pltpu.roll(values, 32, 1))
    return values * cosine + mixed * sine


def allowed_of(frow, flat, r, length):
    flat = jnp.broadcast_to(flat, frow.shape)
    return jnp.where((flat <= frow) & (flat >= r * length), 1.0, 0.0)


def attend_kernel(
    length, rp, n_ref, lo_ref, hi_ref, q_ref, x_ref, w_ref, gain_ref, bias_ref, freq_ref, frow_ref, flat_ref, pos_ref,
    o_ref, st_ref, kv_ref, xbuf, kvbuf, m_scr, l_scr, o_scr, sem,
):
    model = pl.program_id(0)
    f32, bf16 = jnp.float32, jnp.bfloat16
    lane = lax.broadcasted_iota(jnp.int32, (TILE, 128), 1)
    lane_r = lax.broadcasted_iota(jnp.int32, (rp, 128), 1)
    m_scr[...] = jnp.full(m_scr.shape, -1e30, f32)
    l_scr[...] = jnp.zeros_like(l_scr)
    o_scr[...] = jnp.zeros_like(o_scr)

    tiles = (n_ref[0] + TILE - 1) // TILE

    def fetch(i):
        slot = lax.rem(i, 2)
        at = pl.ds(pl.multiple_of(i * TILE, TILE), TILE)
        return pltpu.make_async_copy(x_ref.at[model, at, :], xbuf.at[slot], sem.at[slot])

    @pl.when(tiles > 0)
    def _():
        fetch(0).start()

    def tile(i, _):
        at = pl.ds(pl.multiple_of(i * TILE, TILE), TILE)

        @pl.when(i + 1 < tiles)
        def _():
            fetch(i + 1).start()

        fetch(i).wait()
        x = xbuf[lax.rem(i, 2)].astype(f32)
        scale = lax.rsqrt(jnp.mean(x * x, axis=-1, keepdims=True) + EPS_NORM)
        normed = (x * scale * gain_ref[0]).astype(bf16)
        mixed = straight(normed, w_ref[...]) + bias_ref[0]
        key = turn(mixed[:, :128], column(pos_ref[pl.ds(i, 1), :]), freq_ref[...], lane, 1.0)
        key = key.astype(bf16)
        value = mixed[:, 128:].astype(bf16)
        kvbuf[...] = jnp.concatenate([key, value], axis=1)
        out = pltpu.make_async_copy(kvbuf, kv_ref.at[model, at, :], sem.at[2])
        out.start()
        keys = head_pieces(key.astype(f32), lane)
        values = head_pieces(value.astype(f32), lane)
        one = jnp.ones((TILE, 128), bf16)
        values = tuple(jnp.where((lane < 64) == (c % 2 == 0), v, one) for c, v in enumerate(values))
        flat = flat_ref[pl.ds(i, 1), :]

        def rollout(r, _):
            rows = pl.ds(pl.multiple_of(r * rp, rp), rp)
            ok = allowed_of(frow_ref[rows, :], flat, r, length)[None]
            shift = (ok - 1.0) * 1e30
            falls, adds = {}, {}
            for c, (p0, p1, s0) in enumerate(COMBOS):
                n = p1 - p0
                query = q_ref[p0:p1, rows, :].reshape(n * rp, 128)
                score = last_last(query, keys[c]).reshape(n, rp, TILE) * HEAD_SIZE ** (-0.5)
                score = score * ok + shift
                old = m_scr[s0 : s0 + n, rows, :]
                new = jnp.maximum(old, jnp.max(score, axis=-1, keepdims=True))
                m_scr[s0 : s0 + n, rows, :] = new
                fall = old - new
                prob = jnp.exp(score - new) * ok
                add = straight(prob.astype(bf16).reshape(n * rp, TILE), values[c]).reshape(n, rp, 128)
                for k in range(n):
                    falls[p0 + k, c % 2] = fall[k]
                    adds[p0 + k, c % 2] = add[k]
            for p in range(PAIRS):
                alpha = jnp.exp(jnp.where(lane_r < 64, falls[p, 0], falls[p, 1]))
                turned = pltpu.roll(alpha, 64, 1)
                o_scr[p, rows, :] = o_scr[p, rows, :] * alpha + jnp.where(lane_r < 64, adds[p, 0], adds[p, 1])
                l_scr[p, rows, :] = l_scr[p, rows, :] * turned + jnp.where(lane_r < 64, adds[p, 1], adds[p, 0])
            return 0

        lax.fori_loop(lo_ref[i], hi_ref[i] + 1, rollout, 0)
        out.wait()
        return 0

    lax.fori_loop(0, tiles, tile, 0)

    def leave(r, _):
        rows = pl.ds(pl.multiple_of(r * rp, rp), rp)
        o_ref[:, rows, :] = o_scr[:, rows, :].astype(bf16)
        tops = jnp.full((rp, 128), -1e30, f32)
        totals = jnp.zeros((rp, 128), f32)
        for slot, head in enumerate(HEAD_SLOTS):
            tops = jnp.where(lane_r == head, m_scr[slot, rows, :], tops)
            held = l_scr[head // 2, rows, :]
            held = held[:, 64:65] if head % 2 == 0 else held[:, 0:1]
            totals = jnp.where(lane_r == head, held, totals)
        st_ref[0, rows, :] = tops
        st_ref[1, rows, :] = totals
        return 0

    lax.fori_loop(0, m_scr.shape[1] // rp, leave, 0)


def attend(n_local, lo, hi, q, x, w, gain, bias, freq, frow, flat, pos, length, rp):
    n_rows = q.shape[1]
    width = x.shape[2]
    cap = x.shape[1]
    bf16 = jnp.bfloat16
    whole = lambda shape: pl.BlockSpec(shape, lambda i: (0,) * len(shape))
    smem = pl.BlockSpec(memory_space=pltpu.SMEM)
    anyw = pl.BlockSpec(memory_space=pl.ANY)
    model = lambda shape: pl.BlockSpec(shape, lambda i: (i, 0, 0))
    return pl.pallas_call(
        functools.partial(attend_kernel, length, rp),
        grid=(2,),
        out_shape=[
            jax.ShapeDtypeStruct((2 * PAIRS, n_rows, 128), bf16),
            jax.ShapeDtypeStruct((4, n_rows, 128), jnp.float32),
            jax.ShapeDtypeStruct((2, cap, 256), bf16),
        ],
        in_specs=[
            smem, smem, smem, model((PAIRS, n_rows, 128)), anyw, pl.BlockSpec((width, 256), lambda i: (0, i)), model((1, 1, width)),
            model((1, 1, 256)), whole((1, 128)), whole(frow.shape), whole(flat.shape), whole(pos.shape),
        ],
        out_specs=[model((PAIRS, n_rows, 128)), model((2, n_rows, 128)), anyw],
        scratch_shapes=[
            pltpu.VMEM((2, TILE, width), bf16),
            pltpu.VMEM((TILE, 256), bf16),
            pltpu.VMEM((QUERY_HEADS, n_rows, 128), jnp.float32),
            pltpu.VMEM((PAIRS, n_rows, 128), jnp.float32),
            pltpu.VMEM((PAIRS, n_rows, 128), jnp.float32),
            pltpu.SemaphoreType.DMA((3,)),
        ],
        compiler_params=pltpu.CompilerParams(vmem_limit_bytes=62 * 2**20),
        name="attend",
    )(n_local, lo, hi, q, x, w, gain, bias, freq, frow, flat, pos)


def attend_back_kernel(
    length, rp, n_ref, lo_ref, hi_ref, q_ref, do_ref, st_ref, x_ref, kv_ref, w_ref, gain_ref, freq_ref, frow_ref, flat_ref,
    pos_ref, dq_ref, gkv_ref, gs_ref, gb_ref, dx_ref, xbuf, kvbuf, dxbuf, dq_scr, dk_scr, dv_scr, sem,
):
    f32, bf16 = jnp.float32, jnp.bfloat16
    lane = lax.broadcasted_iota(jnp.int32, (TILE, 128), 1)
    dq_scr[...] = jnp.zeros_like(dq_scr)
    gkv_ref[...] = jnp.zeros_like(gkv_ref)
    gs_ref[...] = jnp.zeros_like(gs_ref)
    gb_ref[...] = jnp.zeros_like(gb_ref)

    tiles = (n_ref[0] + TILE - 1) // TILE

    def fetch(i):
        slot = lax.rem(i, 2)
        at = pl.ds(pl.multiple_of(i * TILE, TILE), TILE)
        return (
            pltpu.make_async_copy(x_ref.at[0, at, :], xbuf.at[slot], sem.at[slot]),
            pltpu.make_async_copy(kv_ref.at[0, at, :], kvbuf.at[slot], sem.at[2 + slot]),
        )

    def leave(i):
        slot = lax.rem(i, 2)
        at = pl.ds(pl.multiple_of(i * TILE, TILE), TILE)
        return pltpu.make_async_copy(dxbuf.at[slot], dx_ref.at[at, :], sem.at[4 + slot])

    @pl.when(tiles > 0)
    def _():
        for copy in fetch(0):
            copy.start()

    def tile(i, _):
        slot = lax.rem(i, 2)

        @pl.when(i + 1 < tiles)
        def _():
            for copy in fetch(i + 1):
                copy.start()

        for copy in fetch(i):
            copy.wait()
        keys = head_pieces(kvbuf[slot, :, :128].astype(f32), lane)
        values = head_pieces(kvbuf[slot, :, 128:].astype(f32), lane)
        flat = flat_ref[pl.ds(i, 1), :]
        dk_scr[...] = jnp.zeros_like(dk_scr)
        dv_scr[...] = jnp.zeros_like(dv_scr)

        def rollout(r, _):
            rows = pl.ds(pl.multiple_of(r * rp, rp), rp)
            ok = allowed_of(frow_ref[rows, :], flat, r, length)[None]
            shift = (ok - 1.0) * 1e30
            stats = st_ref[rows, :]
            adds = {}
            for c, (p0, p1, s0) in enumerate(COMBOS):
                n = p1 - p0
                heads = HEAD_SLOTS[s0 : s0 + n]
                query = q_ref[p0:p1, rows, :].reshape(n * rp, 128)
                back = do_ref[p0:p1, rows, :].reshape(n * rp, 128)
                lse = jnp.stack([stats[:, h : h + 1] for h in heads])
                delta = jnp.stack([stats[:, 16 + h : 17 + h] for h in heads])
                score = last_last(query, keys[c]).reshape(n, rp, TILE) * HEAD_SIZE ** (-0.5)
                prob = jnp.exp(score * ok + shift - lse)
                d_prob = last_last(back, values[c]).reshape(n, rp, TILE)
                d_score = (prob * (d_prob - delta)).astype(bf16).reshape(n * rp, TILE)
                add = straight(d_score, keys[c]).reshape(n, rp, 128)
                dk_scr[c] += first_first(d_score, query)
                dv_scr[c] += first_first(prob.astype(bf16).reshape(n * rp, TILE), back)
                for k in range(n):
                    adds[p0 + k, c % 2] = add[k]
            for p in range(PAIRS):
                dq_scr[p, rows, :] = dq_scr[p, rows, :] + adds[p, 0] + adds[p, 1]
            return 0

        lax.fori_loop(lo_ref[i], hi_ref[i] + 1, rollout, 0)

        def joined(scr):
            return jnp.where(lane < 64, scr[0] + pltpu.roll(scr[1], 64, 1), scr[3] + pltpu.roll(scr[2], 64, 1))

        d_key = turn(joined(dk_scr) * HEAD_SIZE ** (-0.5), column(pos_ref[pl.ds(i, 1), :]), freq_ref[...], lane, -1.0)
        d_mixed = jnp.concatenate([d_key, joined(dv_scr)], axis=1).astype(bf16)
        x = xbuf[slot].astype(f32)
        scale = lax.rsqrt(jnp.mean(x * x, axis=-1, keepdims=True) + EPS_NORM)
        gain = gain_ref[0]
        normed = (x * scale * gain).astype(bf16)
        gkv_ref[...] += first_first(normed, d_mixed)
        gb_ref[...] += jnp.sum(d_mixed.astype(f32).reshape(TILE // 8, 8, 256), axis=0)
        d_normed = last_last(d_mixed, w_ref[...])
        gs_ref[...] += jnp.sum((d_normed * x * scale).reshape(TILE // 8, 8, x.shape[1]), axis=0)
        d_hat = d_normed * gain
        d_x = scale * (d_hat - x * scale * scale * jnp.mean(d_hat * x, axis=-1, keepdims=True))

        @pl.when(i >= 2)
        def _():
            leave(i - 2).wait()

        dxbuf[slot] = d_x.astype(bf16)
        leave(i).start()
        return 0

    lax.fori_loop(0, tiles, tile, 0)
    for k in range(2):

        @pl.when(tiles > k)
        def _():
            leave(tiles - 1 - k).wait()

    dq_ref[...] = (dq_scr[...] * HEAD_SIZE ** (-0.5)).astype(bf16)


def attend_back(n_local, lo, hi, q, do, stats, x, kv, w, gain, freq, frow, flat, pos, length, rp):
    n_rows = q.shape[1]
    width = x.shape[2]
    cap = x.shape[1]
    bf16, f32 = jnp.bfloat16, jnp.float32
    whole = lambda shape: pl.BlockSpec(shape, lambda i: (0,) * len(shape))
    smem = pl.BlockSpec(memory_space=pltpu.SMEM)
    anyw = pl.BlockSpec(memory_space=pl.ANY)
    return pl.pallas_call(
        functools.partial(attend_back_kernel, length, rp),
        grid=(1,),
        out_shape=[
            jax.ShapeDtypeStruct((PAIRS, n_rows, 128), bf16),
            jax.ShapeDtypeStruct((width, 256), f32),
            jax.ShapeDtypeStruct((8, width), f32),
            jax.ShapeDtypeStruct((8, 256), f32),
            jax.ShapeDtypeStruct((cap, width), bf16),
        ],
        in_specs=[
            smem, smem, smem, whole((PAIRS, n_rows, 128)), whole((PAIRS, n_rows, 128)), whole((n_rows, 128)), anyw, anyw,
            whole((width, 256)), whole((1, 1, width)), whole((1, 128)), whole(frow.shape), whole(flat.shape),
            whole(pos.shape),
        ],
        out_specs=[
            whole((PAIRS, n_rows, 128)), whole((width, 256)), whole((8, width)), whole((8, 256)), anyw,
        ],
        scratch_shapes=[
            pltpu.VMEM((2, TILE, width), bf16),
            pltpu.VMEM((2, TILE, 256), bf16),
            pltpu.VMEM((2, TILE, width), bf16),
            pltpu.VMEM((PAIRS, n_rows, 128), f32),
            pltpu.VMEM((4, TILE, 128), f32),
            pltpu.VMEM((4, TILE, 128), f32),
            pltpu.SemaphoreType.DMA((6,)),
        ],
        compiler_params=pltpu.CompilerParams(vmem_limit_bytes=60 * 2**20),
        name="attend_back",
    )(n_local, lo, hi, q, do, stats, x, kv, w, gain, freq, frow, flat, pos)


def table_grad_kernel(
    block, span, n_ref, rows_ref, dl_ref, af_ref, drow_ref, frow_ref, flat_ref, dx_ref,
    g_ref, sq_ref, added, moved, rough, sem,
):
    step = pl.program_id(0)
    f32, bf16 = jnp.float32, jnp.bfloat16

    @pl.when(step == 0)
    def _():
        sq_ref[...] = jnp.zeros_like(sq_ref)
        added[...] = jnp.zeros_like(added)
        n_rows = drow_ref.shape[0]

        tiles = (n_ref[0] + TILE - 1) // TILE

        def fetch(i):
            slot = lax.rem(i, 2)
            at = pl.ds(pl.multiple_of(i * TILE, TILE), TILE)
            return pltpu.make_async_copy(dx_ref.at[at, :], moved.at[slot], sem.at[slot])

        @pl.when(tiles > 0)
        def _():
            fetch(0).start()

        def tile(i, _):
            @pl.when(i + 1 < tiles)
            def _():
                fetch(i + 1).start()

            token = column(flat_ref[pl.ds(i, 1), :])
            token = jnp.concatenate([token] * (n_rows // 128), axis=1)
            match = jnp.where(token == jnp.broadcast_to(frow_ref[...], (TILE, n_rows)), 1.0, 0.0).astype(bf16)
            own = straight(match, drow_ref[...])
            fetch(i).wait()
            rough[...] = own + moved[lax.rem(i, 2)].astype(f32)

            def eight(k, _):
                for j in range(8):
                    place = k * 8 + j
                    row = pl.ds(rows_ref[i * TILE + place], 1)
                    added[row, :] = added[row, :] + rough[pl.ds(place, 1), :]
                return 0

            lax.fori_loop(0, TILE // 8, eight, 0)
            return 0

        lax.fori_loop(0, tiles, tile, 0)

    inside = step * span + lax.broadcasted_iota(jnp.int32, (span, 1), 0) < block
    logit = jnp.where(inside, dl_ref[...].astype(f32), 0.0).astype(bf16)
    total = straight(logit, af_ref[...]) + added[pl.ds(pl.multiple_of(step * span, span), span), :]
    g_ref[...] = total.astype(bf16)
    square = total * total
    sq_ref[...] += jnp.sum(square.reshape(span // 8, 8, square.shape[1]), axis=0)


def table_grad(n_local, rows, dl, af, drow, frow, flat, dx, block):
    n_rows, width = af.shape
    span = 512
    steps = pl.cdiv(block, span)
    whole = lambda shape: pl.BlockSpec(shape, lambda i: (0,) * len(shape))
    smem = pl.BlockSpec(memory_space=pltpu.SMEM)
    return pl.pallas_call(
        functools.partial(table_grad_kernel, block, span),
        grid=(steps,),
        out_shape=[
            jax.ShapeDtypeStruct((block, width), jnp.bfloat16),
            jax.ShapeDtypeStruct((8, width), jnp.float32),
        ],
        in_specs=[
            smem, smem,
            pl.BlockSpec((span, n_rows), lambda i: (i, 0)),
            whole(af.shape), whole(drow.shape), whole(frow.shape), whole(flat.shape),
            pl.BlockSpec(memory_space=pl.ANY),
        ],
        out_specs=[pl.BlockSpec((span, width), lambda i: (i, 0)), whole((8, width))],
        scratch_shapes=[
            pltpu.VMEM((steps * span, width), jnp.float32),
            pltpu.VMEM((2, TILE, width), jnp.bfloat16),
            pltpu.VMEM((TILE, width), jnp.float32),
            pltpu.SemaphoreType.DMA((2,)),
        ],
        compiler_params=pltpu.CompilerParams(vmem_limit_bytes=56 * 2**20),
        name="table_grad",
    )(n_local, rows, dl, af, drow, frow, flat, dx)


def spread_kernel(own_ref, frozen_ref, out_ref):
    devices, _, _, wide = out_ref.shape
    units, rows = wide // 2, own_ref.shape[0]
    bf16 = jnp.bfloat16
    out_ref[...] = jnp.zeros_like(out_ref)
    for side in range(2):
        for d in range(devices):
            at = (side * devices + d) * units
            out_ref[d, 0, :rows, side * units : (side + 1) * units] = own_ref[:, at : at + units].astype(bf16)
            out_ref[d, 1, :rows, side * units : (side + 1) * units] = frozen_ref[:, at : at + units]


def spread(own, frozen, devices, units, rows_up):
    vm = pl.BlockSpec(memory_space=pltpu.VMEM)
    return pl.pallas_call(
        spread_kernel,
        out_shape=jax.ShapeDtypeStruct((devices, 2, rows_up, 2 * units), jnp.bfloat16),
        in_specs=[vm, vm],
        out_specs=vm,
        compiler_params=pltpu.CompilerParams(vmem_limit_bytes=48 * 2**20),
        name="spread",
    )(own, frozen)


def join_kernel(g_ref, out_ref):
    devices, _, wide = g_ref.shape
    units, rows = wide // 2, out_ref.shape[0]
    for side in range(2):
        for d in range(devices):
            at = (side * devices + d) * units
            out_ref[:, at : at + units] = g_ref[d, :rows, side * units : (side + 1) * units].astype(jnp.float32)


def join(g, rows, units):
    vm = pl.BlockSpec(memory_space=pltpu.VMEM)
    return pl.pallas_call(
        join_kernel,
        out_shape=jax.ShapeDtypeStruct((rows, 2 * units * g.shape[0]), jnp.float32),
        in_specs=[vm],
        out_specs=vm,
        compiler_params=pltpu.CompilerParams(vmem_limit_bytes=48 * 2**20),
        name="join",
    )(g)


def head_kernel(block, span, own_ref, frozen_ref, af_ref, aim_ref, st_ref, logit_ref):
    step = pl.program_id(0)
    f32 = jnp.float32
    n_rows = af_ref.shape[1]

    @pl.when(step == 0)
    def _():
        st_ref[...] = jnp.zeros_like(st_ref)
        for model in range(2):
            st_ref[3 * model : 3 * model + 1, :] = jnp.full((1, n_rows), -1e30, f32)

    row = step * span + lax.broadcasted_iota(jnp.int32, (span, n_rows), 0)
    hit = (row == aim_ref[...]) & (row < block)
    for model, ref in enumerate((own_ref, frozen_ref)):
        logit = jnp.where(row < block, last_last(ref[...], af_ref[model]), -1e30)
        if model == 0:
            logit_ref[...] = logit
        top, total, found = (pl.ds(3 * model + k, 1) for k in range(3))
        new = jnp.maximum(st_ref[top, :], jnp.max(logit, axis=0, keepdims=True))
        fall = jnp.exp(st_ref[top, :] - new)
        st_ref[total, :] = st_ref[total, :] * fall + jnp.sum(jnp.exp(logit - new), axis=0, keepdims=True)
        st_ref[top, :] = new
        st_ref[found, :] += jnp.sum(jnp.where(hit, logit, 0.0), axis=0, keepdims=True)


def head(own, frozen, af, aim):
    block, width = own.shape
    n_rows = af.shape[1]
    span = 512
    whole = lambda shape: pl.BlockSpec(shape, lambda i: (0,) * len(shape))
    return pl.pallas_call(
        functools.partial(head_kernel, block, span),
        grid=(pl.cdiv(block, span),),
        out_shape=[jax.ShapeDtypeStruct((8, n_rows), jnp.float32), jax.ShapeDtypeStruct((block, n_rows), jnp.float32)],
        in_specs=[
            pl.BlockSpec((span, width), lambda i: (i, 0)), pl.BlockSpec((span, width), lambda i: (i, 0)),
            whole(af.shape), whole(aim.shape),
        ],
        out_specs=[whole((8, n_rows)), pl.BlockSpec((span, n_rows), lambda i: (i, 0))],
        compiler_params=pltpu.CompilerParams(vmem_limit_bytes=56 * 2**20),
        name="head",
    )(own, frozen, af, aim)


def head_back_kernel(block, span, logit_ref, own_ref, lse_ref, dlp_ref, aim_ref, dl_ref, d_af_ref, acc):
    step = pl.program_id(0)
    f32, bf16 = jnp.float32, jnp.bfloat16

    @pl.when(step == 0)
    def _():
        acc[...] = jnp.zeros_like(acc)

    row = step * span + lax.broadcasted_iota(jnp.int32, logit_ref.shape, 0)
    hot = jnp.where(row == aim_ref[...], 1.0, 0.0)
    d_logit = dlp_ref[...] * (hot - jnp.exp(logit_ref[...] - lse_ref[...]))
    d_logit = jnp.where(row < block, d_logit, 0.0).astype(bf16)
    dl_ref[...] = d_logit
    inside = step * span + lax.broadcasted_iota(jnp.int32, (span, 1), 0) < block
    table = jnp.where(inside, own_ref[...].astype(f32), 0.0).astype(bf16)
    acc[...] += first_first(d_logit, table)

    @pl.when(step == pl.num_programs(0) - 1)
    def _():
        d_af_ref[0] = acc[...].astype(bf16)


def head_back(logits, own, lse, dlp, aim):
    block, width = own.shape
    n_rows = logits.shape[1]
    span = 512
    whole = lambda shape: pl.BlockSpec(shape, lambda i: (0,) * len(shape))
    return pl.pallas_call(
        functools.partial(head_back_kernel, block, span),
        grid=(pl.cdiv(block, span),),
        out_shape=[
            jax.ShapeDtypeStruct((block, n_rows), jnp.bfloat16),
            jax.ShapeDtypeStruct((1, n_rows, width), jnp.bfloat16),
        ],
        in_specs=[
            pl.BlockSpec((span, n_rows), lambda i: (i, 0)), pl.BlockSpec((span, width), lambda i: (i, 0)),
            whole(lse.shape), whole(dlp.shape), whole(aim.shape),
        ],
        out_specs=[pl.BlockSpec((span, n_rows), lambda i: (i, 0)), whole((1, n_rows, width))],
        scratch_shapes=[pltpu.VMEM((n_rows, width), jnp.float32)],
        compiler_params=pltpu.CompilerParams(vmem_limit_bytes=56 * 2**20),
        name="head_back",
    )(logits, own, lse, dlp, aim)


def blend(parts, lane):
    f32 = jnp.float32
    n_models = len(parts[0][1]) // 2
    planes, stats = [], []
    for model in range(n_models):
        tops = [p[1][2 * model] for p in parts]
        top = tops[0]
        for t in tops[1:]:
            top = jnp.maximum(top, t)
        weights = [jnp.exp(t - top) for t in tops]
        stats += [top, sum(p[1][2 * model + 1] * w for p, w in zip(parts, weights))]
        for pair in range(PAIRS):
            acc = None
            for p, w in zip(parts, weights):
                each = jnp.where(lane < 64, w[:, 2 * pair : 2 * pair + 1], w[:, 2 * pair + 1 : 2 * pair + 2])
                term = p[0][model * PAIRS + pair].astype(f32) * each
                acc = term if acc is None else acc + term
            planes.append(acc)
    return planes, stats


def mix_phase(ins, outs, scr, send_sems, recv_sems, line, plane, other):
    (o_ref, st_ref), (oo_ref, so_ref) = ins, outs
    core_o, sum_o, plane_o, keep_o, line_o, core_s, sum_s, plane_s, keep_s, line_s = scr
    _, n_y, n_batch = places()
    half, y, core, batch = coords()
    n_plane = 2 * n_y
    spot = half * n_y + y
    size = oo_ref.shape[1]
    lane = lax.broadcasted_iota(jnp.int32, (size, 128), 1)
    order = list(range(1, n_batch)) + [0]
    spots = [to for _, to, _ in plane] + [spot]
    slots = iter(range(2 * (n_plane * n_batch + (n_plane - 1) * n_batch + n_batch - 1)))

    def send(src, dst, who):
        slot = next(slots)
        return push(src, dst, send_sems.at[slot], recv_sems.at[slot], who)

    def rows(side, where, j):
        at = (side * n_plane + where) * n_batch + lax.rem(batch + j, n_batch)
        return pl.ds(pl.multiple_of(at * size, size), size)

    def store(o, s, merged):
        for k, value in enumerate(merged[0]):
            o[k] = value.astype(o.dtype)
        for k, value in enumerate(merged[1]):
            s[k] = value

    by_core, by_plane, by_line = {}, {}, {}
    for j in order:
        for p in range(n_plane):
            at = rows(1 - core, spots[p], j)
            by_core[p, j] = (
                send(o_ref.at[:, at, :], core_o.at[p, j], other[0]), send(st_ref.at[:, at, :], core_s.at[p, j], other[0])
            )

    def mine(p, j):
        at = rows(core, spots[p], j)
        for copy in by_core[p, j]:
            copy.wait_recv()
        return blend([(o_ref[:, at, :], st_ref[:, at, :]), (core_o[p, j], core_s[p, j])], lane)

    for j in order:
        for p in range(n_plane - 1):
            store(sum_o.at[p, j], sum_s.at[p, j], mine(p, j))
            by_plane[p, j] = (
                send(sum_o.at[p, j], plane_o.at[p, j], plane[p][0]), send(sum_s.at[p, j], plane_s.at[p, j], plane[p][0])
            )
    for j in order:
        parts = [mine(n_plane - 1, j)]
        for p in range(n_plane - 1):
            for copy in by_plane[p, j]:
                copy.wait_recv()
            parts.append((plane_o[p, j], plane_s[p, j]))
        merged = blend(parts, lane)
        if j:
            store(keep_o.at[j - 1], keep_s.at[j - 1], merged)
            by_line[j] = (
                send(keep_o.at[j - 1], line_o.at[j - 1], line[j - 1][0]),
                send(keep_s.at[j - 1], line_s.at[j - 1], line[j - 1][0]),
            )
    parts = [merged]
    for j in range(1, n_batch):
        for copy in by_line[j]:
            copy.wait_recv()
        parts.append((line_o[j - 1], line_s[j - 1]))
    store(oo_ref, so_ref, blend(parts, lane))
    for group in (by_core, by_plane, by_line):
        for pair in group.values():
            for copy in pair:
                copy.wait_send()


def low(x):
    return x.astype(jnp.bfloat16)


def split_dot(x, w):
    high = low(x)
    return straight(high, w) + straight(low(x - high.astype(jnp.float32)), w)


def turn_rows(x, cosine, sine, sign):
    lane = lax.broadcasted_iota(jnp.int32, x.shape, 1)
    mixed = jnp.where(lax.rem(lane, 64) < 32, -sign * pltpu.roll(x, 96, 1), sign * pltpu.roll(x, 32, 1))
    return x * cosine + mixed * sine


def queries(totals, consts, staged, extras):
    w_one, w_two, places_ref, gain_ref, bias_ref, cosine_ref, sine_ref, x_ref = consts
    q_ref, a1_ref = staged
    for model, w_ref in enumerate((w_one, w_two)):
        normed, _ = norm_forward(x_ref[model], gain_ref[model])
        normed = low(normed)
        if model == 0:
            a1_ref[0] = normed
        mixed = straight(low(straight(normed, places_ref[...])), w_ref[...]) + bias_ref[model]
        for p in range(PAIRS):
            part = turn_rows(mixed[:, 128 * p : 128 * p + 128], cosine_ref[...], sine_ref[...], 1.0)
            q_ref[model * PAIRS + p] = low(part)


def attended(totals, consts, staged, extras):
    w_one, w_two, places_ref, gain_ref, x_ref = consts
    a2_ref, o_ref = staged
    x1_ref, own_ref, lse_ref = extras
    lane = lax.broadcasted_iota(jnp.int32, (own_ref.shape[0], 128), 1)
    for model, w_ref in enumerate((w_one, w_two)):
        total = totals[1][2 * model + 1]
        total = jnp.where(lane < QUERY_HEADS, total, 1.0)
        if model == 0:
            lse_ref[...] = totals[1][0] + jnp.log(total)
        share = 1.0 / total
        parts = []
        for p in range(PAIRS):
            each = jnp.where(lane < 64, share[:, 2 * p : 2 * p + 1], share[:, 2 * p + 1 : 2 * p + 2])
            parts.append(low(totals[0][model * PAIRS + p] * each))
        o = jnp.concatenate(parts, axis=1)
        if model == 0:
            o_ref[0] = o
            own_ref[...] = o
        x1 = x_ref[model] + straight(low(straight(o, places_ref[...])), w_ref[...])
        x1_ref[model] = x1
        a2, _ = norm_forward(x1, gain_ref[model])
        a2_ref[model] = low(straight(low(a2), places_ref[...]))


def finals(totals, consts, staged, extras):
    gain_ref, x1_ref = consts
    for model in range(2):
        x2 = x1_ref[model] + totals[0][model]
        extras[0][model] = x2
        af, _ = norm_forward(x2, gain_ref[model])
        staged[0][model] = low(af)


def scale_of(x):
    return lax.rsqrt(jnp.mean(x * x, axis=-1, keepdims=True) + EPS_NORM)


def finals_back(totals, consts, staged, extras):
    gain_ref, x2_ref = consts
    x2 = x2_ref[0]
    d_out, d_gain = norm_backward(totals[0][0], x2, scale_of(x2), gain_ref[0])
    staged[0][0] = low(d_out)
    extras[0][...] = d_out
    extras[1][...] = jnp.sum(d_gain, axis=0, keepdims=True)


def attended_back(totals, consts, staged, extras):
    w_ref, from_ref, gain_ref, x1_ref, d_out_ref, o_ref, lse_ref = consts
    d_attn_ref, d_o_ref, stats_ref = staged
    d_mid_ref, d_gain_ref = extras
    x1 = x1_ref[0]
    d_mid, d_gain = norm_backward(split_dot(totals[0][0], from_ref[...]), x1, scale_of(x1), gain_ref[0])
    d_mid = d_mid + d_out_ref[...]
    d_mid_ref[...] = d_mid
    d_gain_ref[...] = jnp.sum(d_gain, axis=0, keepdims=True)
    d_attn = low(d_mid)
    d_attn_ref[0] = d_attn
    d_o = low(straight(low(last_last(d_attn, w_ref[...])), from_ref[...]))
    product = d_o.astype(jnp.float32) * o_ref[...].astype(jnp.float32)
    lane = lax.broadcasted_iota(jnp.int32, (d_o.shape[0], 128), 1)
    stats = jnp.where(lane < QUERY_HEADS, lse_ref[...], 0.0)
    for p in range(PAIRS):
        d_o_ref[p] = d_o[:, 128 * p : 128 * p + 128]
        part = product[:, 128 * p : 128 * p + 128]
        first = jnp.sum(jnp.where(lane < 64, part, 0.0), axis=-1, keepdims=True)
        second = jnp.sum(jnp.where(lane < 64, 0.0, part), axis=-1, keepdims=True)
        stats = jnp.where(lane == 16 + 2 * p, first, stats)
        stats = jnp.where(lane == 17 + 2 * p, second, stats)
    stats_ref[0] = stats


def queries_back(totals, consts, staged, extras):
    w_ref, from_ref, gain_ref, x_ref, d_mid_ref, cosine_ref, sine_ref = consts
    dq_ref, d_row_ref = staged
    g_kv_ref, d_gain_ref, d_bias_ref = extras
    g_kv_ref[...] = totals[1][0]
    parts = [turn_rows(totals[0][p], cosine_ref[...], sine_ref[...], -1.0) for p in range(PAIRS)]
    dq = low(jnp.concatenate(parts, axis=1))
    dq_ref[0] = dq
    d_bias_ref[...] = jnp.sum(dq.astype(jnp.float32), axis=0, keepdims=True)
    x = x_ref[0]
    d_row, d_gain = norm_backward(split_dot(last_last(dq, w_ref[...]), from_ref[...]), x, scale_of(x), gain_ref[0])
    d_row_ref[0] = low(d_row + d_mid_ref[...])
    d_gain_ref[...] = jnp.sum(d_gain, axis=0, keepdims=True)


def keep(totals, consts, staged, extras):
    for total, extra in zip(totals, extras):
        extra[...] = total[...]


AXES = ("half", "mp", "batch")


def frequencies():
    half_size = HEAD_SIZE // 2
    return THETA ** (-(jnp.arange(half_size, dtype=jnp.float32) * 2.0) / HEAD_SIZE)


def bmm(x, w):
    return jnp.stack([jnp.dot(x[i], w[i], preferred_element_type=jnp.float32) for i in range(2)])


def body(
    tokens, lengths, labels, scored, qkv_weight, out_weight, gu_weight, down_weight, embed_weight, small_params,
    moment_qkv, moment_out, moment_gu, moment_down, moment_embed, moment_small,
    square_qkv, square_out, square_gu, square_down, square_embed, square_small,
    ref_qkv, ref_out, ref_gu, ref_down, ref_embed, ref_small,
):
    masters = (qkv_weight, out_weight, gu_weight, down_weight, embed_weight, small_params)
    firsts = (moment_qkv, moment_out, moment_gu, moment_down, moment_embed, moment_small)
    seconds = (square_qkv, square_out, square_gu, square_down, square_embed, square_small)
    bf16, f32, i32 = jnp.bfloat16, jnp.float32, jnp.int32
    n_mp, n_batch = lax.axis_size("mp"), lax.axis_size("batch")
    devices = 2 * n_mp * n_batch
    n_y = n_mp // 2
    block = embed_weight.shape[0]
    feats = qkv_weight.shape[0]
    units = down_weight.shape[0]
    rollouts = MICRO * n_batch
    length = n_mp * TOK
    rp = n_mp * P_SIZE
    n_rows = rollouts * rp
    own_rows = n_rows // devices
    lin = lax.axis_index(AXES)
    com = comm_index()
    base = lin * block

    feats_up = -(-feats // 16) * 16

    def to_up(x):
        return jnp.pad(x, ((0, feats_up - feats), (0, 0)))

    feat = jnp.arange(MODEL_WIDTH, dtype=i32)
    padded = jnp.arange(devices * feats_up, dtype=i32)
    to_order = (padded[None, :] == (feat // feats * feats_up + feat % feats)[:, None]).astype(bf16)
    from_order = (padded[:, None] == (feat // feats * feats_up + feat % feats)[None, :]).astype(bf16)

    def placed(x):
        x = jnp.pad(x.astype(bf16), ((0, 0), (0, 128 - x.shape[1])))
        x = jnp.roll(x, lin * small_params.shape[1], axis=1)
        return jnp.pad(x, ((0, -x.shape[0] % feats_up), (0, 0)))

    qkv_low = qkv_weight.astype(bf16)
    early = to_up(
        jnp.concatenate(
            [qkv_low[:, :MODEL_WIDTH], ref_qkv[:, :MODEL_WIDTH], qkv_low[:, MODEL_WIDTH:], ref_qkv[:, MODEL_WIDTH:]], axis=1
        )
    )
    smalls = [placed(small_params), placed(ref_small)]
    tall = smalls[0].shape[0] // feats_up
    smalls = [x.reshape(tall, feats_up, 128)[k] for x in smalls for k in range(tall)]
    early = lax.all_gather(jnp.concatenate([early] + smalls, axis=1), AXES, axis=0, tiled=True)
    at_small = 2 * QKV
    down_low = jnp.stack([down_weight.astype(bf16), ref_down])

    ids = tokens.transpose(0, 2, 1, 3).reshape(rollouts, length)
    lens = lengths.reshape(rollouts)
    spots = jnp.arange(length, dtype=i32)
    flat_ids = jnp.arange(rollouts * length, dtype=i32).reshape(rollouts, length)
    bits = max(1, (block - 1).bit_length())
    local = (ids >= base) & (ids < base + block) & (spots[None, :] < lens[:, None])
    key = jnp.where(local, (flat_ids << bits) + (ids - base), jnp.int32(2**31 - 1)).reshape(-1)
    key = lax.sort(key)
    n_local = jnp.sum(local.astype(i32))
    live = jnp.arange(rollouts * length, dtype=i32) < n_local
    row_of = jnp.where(live, key & ((1 << bits) - 1), 0)
    flat_of = jnp.where(live, key >> bits, 1 << 22).reshape(-1, TILE)
    pos_of = jnp.where(live, (key >> bits) % length, 0).reshape(-1, TILE).astype(f32)
    tile_lo = flat_of[:, 0] // length
    tile_hi = jnp.max(jnp.where(live, (key >> bits) // length, -1).reshape(-1, TILE), axis=1)
    n_one = n_local.reshape(1)

    picks = scored.transpose(0, 2, 1, 3) + (jnp.arange(n_mp, dtype=i32) * TOK)[None, None, :, None]
    picks = picks.reshape(rollouts, rp)
    valid = (picks + 1 < lens[:, None]).astype(f32)
    count = jnp.sum(valid)
    after = picks[:, :, None] + 1 == spots[None, None, :]
    targets = jnp.sum(jnp.where(after, ids[:, None, :], 0), axis=2).reshape(-1)
    frow = (picks + (jnp.arange(rollouts, dtype=i32) * length)[:, None]).reshape(-1)
    frow_wide = jnp.broadcast_to(frow[:, None], (n_rows, 128))

    low_table, picked, x_tok = lookup(n_one, row_of, embed_weight, ref_embed, flat_of, frow_wide)
    out_both = to_up(jnp.concatenate([out_weight.astype(bf16), ref_out], axis=1))
    picked, out_both = lax.optimization_barrier((picked, out_both))
    late = lax.all_gather(out_both, AXES, axis=0, tiled=True)
    row = (own_rows, MODEL_WIDTH)
    (x0,) = exchange("rows_found", 1, [picked], [], [], keep, [], [((2,) + row, f32)])

    w_kv = jnp.dot(to_order, early[:, 2 * MODEL_WIDTH : at_small], preferred_element_type=f32).astype(bf16)
    small_rows = small_params.shape[0]
    flat_small = jnp.sum(early[:, at_small:].astype(f32).reshape(devices, feats_up, -1), axis=0)
    flat_small = flat_small.reshape(feats_up, 2, tall, 128).transpose(1, 2, 0, 3).reshape(2, tall * feats_up, 128)
    flat_small = flat_small[:, :small_rows].reshape(2, -1)
    gain_attn = flat_small[:, None, :MODEL_WIDTH]
    gain_mlp = flat_small[:, None, MODEL_WIDTH : 2 * MODEL_WIDTH]
    gain_final = flat_small[:, None, 2 * MODEL_WIDTH : 3 * MODEL_WIDTH]
    bias = flat_small[:, None, 3 * MODEL_WIDTH :]

    freq_wide = jnp.tile(frequencies(), 4).reshape(1, 128)
    my_pos = lax.dynamic_slice_in_dim(picks.reshape(-1), com * own_rows, own_rows)
    angle = my_pos.astype(f32)[:, None] * freq_wide
    cosine, sine = jnp.cos(angle), jnp.sin(angle)
    q_all, a1_all = exchange(
        "rows_queries", 2, [], [(early, 0, MODEL_WIDTH), (early, MODEL_WIDTH, MODEL_WIDTH)],
        [to_order, gain_attn, bias[:, :, :MODEL_WIDTH], cosine, sine, x0], queries,
        [(2 * PAIRS, own_rows, 128, bf16), (1,) + row + (bf16,)], [],
    )
    q_all, gu_sent = lax.optimization_barrier((q_all, spread(gu_weight, ref_gu, devices, units, feats_up)))
    gu_cols = lax.all_to_all(gu_sent, AXES, split_axis=0, concat_axis=0, tiled=True)
    w_gu = tuple(gu_cols[:, model].reshape(devices * feats_up, 2 * units) for model in range(2))

    o_part, st_part, kv_tok = attend(
        n_one, tile_lo, tile_hi, q_all, x_tok, w_kv, gain_attn, bias[:, :, MODEL_WIDTH:], freq_wide, frow_wide, flat_of,
        pos_of, length, rp,
    )
    o_part, late = lax.optimization_barrier((o_part, late))
    a2_all, o_all, x1, o_own, lse = exchange(
        "rows_attended", 3, [o_part, st_part], [(late, 0, MODEL_WIDTH), (late, MODEL_WIDTH, MODEL_WIDTH)],
        [to_order, gain_mlp, x0], attended,
        [(2, own_rows, devices * feats_up, bf16), (1,) + row + (bf16,)],
        [((2,) + row, f32), (row, bf16), ((own_rows, 128), f32)], mix_phase,
    )
    gate_up = bmm(a2_all, w_gu)
    gate, up = gate_up[:, :, :units], gate_up[:, :, units:]
    hidden = (jax.nn.silu(gate) * up).astype(bf16)
    af_all, x2 = exchange(
        "rows_finals", 5, [bmm(hidden, down_low).astype(bf16)], [], [gain_final, x1], finals, [(2,) + row + (bf16,)],
        [((2,) + row, f32)],
    )

    aim = (targets - base).reshape(1, -1)
    stats, logits = head(low_table, ref_embed, af_all, aim)
    (stats_all,) = gather([stats[None]], 7)
    stats_all = stats_all.reshape(devices, 8, n_rows)
    lps, lses = [], []
    for i in range(2):
        peaks = stats_all[:, 3 * i]
        peak = jnp.max(peaks, axis=0)
        sums = jnp.sum(stats_all[:, 3 * i + 1] * jnp.exp(peaks - peak[None]), axis=0)
        lses.append(peak + jnp.log(sums))
        lps.append(jnp.sum(stats_all[:, 3 * i + 2], axis=0) - lses[i])
    ratio = (lps[0] - lps[1]).reshape(rollouts, rp)
    factor = BETA * n_rows / count
    reward = factor * jnp.sum(valid * ratio, axis=1)
    d_reward = (jax.nn.sigmoid(reward) - labels.reshape(rollouts).astype(f32)) / rollouts
    d_lp = (valid * (d_reward * factor)[:, None]).reshape(-1)

    d_logits, d_af = head_back(logits, low_table, lses[0].reshape(1, -1), d_lp.reshape(1, -1), aim)
    d_branch, d_out, g_gain_final = exchange(
        "rows_finals_back", 8, [d_af], [], [gain_final, x2], finals_back, [(1,) + row + (bf16,)],
        [(row, f32), ((1, MODEL_WIDTH), f32)],
    )
    d_branch = d_branch[0]
    g_down = lax.dot_general(hidden[0], d_branch, (((0,), (0,)), ((), ())), preferred_element_type=f32)
    d_hidden = lax.dot_general(d_branch, down_low[0], (((1,), (1,)), ((), ())), preferred_element_type=f32)
    sigma = jax.nn.sigmoid(gate[0])
    d_gate = d_hidden * up[0] * sigma * (1.0 + gate[0] * (1.0 - sigma))
    d_up = d_hidden * gate[0] * sigma
    d_gate_up = jnp.concatenate([d_gate, d_up], axis=1).astype(bf16)
    d_a2 = lax.dot_general(d_gate_up, w_gu[0], (((1,), (1,)), ((), ())), preferred_element_type=f32)
    d_attn_all, d_o_all, row_stats_all, d_mid, g_gain_mlp = exchange(
        "rows_attended_back", 10, [d_a2.astype(bf16)[None]], [(late, 0, MODEL_WIDTH)], [from_order, gain_mlp, x1, d_out, o_own, lse],
        attended_back, [(1,) + row + (bf16,), (PAIRS, own_rows, 128, bf16), (1, own_rows, 128, f32)],
        [(row, f32), ((1, MODEL_WIDTH), f32)],
    )
    d_attn_all = d_attn_all[0]

    g_gu = lax.dot_general(a2_all[0], d_gate_up, (((0,), (0,)), ((), ())), preferred_element_type=f32)
    gu_square = jnp.sum(g_gu * g_gu)
    g_gu = g_gu.astype(bf16).reshape(devices, feats_up, 2 * units)
    g_gu, d_o_all = lax.optimization_barrier((g_gu, d_o_all))
    g_gu = lax.all_to_all(g_gu, AXES, split_axis=0, concat_axis=0, tiled=True)
    dq_part, g_kv_part, g_gain_kv, g_bias_kv, dx_tok = attend_back(
        n_one, tile_lo, tile_hi, q_all[:PAIRS], d_o_all, row_stats_all[0], x_tok, kv_tok, w_kv, gain_attn[:1],
        freq_wide, frow_wide, flat_of, pos_of, length, rp,
    )
    dq_part, g_gu = lax.optimization_barrier((dq_part, g_gu))
    g_kv_part = g_kv_part.reshape(2, n_y, 2, n_batch, feats, 256).transpose(2, 0, 1, 3, 4, 5)
    g_kv_part = jnp.pad(g_kv_part.reshape(devices, feats, 256), ((0, 0), (0, feats_up - feats), (0, 0)))
    dq_all, d_row_all, g_kv, g_gain_row, g_bias_q = exchange(
        "rows_queries_back", 12, [dq_part, g_kv_part.reshape(1, devices * feats_up, 256)],
        [(early, 0, MODEL_WIDTH)], [from_order, gain_attn, x0, d_mid, cosine, sine], queries_back,
        [(1,) + row + (bf16,), (1,) + row + (bf16,)],
        [((feats_up, 256), f32), ((1, MODEL_WIDTH), f32), ((1, MODEL_WIDTH), f32)],
    )
    g_kv = g_kv[:feats]
    dq_all = dq_all[0]

    embed_grad, embed_square = table_grad(
        n_one, row_of, d_logits, af_all[0], d_row_all[0], frow.reshape(1, -1).astype(f32), flat_of, dx_tok, block
    )

    def mine(rows, grads):
        cols = lax.dynamic_slice_in_dim(rows, lin * feats, feats, 1)
        return lax.dot_general(cols, grads, (((0,), (0,)), ((), ())), preferred_element_type=f32)

    g_out = mine(o_all[0], d_attn_all)
    g_q = mine(a1_all[0], dq_all)
    g_qkv = jnp.concatenate([g_q, g_kv], axis=1)

    small_part = jnp.concatenate(
        [
            jnp.sum(g_gain_kv, axis=0) + g_gain_row[0],
            g_gain_mlp[0],
            g_gain_final[0],
            g_bias_q[0],
            jnp.sum(g_bias_kv, axis=0),
        ]
    )
    square_part = (
        jnp.sum(g_qkv * g_qkv) + jnp.sum(g_out * g_out) + gu_square + jnp.sum(g_down * g_down) + jnp.sum(embed_square)
    )
    last = jnp.concatenate([small_part, jnp.full((128,), square_part, f32), jnp.zeros((128,), f32)]).reshape(1, -1, 128)
    (last_all,) = gather([last], 14)
    last_all = jnp.sum(last_all.reshape(devices, -1, 128), axis=0)
    g_small = last_all[:small_rows]
    norm = jnp.sqrt(jnp.sum(g_small * g_small) + last_all[small_rows, 0])
    g_small = lax.dynamic_slice_in_dim(g_small, lin * small_params.shape[1], small_params.shape[1], 1)

    g_gu = join(g_gu, feats, units)
    owned_grads = (g_qkv, g_out, g_gu, g_down, embed_grad, g_small)
    clip = jnp.minimum(1.0, CLIP / (norm + 1e-06))
    new_weights, new_firsts, new_seconds, new_lows, clipped_list = ([], [], [], [], [])
    for w, g, m, v in zip(masters, owned_grads, firsts, seconds):
        g = g.astype(f32) * clip
        m_new = MOM1 * m + (1.0 - MOM1) * g
        v_new = MOM2 * v + (1.0 - MOM2) * g * g
        update = m_new / (1.0 - MOM1**STEP) / (jnp.sqrt(v_new / (1.0 - MOM2**STEP)) + EPS_ADAM)
        w_new = w - RATE * (update + DECAY * w)
        new_weights.append(w_new)
        new_firsts.append(m_new)
        new_seconds.append(v_new)
        clipped_list.append(g)
        new_lows.append(w_new.astype(bf16))
    return (
        *new_weights[:5], clipped_list[5], *new_firsts, *new_seconds, *new_lows[:5], norm,
    )


def solution(mesh):
    rows, cols = P(AXES, None), P(None, AXES)
    six = (rows, rows, rows, rows, rows, cols)
    in_specs = (P(), P(), P(), P()) + six * 4
    out_specs = six * 3 + (rows,) * 5 + (P(),)
    return jax.shard_map(body, mesh=mesh, in_specs=in_specs, out_specs=out_specs, check_vma=False)
```

```python
import functools

import jax
import jax.numpy as jnp
from jax import lax
from jax.experimental import pallas as pl
from jax.experimental.pallas import tpu as pltpu
from jax.sharding import PartitionSpec as P

MODEL_WIDTH = 896
QUERY_HEADS = 14
KEY_VALUE_HEADS = 2
HEAD_SIZE = 64
FF = 4864
QKV = 1152
TOK = 256
P_SIZE = 16
MICRO = 2
STEP = 5

EPS_NORM = 1e-06
THETA = 1000000.0
BETA = 0.05
CLIP = 0.1
RATE = 0.03
DECAY = 0.01
MOM1 = 0.5
MOM2 = 0.5
EPS_ADAM = 1e-08

MESH = pl.DeviceIdType.MESH

def places():
    n_mp, n_batch = lax.axis_size("mp"), lax.axis_size("batch")
    return 2, n_mp // 2, n_batch


def coords():
    mp = lax.axis_index("mp")
    return lax.axis_index("half"), mp // 2, lax.rem(mp, 2), lax.axis_index("batch")


def comm_index():
    _, n_y, n_batch = places()
    half, y, core, batch = coords()
    return ((core * 2 + half) * n_y + y) * n_batch + batch


def peers():
    _, n_y, n_batch = places()
    half, y, core, batch = coords()
    line = []
    for k in range(1, n_batch):
        to, frm = lax.rem(batch + k, n_batch), lax.rem(batch + n_batch - k, n_batch)
        line.append(({"half": half, "mp": y * 2 + core, "batch": to}, to, frm))
    plane = []
    n_plane = 2 * n_y
    spot = half * n_y + y
    for k in range(1, n_plane):
        to, frm = lax.rem(spot + k, n_plane), lax.rem(spot + n_plane - k, n_plane)
        plane.append(
            ({"half": to // n_y, "mp": lax.rem(to, n_y) * 2 + core, "batch": batch}, to, frm)
        )
    other = ({"half": half, "mp": y * 2 + (1 - core), "batch": batch}, 1 - core, 1 - core)
    return line, plane, other


def greet(line, plane, other):
    barrier = pltpu.get_barrier_semaphore()
    everyone = line + plane + [other]
    for who, _, _ in everyone:
        pl.semaphore_signal(barrier, inc=1, device_id=who, device_id_type=MESH)
    pl.semaphore_wait(barrier, len(everyone))


def push(src, dst, send_sem, recv_sem, who):
    copy = pltpu.make_async_remote_copy(
        src_ref=src,
        dst_ref=dst,
        send_sem=send_sem,
        recv_sem=recv_sem,
        device_id=who,
        device_id_type=MESH,
    )
    copy.start()
    return copy


def gather_phase(ins, outs, send_sems, recv_sems, own_sem, line, plane, other):
    n_arr = len(ins)
    _, n_y, n_batch = places()
    half, y, core, batch = coords()
    n_plane = 2 * n_y
    spot = half * n_y + y
    slots = iter(range(n_arr * (n_batch - 1 + n_plane * n_batch + (n_plane - 1) * n_batch)))

    def rows(i, where, j):
        size = ins[i].shape[1]
        at = (core * n_plane + where) * n_batch + lax.rem(batch + n_batch - j, n_batch)
        return outs[i].at[:, pl.ds(pl.multiple_of(at * size, size), size), :]

    def send(src, dst, who):
        slot = next(slots)
        return push(src, dst, send_sems.at[slot], recv_sems.at[slot], who)

    local, by_line, by_plane, by_core = [], [], [], []
    for i in range(n_arr):
        by_line.append([send(ins[i], rows(i, spot, 0), who) for who, _, _ in line])
    for i in range(n_arr):
        by_plane.append([[send(ins[i], rows(i, spot, 0), who) for who, _, _ in plane]])
        by_core.append(send(ins[i], rows(i, spot, 0), other[0]))
        copy = pltpu.make_async_copy(ins[i], rows(i, spot, 0), own_sem.at[i])
        copy.start()
        local.append(copy)
    for j in range(1, n_batch):
        for i in range(n_arr):
            by_line[i][j - 1].wait_recv()
            by_plane[i].append([send(rows(i, spot, j), rows(i, spot, j), who) for who, _, _ in plane])
            by_core.append(send(rows(i, spot, j), rows(i, spot, j), other[0]))
    for j in range(n_batch):
        for i in range(n_arr):
            for k, (_, _, frm) in enumerate(plane):
                by_plane[i][j][k].wait_recv()
                by_core.append(send(rows(i, frm, j), rows(i, frm, j), other[0]))
    for copy in local:
        copy.wait()
    for copy in by_core:
        copy.wait_recv()
    for i in range(n_arr):
        for copy in by_line[i] + sum(by_plane[i], []):
            copy.wait_send()
    for copy in by_core:
        copy.wait_send()


def gather_kernel(n_arr, *refs):
    ins, outs = refs[:n_arr], refs[n_arr : 2 * n_arr]
    line, plane, other = peers()
    greet(line, plane, other)
    gather_phase(ins, outs, *refs[2 * n_arr :], line, plane, other)


def gather(arrays, cid, vmem=48):
    _, n_y, n_batch = places()
    n_plane = 2 * n_y
    total = 2 * n_plane * n_batch
    n = len(arrays)
    copies = n * ((n_batch - 1) + (n_plane - 1) * n_batch + n_plane * n_batch)
    return pl.pallas_call(
        functools.partial(gather_kernel, n),
        out_shape=[jax.ShapeDtypeStruct((a.shape[0], a.shape[1] * total, a.shape[2]), a.dtype) for a in arrays],
        in_specs=[pl.BlockSpec(memory_space=pltpu.VMEM)] * n,
        out_specs=[pl.BlockSpec(memory_space=pltpu.VMEM)] * n,
        scratch_shapes=[
            pltpu.SemaphoreType.DMA((copies,)),
            pltpu.SemaphoreType.DMA((copies,)),
            pltpu.SemaphoreType.DMA((n,)),
        ],
        compiler_params=pltpu.CompilerParams(
            collective_id=cid, has_side_effects=True, vmem_limit_bytes=vmem * 2**20
        ),
        name=f"gather_{cid}",
    )(*arrays)


def reduce_phase(ins, outs, scr, send_sems, recv_sems, line, plane, other):
    n_arr = len(ins)
    _, n_y, n_batch = places()
    half, y, core, batch = coords()
    n_plane = 2 * n_y
    spot = half * n_y + y
    f32 = jnp.float32
    slots = iter(range(n_arr * (n_plane * n_batch + (n_plane - 1) * n_batch + n_batch - 1)))
    order = list(range(1, n_batch)) + [0]
    spots = [to for _, to, _ in plane] + [spot]

    def send(src, dst, who):
        slot = next(slots)
        return push(src, dst, send_sems.at[slot], recv_sems.at[slot], who)

    def rows(i, side, where, j):
        size = outs[i].shape[1]
        at = (side * n_plane + where) * n_batch + lax.rem(batch + j, n_batch)
        return pl.ds(pl.multiple_of(at * size, size), size)

    by_core, by_plane, by_line = {}, {}, {}
    for j in order:
        for p in range(n_plane):
            for i in range(n_arr):
                src = ins[i].at[:, rows(i, 1 - core, spots[p], j), :]
                by_core[i, p, j] = send(src, scr[5 * i].at[p, j], other[0])

    def mine(i, p, j):
        by_core[i, p, j].wait_recv()
        return ins[i][:, rows(i, core, spots[p], j), :].astype(f32) + scr[5 * i][p, j].astype(f32)

    for j in order:
        for p in range(n_plane - 1):
            for i in range(n_arr):
                out = scr[5 * i + 1]
                out[p, j] = mine(i, p, j).astype(out.dtype)
                by_plane[i, p, j] = send(out.at[p, j], scr[5 * i + 2].at[p, j], plane[p][0])
    totals = {}
    for j in order:
        for i in range(n_arr):
            total = mine(i, n_plane - 1, j)
            for p in range(n_plane - 1):
                by_plane[i, p, j].wait_recv()
                total = total + scr[5 * i + 2][p, j].astype(f32)
            if j:
                out = scr[5 * i + 3]
                out[j - 1] = total.astype(out.dtype)
                by_line[i, j] = send(out.at[j - 1], scr[5 * i + 4].at[j - 1], line[j - 1][0])
            else:
                outs[i][...] = total
    for i in range(n_arr):
        for j in range(1, n_batch):
            by_line[i, j].wait_recv()
            outs[i][...] += scr[5 * i + 4][j - 1].astype(f32)
    for group in (by_core, by_plane, by_line):
        for copy in group.values():
            copy.wait_send()


def reduce_scratch(arrays):
    _, n_y, n_batch = places()
    n_plane = 2 * n_y
    scratch = []
    for a in arrays:
        m, rows, w = a.shape
        size = rows // (2 * n_plane * n_batch)
        for lead in ((n_plane, n_batch), (n_plane - 1, n_batch), (n_plane - 1, n_batch), (n_batch - 1,), (n_batch - 1,)):
            scratch.append(pltpu.VMEM(lead + (m, size, w), a.dtype))
    return scratch


def exchange_kernel(n_in, columns, n_const, n_out, n_extra, reducer, compute, *refs):
    refs = list(refs)

    def take(n):
        part = refs[:n]
        del refs[:n]
        return part

    n_fetch = len(columns)
    ins, sources, consts, outs, extras = take(n_in), take(n_fetch), take(n_const), take(n_out), take(n_extra)
    totals, staged, fetched = take(n_in), take(n_out), take(n_fetch)
    send_one, recv_one, send_two, recv_two, own_sem, fetch_sem = refs[-6:]
    line, plane, other = peers()
    copies = []
    for k, (first, width) in enumerate(columns):
        copy = pltpu.make_async_copy(sources[k].at[:, pl.ds(first, width)], fetched[k], fetch_sem.at[k])
        copy.start()
        copies.append(copy)
    greet(line, plane, other)
    if ins:
        reducer(ins, totals, refs[:-6], send_one, recv_one, line, plane, other)
    for copy in copies:
        copy.wait()
    compute(totals, fetched + consts, staged, extras)
    if outs:
        gather_phase(staged, outs, send_two, recv_two, own_sem, line, plane, other)


def exchange(name, cid, arrays, fetches, consts, compute, gathered, extras, reducer=reduce_phase):
    _, n_y, n_batch = places()
    n_plane = 2 * n_y
    total = 2 * n_plane * n_batch
    f32 = jnp.float32
    n_in, n_out = len(arrays), len(gathered)
    one = max(1, n_in) * (n_plane * n_batch + (n_plane - 1) * n_batch + n_batch - 1)
    two = max(1, n_out) * (n_batch - 1 + (n_plane - 1) * n_batch + n_plane * n_batch)
    vm = pl.BlockSpec(memory_space=pltpu.VMEM)
    dma = pltpu.SemaphoreType.DMA
    columns = tuple((first, width) for _, first, width in fetches)
    return pl.pallas_call(
        functools.partial(
            exchange_kernel, n_in, columns, len(consts), n_out, len(extras), reducer, compute
        ),
        out_shape=[jax.ShapeDtypeStruct((m, rows * total, w), t) for m, rows, w, t in gathered]
        + [jax.ShapeDtypeStruct(shape, t) for shape, t in extras],
        in_specs=[vm] * n_in + [pl.BlockSpec(memory_space=pl.ANY)] * len(fetches) + [vm] * len(consts),
        out_specs=[vm] * (n_out + len(extras)),
        scratch_shapes=[pltpu.VMEM((a.shape[0], a.shape[1] // total, a.shape[2]), f32) for a in arrays]
        + [pltpu.VMEM((m, rows, w), t) for m, rows, w, t in gathered]
        + [pltpu.VMEM((a.shape[0], width), a.dtype) for a, _, width in fetches]
        + reduce_scratch(arrays)
        + [dma((one,)), dma((one,)), dma((two,)), dma((two,)), dma((max(1, n_out),)), dma((max(1, len(fetches)),))],
        compiler_params=pltpu.CompilerParams(collective_id=cid, has_side_effects=True, vmem_limit_bytes=60 * 2**20),
        name=name,
    )(*arrays, *[a for a, _, _ in fetches], *consts)


def norm_forward(x, gain):
    scale = lax.rsqrt(jnp.mean(x * x, axis=-1, keepdims=True) + EPS_NORM)
    return (x * scale * gain, scale)


def norm_backward(d_out, x, scale, gain):
    d_gain = d_out * x * scale
    d_hat = d_out * gain
    d_x = scale * (d_hat - x * scale * scale * jnp.mean(d_hat * x, axis=-1, keepdims=True))
    return (d_x, d_gain)


HEAD_SLOTS = (0, 2, 4, 6, 1, 3, 5, 8, 10, 12, 7, 9, 11, 13)
COMBOS = ((0, 4, 0), (0, 3, 4), (4, 7, 7), (3, 7, 10))
PAIRS = QUERY_HEADS // 2
TILE = 128


def column(vector):
    return jnp.transpose(jnp.broadcast_to(vector.astype(jnp.float32), (128, 128)))


def last_last(a, b):
    return lax.dot_general(a, b, (((1,), (1,)), ((), ())), preferred_element_type=jnp.float32)


def first_first(a, b):
    return lax.dot_general(a, b, (((0,), (0,)), ((), ())), preferred_element_type=jnp.float32)


def straight(a, b):
    return jnp.dot(a, b, preferred_element_type=jnp.float32)


def lookup_kernel(
    block, span, n_ref, rows_ref, table_ref, frozen_ref, flat_ref, frow_ref,
    low_ref, picked_ref, x_ref, held, rough, staged, sem,
):
    step = pl.program_id(0)
    f32, bf16 = jnp.float32, jnp.bfloat16
    inside = step * span + lax.broadcasted_iota(jnp.int32, (span, 1), 0) < block
    low = jnp.where(inside, table_ref[...], 0.0).astype(bf16)
    low_ref[...] = low
    at = pl.multiple_of(step * span, span)
    held[0, pl.ds(at, span), :] = table_ref[...]
    held[1, pl.ds(at, span), :] = frozen_ref[...].astype(f32)

    @pl.when(step == pl.num_programs(0) - 1)
    def _():
        picked_ref[...] = jnp.zeros_like(picked_ref)
        n_rows = frow_ref.shape[0]

        def tile(i, _):
            def eight(k, _):
                for j in range(8):
                    place = k * 8 + j
                    row = rows_ref[i * TILE + place]
                    for model in range(2):
                        rough[model, pl.ds(place, 1), :] = held[model, pl.ds(row, 1), :]
                return 0

            lax.fori_loop(0, TILE // 8, eight, 0)
            slot = lax.rem(i, 2)
            where = pl.ds(pl.multiple_of(i * TILE, TILE), TILE)
            copy = pltpu.make_async_copy(staged.at[slot], x_ref.at[:, where, :], sem.at[slot])

            @pl.when(i >= 2)
            def _():
                copy.wait()

            staged[slot] = rough[...].astype(bf16)
            copy.start()
            match = frow_ref[...] == jnp.broadcast_to(flat_ref[pl.ds(i, 1), :], (n_rows, TILE))
            match = jnp.where(match, 1.0, 0.0).astype(bf16)
            for model in range(2):
                picked_ref[model] = picked_ref[model] + straight(match, staged[slot, model]).astype(bf16)
            return 0

        tiles = (n_ref[0] + TILE - 1) // TILE
        lax.fori_loop(0, tiles, tile, 0)
        for k in range(2):

            @pl.when(tiles > k)
            def _():
                where = pl.ds(0, TILE)
                pltpu.make_async_copy(staged.at[k], x_ref.at[:, where, :], sem.at[k]).wait()


def lookup(n_local, rows, table, frozen, flat, frow):
    block, width = table.shape
    span = 512
    steps = pl.cdiv(block, span)
    cap = flat.shape[0] * TILE
    n_rows = frow.shape[0]
    bf16 = jnp.bfloat16
    whole = lambda shape: pl.BlockSpec(shape, lambda i: (0,) * len(shape))
    smem = pl.BlockSpec(memory_space=pltpu.SMEM)
    return pl.pallas_call(
        functools.partial(lookup_kernel, block, span),
        grid=(steps,),
        out_shape=[
            jax.ShapeDtypeStruct((steps * span, width), bf16),
            jax.ShapeDtypeStruct((2, n_rows, width), bf16),
            jax.ShapeDtypeStruct((2, cap, width), bf16),
        ],
        in_specs=[
            smem,
            smem,
            pl.BlockSpec((span, width), lambda i: (i, 0)),
            pl.BlockSpec((span, width), lambda i: (i, 0)),
            whole(flat.shape),
            whole(frow.shape),
        ],
        out_specs=[
            pl.BlockSpec((span, width), lambda i: (i, 0)),
            whole((2, n_rows, width)),
            pl.BlockSpec(memory_space=pl.ANY),
        ],
        scratch_shapes=[
            pltpu.VMEM((2, steps * span, width), jnp.float32),
            pltpu.VMEM((2, TILE, width), jnp.float32),
            pltpu.VMEM((2, 2, TILE, width), bf16),
            pltpu.SemaphoreType.DMA((2,)),
        ],
        compiler_params=pltpu.CompilerParams(vmem_limit_bytes=60 * 2**20),
        name="lookup",
    )(n_local, rows, table, frozen, flat, frow)


def head_pieces(both, lane):
    turned = pltpu.roll(both, 64, 1)
    low, high = lane < 64, lane >= 64
    bf16 = jnp.bfloat16
    zero = jnp.zeros_like(both)
    return (
        jnp.where(low, both, zero).astype(bf16),
        jnp.where(high, turned, zero).astype(bf16),
        jnp.where(low, turned, zero).astype(bf16),
        jnp.where(high, both, zero).astype(bf16),
    )


def turn(values, positions, freq, lane, sign):
    angle = positions * freq
    cosine, sine = jnp.cos(angle), jnp.sin(angle)
    first = lax.rem(lane, 64) < 32
    mixed = jnp.where(first, -sign * pltpu.roll(values, 96, 1), sign * pltpu.roll(values, 32, 1))
    return values * cosine + mixed * sine


def allowed_of(frow, flat, r, length):
    flat = jnp.broadcast_to(flat, frow.shape)
    return jnp.where((flat <= frow) & (flat >= r * length), 1.0, 0.0)


def attend_kernel(
    length, rp, n_ref, lo_ref, hi_ref, q_ref, x_ref, w_ref, gain_ref, bias_ref, freq_ref, frow_ref, flat_ref, pos_ref,
    o_ref, st_ref, kv_ref, xbuf, kvbuf, m_scr, l_scr, o_scr, sem,
):
    model = pl.program_id(0)
    f32, bf16 = jnp.float32, jnp.bfloat16
    lane = lax.broadcasted_iota(jnp.int32, (TILE, 128), 1)
    lane_r = lax.broadcasted_iota(jnp.int32, (rp, 128), 1)
    m_scr[...] = jnp.full(m_scr.shape, -1e30, f32)
    l_scr[...] = jnp.zeros_like(l_scr)
    o_scr[...] = jnp.zeros_like(o_scr)

    tiles = (n_ref[0] + TILE - 1) // TILE

    def fetch(i):
        slot = lax.rem(i, 2)
        at = pl.ds(pl.multiple_of(i * TILE, TILE), TILE)
        return pltpu.make_async_copy(x_ref.at[model, at, :], xbuf.at[slot], sem.at[slot])

    @pl.when(tiles > 0)
    def _():
        fetch(0).start()

    def tile(i, _):
        at = pl.ds(pl.multiple_of(i * TILE, TILE), TILE)

        @pl.when(i + 1 < tiles)
        def _():
            fetch(i + 1).start()

        fetch(i).wait()
        x = xbuf[lax.rem(i, 2)].astype(f32)
        scale = lax.rsqrt(jnp.mean(x * x, axis=-1, keepdims=True) + EPS_NORM)
        normed = (x * scale * gain_ref[0]).astype(bf16)
        mixed = straight(normed, w_ref[...]) + bias_ref[0]
        key = turn(mixed[:, :128], column(pos_ref[pl.ds(i, 1), :]), freq_ref[...], lane, 1.0)
        key = key.astype(bf16)
        value = mixed[:, 128:].astype(bf16)
        kvbuf[...] = jnp.concatenate([key, value], axis=1)
        out = pltpu.make_async_copy(kvbuf, kv_ref.at[model, at, :], sem.at[2])
        out.start()
        keys = head_pieces(key.astype(f32), lane)
        values = head_pieces(value.astype(f32), lane)
        one = jnp.ones((TILE, 128), bf16)
        values = tuple(jnp.where((lane < 64) == (c % 2 == 0), v, one) for c, v in enumerate(values))
        flat = flat_ref[pl.ds(i, 1), :]

        def rollout(r, _):
            rows = pl.ds(pl.multiple_of(r * rp, rp), rp)
            ok = allowed_of(frow_ref[rows, :], flat, r, length)[None]
            shift = (ok - 1.0) * 1e30
            falls, adds = {}, {}
            for c, (p0, p1, s0) in enumerate(COMBOS):
                n = p1 - p0
                query = q_ref[p0:p1, rows, :].reshape(n * rp, 128)
                score = last_last(query, keys[c]).reshape(n, rp, TILE) * HEAD_SIZE ** (-0.5)
                score = score * ok + shift
                old = m_scr[s0 : s0 + n, rows, :]
                new = jnp.maximum(old, jnp.max(score, axis=-1, keepdims=True))
                m_scr[s0 : s0 + n, rows, :] = new
                fall = old - new
                prob = jnp.exp(score - new) * ok
                add = straight(prob.astype(bf16).reshape(n * rp, TILE), values[c]).reshape(n, rp, 128)
                for k in range(n):
                    falls[p0 + k, c % 2] = fall[k]
                    adds[p0 + k, c % 2] = add[k]
            for p in range(PAIRS):
                alpha = jnp.exp(jnp.where(lane_r < 64, falls[p, 0], falls[p, 1]))
                turned = pltpu.roll(alpha, 64, 1)
                o_scr[p, rows, :] = o_scr[p, rows, :] * alpha + jnp.where(lane_r < 64, adds[p, 0], adds[p, 1])
                l_scr[p, rows, :] = l_scr[p, rows, :] * turned + jnp.where(lane_r < 64, adds[p, 1], adds[p, 0])
            return 0

        lax.fori_loop(lo_ref[i], hi_ref[i] + 1, rollout, 0)
        out.wait()
        return 0

    lax.fori_loop(0, tiles, tile, 0)

    def leave(r, _):
        rows = pl.ds(pl.multiple_of(r * rp, rp), rp)
        o_ref[:, rows, :] = o_scr[:, rows, :].astype(bf16)
        packed = jnp.where(model == 0, jnp.zeros((rp, 128), f32), st_ref[0, rows, :])
        for slot, head in enumerate(HEAD_SLOTS):
            held = l_scr[head // 2, rows, :]
            held = held[:, 64:65] if head % 2 == 0 else held[:, 0:1]
            packed = jnp.where(lane_r == head + 32 * model, m_scr[slot, rows, :], packed)
            packed = jnp.where(lane_r == 16 + head + 32 * model, held, packed)
        st_ref[0, rows, :] = packed
        return 0

    lax.fori_loop(0, m_scr.shape[1] // rp, leave, 0)


def attend(n_local, lo, hi, q, x, w, gain, bias, freq, frow, flat, pos, length, rp):
    n_rows = q.shape[1]
    width = x.shape[2]
    cap = x.shape[1]
    bf16 = jnp.bfloat16
    whole = lambda shape: pl.BlockSpec(shape, lambda i: (0,) * len(shape))
    smem = pl.BlockSpec(memory_space=pltpu.SMEM)
    anyw = pl.BlockSpec(memory_space=pl.ANY)
    model = lambda shape: pl.BlockSpec(shape, lambda i: (i, 0, 0))
    return pl.pallas_call(
        functools.partial(attend_kernel, length, rp),
        grid=(2,),
        out_shape=[
            jax.ShapeDtypeStruct((2 * PAIRS, n_rows, 128), bf16),
            jax.ShapeDtypeStruct((1, n_rows, 128), jnp.float32),
            jax.ShapeDtypeStruct((2, cap, 256), bf16),
        ],
        in_specs=[
            smem, smem, smem, model((PAIRS, n_rows, 128)), anyw, pl.BlockSpec((width, 256), lambda i: (0, i)), model((1, 1, width)),
            model((1, 1, 256)), whole((1, 128)), whole(frow.shape), whole(flat.shape), whole(pos.shape),
        ],
        out_specs=[model((PAIRS, n_rows, 128)), whole((1, n_rows, 128)), anyw],
        scratch_shapes=[
            pltpu.VMEM((2, TILE, width), bf16),
            pltpu.VMEM((TILE, 256), bf16),
            pltpu.VMEM((QUERY_HEADS, n_rows, 128), jnp.float32),
            pltpu.VMEM((PAIRS, n_rows, 128), jnp.float32),
            pltpu.VMEM((PAIRS, n_rows, 128), jnp.float32),
            pltpu.SemaphoreType.DMA((3,)),
        ],
        compiler_params=pltpu.CompilerParams(vmem_limit_bytes=62 * 2**20),
        name="attend",
    )(n_local, lo, hi, q, x, w, gain, bias, freq, frow, flat, pos)


def attend_back_kernel(
    length, rp, n_ref, lo_ref, hi_ref, q_ref, do_ref, st_ref, x_ref, kv_ref, w_ref, gain_ref, freq_ref, frow_ref, flat_ref,
    pos_ref, dq_ref, gkv_ref, gs_ref, gb_ref, dx_ref, xbuf, kvbuf, dxbuf, dq_scr, dk_scr, dv_scr, sem,
):
    f32, bf16 = jnp.float32, jnp.bfloat16
    lane = lax.broadcasted_iota(jnp.int32, (TILE, 128), 1)
    dq_scr[...] = jnp.zeros_like(dq_scr)
    gkv_ref[...] = jnp.zeros_like(gkv_ref)
    gs_ref[...] = jnp.zeros_like(gs_ref)
    gb_ref[...] = jnp.zeros_like(gb_ref)

    tiles = (n_ref[0] + TILE - 1) // TILE

    def fetch(i):
        slot = lax.rem(i, 2)
        at = pl.ds(pl.multiple_of(i * TILE, TILE), TILE)
        return (
            pltpu.make_async_copy(x_ref.at[0, at, :], xbuf.at[slot], sem.at[slot]),
            pltpu.make_async_copy(kv_ref.at[0, at, :], kvbuf.at[slot], sem.at[2 + slot]),
        )

    def leave(i):
        slot = lax.rem(i, 2)
        at = pl.ds(pl.multiple_of(i * TILE, TILE), TILE)
        return pltpu.make_async_copy(dxbuf.at[slot], dx_ref.at[at, :], sem.at[4 + slot])

    @pl.when(tiles > 0)
    def _():
        for copy in fetch(0):
            copy.start()

    def tile(i, _):
        slot = lax.rem(i, 2)

        @pl.when(i + 1 < tiles)
        def _():
            for copy in fetch(i + 1):
                copy.start()

        for copy in fetch(i):
            copy.wait()
        keys = head_pieces(kvbuf[slot, :, :128].astype(f32), lane)
        values = head_pieces(kvbuf[slot, :, 128:].astype(f32), lane)
        flat = flat_ref[pl.ds(i, 1), :]
        dk_scr[...] = jnp.zeros_like(dk_scr)
        dv_scr[...] = jnp.zeros_like(dv_scr)

        def rollout(r, _):
            rows = pl.ds(pl.multiple_of(r * rp, rp), rp)
            ok = allowed_of(frow_ref[rows, :], flat, r, length)[None]
            shift = (ok - 1.0) * 1e30
            stats = st_ref[rows, :]
            adds = {}
            for c, (p0, p1, s0) in enumerate(COMBOS):
                n = p1 - p0
                heads = HEAD_SLOTS[s0 : s0 + n]
                query = q_ref[p0:p1, rows, :].reshape(n * rp, 128)
                back = do_ref[p0:p1, rows, :].reshape(n * rp, 128)
                lse = jnp.stack([stats[:, h : h + 1] for h in heads])
                delta = jnp.stack([stats[:, 16 + h : 17 + h] for h in heads])
                score = last_last(query, keys[c]).reshape(n, rp, TILE) * HEAD_SIZE ** (-0.5)
                prob = jnp.exp(score * ok + shift - lse)
                d_prob = last_last(back, values[c]).reshape(n, rp, TILE)
                d_score = (prob * (d_prob - delta)).astype(bf16).reshape(n * rp, TILE)
                add = straight(d_score, keys[c]).reshape(n, rp, 128)
                dk_scr[c] += first_first(d_score, query)
                dv_scr[c] += first_first(prob.astype(bf16).reshape(n * rp, TILE), back)
                for k in range(n):
                    adds[p0 + k, c % 2] = add[k]
            for p in range(PAIRS):
                dq_scr[p, rows, :] = dq_scr[p, rows, :] + adds[p, 0] + adds[p, 1]
            return 0

        lax.fori_loop(lo_ref[i], hi_ref[i] + 1, rollout, 0)

        def joined(scr):
            return jnp.where(lane < 64, scr[0] + pltpu.roll(scr[1], 64, 1), scr[3] + pltpu.roll(scr[2], 64, 1))

        d_key = turn(joined(dk_scr) * HEAD_SIZE ** (-0.5), column(pos_ref[pl.ds(i, 1), :]), freq_ref[...], lane, -1.0)
        d_mixed = jnp.concatenate([d_key, joined(dv_scr)], axis=1).astype(bf16)
        x = xbuf[slot].astype(f32)
        scale = lax.rsqrt(jnp.mean(x * x, axis=-1, keepdims=True) + EPS_NORM)
        gain = gain_ref[0]
        normed = (x * scale * gain).astype(bf16)
        gkv_ref[...] += first_first(normed, d_mixed)
        gb_ref[...] += jnp.sum(d_mixed.astype(f32).reshape(TILE // 8, 8, 256), axis=0)
        d_normed = last_last(d_mixed, w_ref[...])
        gs_ref[...] += jnp.sum((d_normed * x * scale).reshape(TILE // 8, 8, x.shape[1]), axis=0)
        d_hat = d_normed * gain
        d_x = scale * (d_hat - x * scale * scale * jnp.mean(d_hat * x, axis=-1, keepdims=True))

        @pl.when(i >= 2)
        def _():
            leave(i - 2).wait()

        dxbuf[slot] = d_x.astype(bf16)
        leave(i).start()
        return 0

    lax.fori_loop(0, tiles, tile, 0)
    for k in range(2):

        @pl.when(tiles > k)
        def _():
            leave(tiles - 1 - k).wait()

    dq_ref[...] = (dq_scr[...] * HEAD_SIZE ** (-0.5)).astype(bf16)


def attend_back(n_local, lo, hi, q, do, stats, x, kv, w, gain, freq, frow, flat, pos, length, rp):
    n_rows = do.shape[1]
    width = x.shape[2]
    cap = x.shape[1]
    bf16, f32 = jnp.bfloat16, jnp.float32
    whole = lambda shape: pl.BlockSpec(shape, lambda i: (0,) * len(shape))
    smem = pl.BlockSpec(memory_space=pltpu.SMEM)
    anyw = pl.BlockSpec(memory_space=pl.ANY)
    return pl.pallas_call(
        functools.partial(attend_back_kernel, length, rp),
        grid=(1,),
        out_shape=[
            jax.ShapeDtypeStruct((PAIRS, n_rows, 128), bf16),
            jax.ShapeDtypeStruct((width, 256), f32),
            jax.ShapeDtypeStruct((8, width), f32),
            jax.ShapeDtypeStruct((8, 256), f32),
            jax.ShapeDtypeStruct((cap, width), bf16),
        ],
        in_specs=[
            smem, smem, smem, whole((PAIRS, n_rows, 128)), whole((PAIRS, n_rows, 128)), whole((n_rows, 128)), anyw, anyw,
            whole((width, 256)), whole((1, 1, width)), whole((1, 128)), whole(frow.shape), whole(flat.shape),
            whole(pos.shape),
        ],
        out_specs=[
            whole((PAIRS, n_rows, 128)), whole((width, 256)), whole((8, width)), whole((8, 256)), anyw,
        ],
        scratch_shapes=[
            pltpu.VMEM((2, TILE, width), bf16),
            pltpu.VMEM((2, TILE, 256), bf16),
            pltpu.VMEM((2, TILE, width), bf16),
            pltpu.VMEM((PAIRS, n_rows, 128), f32),
            pltpu.VMEM((4, TILE, 128), f32),
            pltpu.VMEM((4, TILE, 128), f32),
            pltpu.SemaphoreType.DMA((6,)),
        ],
        compiler_params=pltpu.CompilerParams(vmem_limit_bytes=60 * 2**20),
        name="attend_back",
    )(n_local, lo, hi, q, do, stats, x, kv, w, gain, freq, frow, flat, pos)


def table_grad_kernel(
    span, n_ref, rows_ref, dl_ref, af_ref, drow_ref, frow_ref, flat_ref, dx_ref,
    g_ref, sq_ref, added, moved, rough, sem,
):
    step = pl.program_id(0)
    f32, bf16 = jnp.float32, jnp.bfloat16

    @pl.when(step == 0)
    def _():
        sq_ref[...] = jnp.zeros_like(sq_ref)
        added[...] = jnp.zeros_like(added)
        n_rows = drow_ref.shape[0]

        tiles = (n_ref[0] + TILE - 1) // TILE

        def fetch(i):
            slot = lax.rem(i, 2)
            at = pl.ds(pl.multiple_of(i * TILE, TILE), TILE)
            return pltpu.make_async_copy(dx_ref.at[at, :], moved.at[slot], sem.at[slot])

        @pl.when(tiles > 0)
        def _():
            fetch(0).start()

        def tile(i, _):
            @pl.when(i + 1 < tiles)
            def _():
                fetch(i + 1).start()

            token = column(flat_ref[pl.ds(i, 1), :])
            token = jnp.concatenate([token] * (n_rows // 128), axis=1)
            match = jnp.where(token == jnp.broadcast_to(frow_ref[...], (TILE, n_rows)), 1.0, 0.0).astype(bf16)
            own = straight(match, drow_ref[...])
            fetch(i).wait()
            rough[...] = own + moved[lax.rem(i, 2)].astype(f32)

            def eight(k, _):
                for j in range(8):
                    place = k * 8 + j
                    row = pl.ds(rows_ref[i * TILE + place], 1)
                    added[row, :] = added[row, :] + rough[pl.ds(place, 1), :]
                return 0

            lax.fori_loop(0, TILE // 8, eight, 0)
            return 0

        lax.fori_loop(0, tiles, tile, 0)

    total = straight(dl_ref[...], af_ref[0]) + added[pl.ds(pl.multiple_of(step * span, span), span), :]
    g_ref[...] = total.astype(bf16)
    square = total * total
    sq_ref[...] += jnp.sum(square.reshape(span // 8, 8, square.shape[1]), axis=0)


def table_grad(n_local, rows, dl, af, drow, frow, flat, dx, block):
    _, n_rows, width = af.shape
    span = wide(dl.shape[0])
    steps = dl.shape[0] // span
    whole = lambda shape: pl.BlockSpec(shape, lambda i: (0,) * len(shape))
    smem = pl.BlockSpec(memory_space=pltpu.SMEM)
    return pl.pallas_call(
        functools.partial(table_grad_kernel, span),
        grid=(steps,),
        out_shape=[
            jax.ShapeDtypeStruct((block, width), jnp.bfloat16),
            jax.ShapeDtypeStruct((8, width), jnp.float32),
        ],
        in_specs=[
            smem, smem,
            pl.BlockSpec((span, n_rows), lambda i: (i, 0)),
            whole((1, n_rows, width)), whole(drow.shape), whole(frow.shape), whole(flat.shape),
            pl.BlockSpec(memory_space=pl.ANY),
        ],
        out_specs=[pl.BlockSpec((span, width), lambda i: (i, 0)), whole((8, width))],
        scratch_shapes=[
            pltpu.VMEM((steps * span, width), jnp.float32),
            pltpu.VMEM((2, TILE, width), jnp.bfloat16),
            pltpu.VMEM((TILE, width), jnp.float32),
            pltpu.SemaphoreType.DMA((2,)),
        ],
        compiler_params=pltpu.CompilerParams(vmem_limit_bytes=56 * 2**20),
        name="table_grad",
    )(n_local, rows, dl, af, drow, frow, flat, dx)


def spread_kernel(own_ref, frozen_ref, out_ref):
    devices, _, _, wide = out_ref.shape
    units, rows = wide // 2, own_ref.shape[0]
    bf16 = jnp.bfloat16
    out_ref[...] = jnp.zeros_like(out_ref)
    for side in range(2):
        for d in range(devices):
            at = (side * devices + d) * units
            out_ref[d, 0, :rows, side * units : (side + 1) * units] = own_ref[:, at : at + units].astype(bf16)
            out_ref[d, 1, :rows, side * units : (side + 1) * units] = frozen_ref[:, at : at + units]


def spread(own, frozen, devices, units, rows_up):
    vm = pl.BlockSpec(memory_space=pltpu.VMEM)
    return pl.pallas_call(
        spread_kernel,
        out_shape=jax.ShapeDtypeStruct((devices, 2, rows_up, 2 * units), jnp.bfloat16),
        in_specs=[vm, vm],
        out_specs=vm,
        compiler_params=pltpu.CompilerParams(vmem_limit_bytes=48 * 2**20),
        name="spread",
    )(own, frozen)


def join_kernel(g_ref, out_ref):
    devices, _, wide = g_ref.shape
    units, rows = wide // 2, out_ref.shape[0]
    for side in range(2):
        for d in range(devices):
            at = (side * devices + d) * units
            out_ref[:, at : at + units] = g_ref[d, :rows, side * units : (side + 1) * units].astype(jnp.float32)


def join(g, rows, units):
    vm = pl.BlockSpec(memory_space=pltpu.VMEM)
    return pl.pallas_call(
        join_kernel,
        out_shape=jax.ShapeDtypeStruct((rows, 2 * units * g.shape[0]), jnp.float32),
        in_specs=[vm],
        out_specs=vm,
        compiler_params=pltpu.CompilerParams(vmem_limit_bytes=48 * 2**20),
        name="join",
    )(g)


def wide(rows):
    return 1024 if rows % 1024 == 0 else 512


def head_kernel(block, span, own_ref, frozen_ref, af_ref, aim_ref, st_ref, logit_ref):
    step = pl.program_id(0)
    f32 = jnp.float32
    n_rows = af_ref.shape[1]

    @pl.when(step == 0)
    def _():
        st_ref[...] = jnp.zeros_like(st_ref)
        for model in range(2):
            st_ref[3 * model : 3 * model + 1, :] = jnp.full((1, n_rows), -1e30, f32)

    inside = step * span + lax.broadcasted_iota(jnp.int32, (span, 1), 0) < block
    shift = jnp.where(inside, 0.0, -1e30)
    frozen = jnp.where(inside, frozen_ref[...].astype(f32), 0.0).astype(jnp.bfloat16)
    logits = [last_last(own_ref[...], af_ref[0]) + shift, last_last(frozen, af_ref[1]) + shift]
    logit_ref[...] = logits[0]
    hit = lax.broadcasted_iota(jnp.int32, (span, n_rows), 0) == aim_ref[...] - step * span
    for model, logit in enumerate(logits):
        top, total, found = (pl.ds(3 * model + k, 1) for k in range(3))
        new = jnp.maximum(st_ref[top, :], jnp.max(logit, axis=0, keepdims=True))
        fall = jnp.exp(st_ref[top, :] - new)
        st_ref[total, :] = st_ref[total, :] * fall + jnp.sum(jnp.exp(logit - new), axis=0, keepdims=True)
        st_ref[top, :] = new
        st_ref[found, :] += jnp.sum(jnp.where(hit, logit, 0.0), axis=0, keepdims=True)


def head(own, frozen, af, aim):
    rows, width = own.shape
    n_rows = af.shape[1]
    span = wide(rows)
    whole = lambda shape: pl.BlockSpec(shape, lambda i: (0,) * len(shape))
    return pl.pallas_call(
        functools.partial(head_kernel, frozen.shape[0], span),
        grid=(rows // span,),
        out_shape=[jax.ShapeDtypeStruct((8, n_rows), jnp.float32), jax.ShapeDtypeStruct((rows, n_rows), jnp.float32)],
        in_specs=[
            pl.BlockSpec((span, width), lambda i: (i, 0)), pl.BlockSpec((span, width), lambda i: (i, 0)),
            whole(af.shape), whole(aim.shape),
        ],
        out_specs=[whole((8, n_rows)), pl.BlockSpec((span, n_rows), lambda i: (i, 0))],
        compiler_params=pltpu.CompilerParams(vmem_limit_bytes=56 * 2**20),
        name="head",
    )(own, frozen, af, aim)


def head_back_kernel(logit_ref, own_ref, lse_ref, dlp_ref, aim_ref, dl_ref, d_af_ref, acc):
    step = pl.program_id(0)
    bf16 = jnp.bfloat16

    @pl.when(step == 0)
    def _():
        acc[...] = jnp.zeros_like(acc)

    place = lax.broadcasted_iota(jnp.int32, logit_ref.shape, 0)
    hot = jnp.where(place == aim_ref[...] - step * logit_ref.shape[0], 1.0, 0.0)
    d_logit = (dlp_ref[...] * (hot - jnp.exp(logit_ref[...] - lse_ref[...]))).astype(bf16)
    dl_ref[...] = d_logit
    acc[...] += first_first(d_logit, own_ref[...])

    @pl.when(step == pl.num_programs(0) - 1)
    def _():
        d_af_ref[0] = acc[...].astype(bf16)


def head_back(logits, own, lse, dlp, aim):
    rows, width = own.shape
    n_rows = logits.shape[1]
    span = wide(rows)
    whole = lambda shape: pl.BlockSpec(shape, lambda i: (0,) * len(shape))
    return pl.pallas_call(
        head_back_kernel,
        grid=(rows // span,),
        out_shape=[
            jax.ShapeDtypeStruct((rows, n_rows), jnp.bfloat16),
            jax.ShapeDtypeStruct((1, n_rows, width), jnp.bfloat16),
        ],
        in_specs=[
            pl.BlockSpec((span, n_rows), lambda i: (i, 0)), pl.BlockSpec((span, width), lambda i: (i, 0)),
            whole(lse.shape), whole(dlp.shape), whole(aim.shape),
        ],
        out_specs=[pl.BlockSpec((span, n_rows), lambda i: (i, 0)), whole((1, n_rows, width))],
        scratch_shapes=[pltpu.VMEM((n_rows, width), jnp.float32)],
        compiler_params=pltpu.CompilerParams(vmem_limit_bytes=56 * 2**20),
        name="head_back",
    )(logits, own, lse, dlp, aim)


def adam_step(w, g, m, v, clip):
    g = g.astype(jnp.float32) * clip
    m_new = MOM1 * m + (1.0 - MOM1) * g
    v_new = MOM2 * v + (1.0 - MOM2) * g * g
    update = m_new / (1.0 - MOM1**STEP) / (jnp.sqrt(v_new / (1.0 - MOM2**STEP)) + EPS_ADAM)
    return w - RATE * (update + DECAY * w), m_new, v_new, g


def blend(parts, lane):
    f32 = jnp.float32
    n_models = len(parts[0][0]) // PAIRS
    is_top = lax.rem(lane, 32) < 16
    stats = [p[1][0] for p in parts]
    top = stats[0]
    for s in stats[1:]:
        top = jnp.maximum(top, s)
    weights = [jnp.exp(jnp.where(is_top, s - top, 0.0)) for s in stats]
    total = sum(s * pltpu.roll(w, 16, 1) for s, w in zip(stats, weights))
    planes = []
    for model in range(n_models):
        for pair in range(PAIRS):
            at = 32 * model + 2 * pair
            acc = None
            for p, w in zip(parts, weights):
                each = jnp.where(lane < 64, w[:, at : at + 1], w[:, at + 1 : at + 2])
                term = p[0][model * PAIRS + pair].astype(f32) * each
                acc = term if acc is None else acc + term
            planes.append(acc)
    return planes, [jnp.where(is_top, top, total)]


def mix_phase(ins, outs, scr, send_sems, recv_sems, line, plane, other):
    (o_ref, st_ref), (oo_ref, so_ref) = ins, outs
    core_o, sum_o, plane_o, keep_o, line_o, core_s, sum_s, plane_s, keep_s, line_s = scr
    _, n_y, n_batch = places()
    half, y, core, batch = coords()
    n_plane = 2 * n_y
    spot = half * n_y + y
    size = oo_ref.shape[1]
    lane = lax.broadcasted_iota(jnp.int32, (size, 128), 1)
    order = list(range(1, n_batch)) + [0]
    spots = [to for _, to, _ in plane] + [spot]
    slots = iter(range(2 * (n_plane * n_batch + (n_plane - 1) * n_batch + n_batch - 1)))

    def send(src, dst, who):
        slot = next(slots)
        return push(src, dst, send_sems.at[slot], recv_sems.at[slot], who)

    def rows(side, where, j):
        at = (side * n_plane + where) * n_batch + lax.rem(batch + j, n_batch)
        return pl.ds(pl.multiple_of(at * size, size), size)

    def store(o, s, merged):
        for k, value in enumerate(merged[0]):
            o[k] = value.astype(o.dtype)
        for k, value in enumerate(merged[1]):
            s[k] = value

    by_core, by_plane, by_line = {}, {}, {}
    for j in order:
        for p in range(n_plane):
            at = rows(1 - core, spots[p], j)
            by_core[p, j] = (
                send(o_ref.at[:, at, :], core_o.at[p, j], other[0]), send(st_ref.at[:, at, :], core_s.at[p, j], other[0])
            )

    def mine(p, j):
        at = rows(core, spots[p], j)
        for copy in by_core[p, j]:
            copy.wait_recv()
        return blend([(o_ref[:, at, :], st_ref[:, at, :]), (core_o[p, j], core_s[p, j])], lane)

    for j in order:
        for p in range(n_plane - 1):
            store(sum_o.at[p, j], sum_s.at[p, j], mine(p, j))
            by_plane[p, j] = (
                send(sum_o.at[p, j], plane_o.at[p, j], plane[p][0]), send(sum_s.at[p, j], plane_s.at[p, j], plane[p][0])
            )
    for j in order:
        parts = [mine(n_plane - 1, j)]
        for p in range(n_plane - 1):
            for copy in by_plane[p, j]:
                copy.wait_recv()
            parts.append((plane_o[p, j], plane_s[p, j]))
        merged = blend(parts, lane)
        if j:
            store(keep_o.at[j - 1], keep_s.at[j - 1], merged)
            by_line[j] = (
                send(keep_o.at[j - 1], line_o.at[j - 1], line[j - 1][0]),
                send(keep_s.at[j - 1], line_s.at[j - 1], line[j - 1][0]),
            )
    parts = [merged]
    for j in range(1, n_batch):
        for copy in by_line[j]:
            copy.wait_recv()
        parts.append((line_o[j - 1], line_s[j - 1]))
    store(oo_ref, so_ref, blend(parts, lane))
    for group in (by_core, by_plane, by_line):
        for pair in group.values():
            for copy in pair:
                copy.wait_send()


def low(x):
    return x.astype(jnp.bfloat16)


def split_dot(x, w):
    high = low(x)
    return straight(high, w) + straight(low(x - high.astype(jnp.float32)), w)


def turn_rows(x, cosine, sine, sign):
    lane = lax.broadcasted_iota(jnp.int32, x.shape, 1)
    mixed = jnp.where(lax.rem(lane, 64) < 32, -sign * pltpu.roll(x, 96, 1), sign * pltpu.roll(x, 32, 1))
    return x * cosine + mixed * sine


def queries(totals, consts, staged, extras):
    w_one, w_two, places_ref, gain_ref, bias_ref, cosine_ref, sine_ref, x_ref = consts
    q_ref, a1_ref = staged
    for model, w_ref in enumerate((w_one, w_two)):
        normed, _ = norm_forward(x_ref[model], gain_ref[model])
        normed = low(normed)
        if model == 0:
            a1_ref[0] = normed
        mixed = straight(low(straight(normed, places_ref[...])), w_ref[...]) + bias_ref[model]
        for p in range(PAIRS):
            part = turn_rows(mixed[:, 128 * p : 128 * p + 128], cosine_ref[...], sine_ref[...], 1.0)
            q_ref[model * PAIRS + p] = low(part)


def attended(totals, consts, staged, extras):
    w_one, w_two, places_ref, gain_ref, x_ref = consts
    a2_ref, o_ref = staged
    x1_ref, own_ref, lse_ref = extras
    lane = lax.broadcasted_iota(jnp.int32, (own_ref.shape[0], 128), 1)
    for model, w_ref in enumerate((w_one, w_two)):
        stats = totals[1][0]
        if model == 0:
            total = jnp.where(lane < QUERY_HEADS, pltpu.roll(stats, 112, 1), 1.0)
            lse_ref[...] = stats + jnp.log(total)
        first = 32 * model + 16
        share = 1.0 / jnp.where((lane >= first) & (lane < first + QUERY_HEADS), stats, 1.0)
        parts = []
        for p in range(PAIRS):
            at = first + 2 * p
            each = jnp.where(lane < 64, share[:, at : at + 1], share[:, at + 1 : at + 2])
            parts.append(low(totals[0][model * PAIRS + p] * each))
        o = jnp.concatenate(parts, axis=1)
        if model == 0:
            o_ref[0] = o
            own_ref[...] = o
        x1 = x_ref[model] + straight(low(straight(o, places_ref[...])), w_ref[...])
        x1_ref[model] = x1
        a2, _ = norm_forward(x1, gain_ref[model])
        a2_ref[model] = low(straight(low(a2), places_ref[...]))


def finals(totals, consts, staged, extras):
    gain_ref, x1_ref = consts
    for model in range(2):
        x2 = x1_ref[model] + totals[0][model]
        extras[0][model] = x2
        af, _ = norm_forward(x2, gain_ref[model])
        staged[0][model] = low(af)


def scale_of(x):
    return lax.rsqrt(jnp.mean(x * x, axis=-1, keepdims=True) + EPS_NORM)


def finals_back(totals, consts, staged, extras):
    gain_ref, x2_ref = consts
    x2 = x2_ref[0]
    d_out, d_gain = norm_backward(totals[0][0], x2, scale_of(x2), gain_ref[0])
    staged[0][0] = low(d_out)
    extras[0][...] = d_out
    extras[1][...] = jnp.sum(d_gain, axis=0, keepdims=True)


def attended_back(totals, consts, staged, extras):
    w_ref, from_ref, gain_ref, x1_ref, d_out_ref, o_ref, lse_ref = consts
    d_attn_ref, d_o_ref, stats_ref = staged
    d_mid_ref, d_gain_ref = extras
    x1 = x1_ref[0]
    d_mid, d_gain = norm_backward(split_dot(totals[0][0], from_ref[...]), x1, scale_of(x1), gain_ref[0])
    d_mid = d_mid + d_out_ref[...]
    d_mid_ref[...] = d_mid
    d_gain_ref[...] = jnp.sum(d_gain, axis=0, keepdims=True)
    d_attn = low(d_mid)
    d_attn_ref[0] = d_attn
    d_o = low(straight(low(last_last(d_attn, w_ref[...])), from_ref[...]))
    product = d_o.astype(jnp.float32) * o_ref[...].astype(jnp.float32)
    lane = lax.broadcasted_iota(jnp.int32, (d_o.shape[0], 128), 1)
    stats = jnp.where(lane < QUERY_HEADS, lse_ref[...], 0.0)
    for p in range(PAIRS):
        d_o_ref[p] = d_o[:, 128 * p : 128 * p + 128]
        part = product[:, 128 * p : 128 * p + 128]
        first = jnp.sum(jnp.where(lane < 64, part, 0.0), axis=-1, keepdims=True)
        second = jnp.sum(jnp.where(lane < 64, 0.0, part), axis=-1, keepdims=True)
        stats = jnp.where(lane == 16 + 2 * p, first, stats)
        stats = jnp.where(lane == 17 + 2 * p, second, stats)
    stats_ref[0] = stats


def queries_back(totals, consts, staged, extras):
    w_ref, from_ref, gain_ref, x_ref, d_mid_ref, cosine_ref, sine_ref = consts
    dq_ref, d_row_ref = staged
    g_kv_ref, d_gain_ref, d_bias_ref = extras
    g_kv_ref[...] = totals[1][0]
    parts = [turn_rows(totals[0][p], cosine_ref[...], sine_ref[...], -1.0) for p in range(PAIRS)]
    dq = low(jnp.concatenate(parts, axis=1))
    dq_ref[0] = dq
    d_bias_ref[...] = jnp.sum(dq.astype(jnp.float32), axis=0, keepdims=True)
    x = x_ref[0]
    d_row, d_gain = norm_backward(split_dot(last_last(dq, w_ref[...]), from_ref[...]), x, scale_of(x), gain_ref[0])
    d_row_ref[0] = low(d_row + d_mid_ref[...])
    d_gain_ref[...] = jnp.sum(d_gain, axis=0, keepdims=True)


def keep(totals, consts, staged, extras):
    for total, extra in zip(totals, extras):
        extra[...] = total[...]


AXES = ("half", "mp", "batch")


def frequencies():
    half_size = HEAD_SIZE // 2
    return THETA ** (-(jnp.arange(half_size, dtype=jnp.float32) * 2.0) / HEAD_SIZE)


def bmm(x, w):
    return jnp.stack([jnp.dot(x[i], w[i], preferred_element_type=jnp.float32) for i in range(2)])


def body(
    tokens, lengths, labels, scored, qkv_weight, out_weight, gu_weight, down_weight, embed_weight, small_params,
    moment_qkv, moment_out, moment_gu, moment_down, moment_embed, moment_small,
    square_qkv, square_out, square_gu, square_down, square_embed, square_small,
    ref_qkv, ref_out, ref_gu, ref_down, ref_embed, ref_small,
):
    masters = (qkv_weight, out_weight, gu_weight, down_weight, embed_weight, small_params)
    firsts = (moment_qkv, moment_out, moment_gu, moment_down, moment_embed, moment_small)
    seconds = (square_qkv, square_out, square_gu, square_down, square_embed, square_small)
    bf16, f32, i32 = jnp.bfloat16, jnp.float32, jnp.int32
    n_mp, n_batch = lax.axis_size("mp"), lax.axis_size("batch")
    devices = 2 * n_mp * n_batch
    n_y = n_mp // 2
    block = embed_weight.shape[0]
    feats = qkv_weight.shape[0]
    units = down_weight.shape[0]
    rollouts = MICRO * n_batch
    length = n_mp * TOK
    rp = n_mp * P_SIZE
    n_rows = rollouts * rp
    own_rows = n_rows // devices
    lin = lax.axis_index(AXES)
    com = comm_index()
    base = lin * block

    feats_up = -(-feats // 16) * 16

    def to_up(x):
        return jnp.pad(x, ((0, feats_up - feats), (0, 0)))

    feat = jnp.arange(MODEL_WIDTH, dtype=i32)
    padded = jnp.arange(devices * feats_up, dtype=i32)
    to_order = (padded[None, :] == (feat // feats * feats_up + feat % feats)[:, None]).astype(bf16)
    owner = feat // feats
    mp_of = owner // n_batch % n_mp
    exchanged = ((mp_of % 2 * 2 + owner // (n_mp * n_batch)) * n_y + mp_of // 2) * n_batch + owner % n_batch
    to_exchange = (padded[:, None] == (exchanged * feats_up + feat % feats)[None, :]).astype(bf16)
    from_order = (padded[:, None] == (feat // feats * feats_up + feat % feats)[None, :]).astype(bf16)

    def placed(x):
        x = jnp.pad(x.astype(bf16), ((0, 0), (0, 128 - x.shape[1])))
        x = jnp.roll(x, lin * small_params.shape[1], axis=1)
        return jnp.pad(x, ((0, -x.shape[0] % feats_up), (0, 0)))

    qkv_low = qkv_weight.astype(bf16)
    early = to_up(
        jnp.concatenate(
            [qkv_low[:, :MODEL_WIDTH], ref_qkv[:, :MODEL_WIDTH], qkv_low[:, MODEL_WIDTH:], ref_qkv[:, MODEL_WIDTH:]], axis=1
        )
    )
    smalls = [placed(small_params), placed(ref_small)]
    tall = smalls[0].shape[0] // feats_up
    smalls = [x.reshape(tall, feats_up, 128)[k] for x in smalls for k in range(tall)]
    early = lax.all_gather(jnp.concatenate([early] + smalls, axis=1), AXES, axis=0, tiled=True)
    at_small = 2 * QKV
    down_low = jnp.stack([down_weight.astype(bf16), ref_down])

    ids = tokens.transpose(0, 2, 1, 3).reshape(rollouts, length)
    lens = lengths.reshape(rollouts)
    spots = jnp.arange(length, dtype=i32)
    flat_ids = jnp.arange(rollouts * length, dtype=i32).reshape(rollouts, length)
    bits = max(1, (block - 1).bit_length())
    local = (ids >= base) & (ids < base + block) & (spots[None, :] < lens[:, None])
    key = jnp.where(local, (flat_ids << bits) + (ids - base), jnp.int32(2**31 - 1)).reshape(-1)
    key = lax.sort(key)
    n_local = jnp.sum(local.astype(i32))
    live = jnp.arange(rollouts * length, dtype=i32) < n_local
    row_of = jnp.where(live, key & ((1 << bits) - 1), 0)
    flat_of = jnp.where(live, key >> bits, 1 << 22).reshape(-1, TILE)
    pos_of = jnp.where(live, (key >> bits) % length, 0).reshape(-1, TILE).astype(f32)
    tile_lo = flat_of[:, 0] // length
    tile_hi = jnp.max(jnp.where(live, (key >> bits) // length, -1).reshape(-1, TILE), axis=1)
    n_one = n_local.reshape(1)

    picks = scored.transpose(0, 2, 1, 3) + (jnp.arange(n_mp, dtype=i32) * TOK)[None, None, :, None]
    picks = picks.reshape(rollouts, rp)
    valid = (picks + 1 < lens[:, None]).astype(f32)
    count = jnp.sum(valid)
    after = picks[:, :, None] + 1 == spots[None, None, :]
    targets = jnp.sum(jnp.where(after, ids[:, None, :], 0), axis=2).reshape(-1)
    frow = (picks + (jnp.arange(rollouts, dtype=i32) * length)[:, None]).reshape(-1)
    frow_wide = jnp.broadcast_to(frow[:, None], (n_rows, 128))

    low_table, picked, x_tok = lookup(n_one, row_of, embed_weight, ref_embed, flat_of, frow_wide)
    out_both = to_up(jnp.concatenate([out_weight.astype(bf16), ref_out], axis=1))
    picked, out_both = lax.optimization_barrier((picked, out_both))
    late = lax.all_gather(out_both, AXES, axis=0, tiled=True)
    row = (own_rows, MODEL_WIDTH)
    (x0,) = exchange("rows_found", 1, [picked], [], [], keep, [], [((2,) + row, f32)])

    x0, tile_lo, tile_hi, targets, valid, to_exchange, from_order, flat_of, pos_of = lax.optimization_barrier(
        (x0, tile_lo, tile_hi, targets, valid, to_exchange, from_order, flat_of, pos_of)
    )

    w_kv = jnp.dot(to_order, early[:, 2 * MODEL_WIDTH : at_small], preferred_element_type=f32).astype(bf16)
    small_rows = small_params.shape[0]
    flat_small = jnp.sum(early[:, at_small:].astype(f32).reshape(devices, feats_up, -1), axis=0)
    flat_small = flat_small.reshape(feats_up, 2, tall, 128).transpose(1, 2, 0, 3).reshape(2, tall * feats_up, 128)
    flat_small = flat_small[:, :small_rows].reshape(2, -1)
    gain_attn = flat_small[:, None, :MODEL_WIDTH]
    gain_mlp = flat_small[:, None, MODEL_WIDTH : 2 * MODEL_WIDTH]
    gain_final = flat_small[:, None, 2 * MODEL_WIDTH : 3 * MODEL_WIDTH]
    bias = flat_small[:, None, 3 * MODEL_WIDTH :]

    freq_wide = jnp.tile(frequencies(), 4).reshape(1, 128)
    my_pos = lax.dynamic_slice_in_dim(picks.reshape(-1), com * own_rows, own_rows)
    angle = my_pos.astype(f32)[:, None] * freq_wide
    cosine, sine = jnp.cos(angle), jnp.sin(angle)
    q_all, a1_all = exchange(
        "rows_queries", 2, [], [(early, 0, MODEL_WIDTH), (early, MODEL_WIDTH, MODEL_WIDTH)],
        [to_order, gain_attn, bias[:, :, :MODEL_WIDTH], cosine, sine, x0], queries,
        [(2 * PAIRS, own_rows, 128, bf16), (1,) + row + (bf16,)], [],
    )
    q_all, gu_sent = lax.optimization_barrier((q_all, spread(gu_weight, ref_gu, devices, units, feats_up)))
    gu_cols = lax.all_to_all(gu_sent, AXES, split_axis=0, concat_axis=0, tiled=True)
    w_gu = tuple(gu_cols[:, model].reshape(devices * feats_up, 2 * units) for model in range(2))

    o_part, st_part, kv_tok = attend(
        n_one, tile_lo, tile_hi, q_all, x_tok, w_kv, gain_attn, bias[:, :, MODEL_WIDTH:], freq_wide, frow_wide, flat_of,
        pos_of, length, rp,
    )
    o_part, late = lax.optimization_barrier((o_part, late))
    a2_all, o_all, x1, o_own, lse = exchange(
        "rows_attended", 3, [o_part, st_part], [(late, 0, MODEL_WIDTH), (late, MODEL_WIDTH, MODEL_WIDTH)],
        [to_order, gain_mlp, x0], attended,
        [(2, own_rows, devices * feats_up, bf16), (1,) + row + (bf16,)],
        [((2,) + row, f32), (row, bf16), ((own_rows, 128), f32)], mix_phase,
    )
    gate_up = bmm(a2_all, w_gu)
    gate, up = gate_up[:, :, :units], gate_up[:, :, units:]
    hidden = (jax.nn.silu(gate) * up).astype(bf16)
    af_all, x2 = exchange(
        "rows_finals", 5, [bmm(hidden, down_low).astype(bf16)], [], [gain_final, x1], finals, [(2,) + row + (bf16,)],
        [((2,) + row, f32)],
    )

    aim = jnp.where((targets >= base) & (targets < base + block), targets - base, -1).reshape(1, -1)
    stats, logits = head(low_table, ref_embed, af_all, aim)
    (stats_all,) = gather([stats[None]], 7)
    stats_all = stats_all.reshape(devices, 8, n_rows)
    lps, lses = [], []
    for i in range(2):
        peaks = stats_all[:, 3 * i]
        peak = jnp.max(peaks, axis=0)
        sums = jnp.sum(stats_all[:, 3 * i + 1] * jnp.exp(peaks - peak[None]), axis=0)
        lses.append(peak + jnp.log(sums))
        lps.append(jnp.sum(stats_all[:, 3 * i + 2], axis=0) - lses[i])
    ratio = (lps[0] - lps[1]).reshape(rollouts, rp)
    factor = BETA * n_rows / count
    reward = factor * jnp.sum(valid * ratio, axis=1)
    d_reward = (jax.nn.sigmoid(reward) - labels.reshape(rollouts).astype(f32)) / rollouts
    d_lp = (valid * (d_reward * factor)[:, None]).reshape(-1)

    d_logits, d_af = head_back(logits, low_table, lses[0].reshape(1, -1), d_lp.reshape(1, -1), aim)
    d_branch, d_out, g_gain_final = exchange(
        "rows_finals_back", 8, [d_af], [], [gain_final, x2], finals_back, [(1,) + row + (bf16,)],
        [(row, f32), ((1, MODEL_WIDTH), f32)],
    )
    d_branch = d_branch[0]
    g_down = lax.dot_general(hidden[0], d_branch, (((0,), (0,)), ((), ())), preferred_element_type=f32)
    d_hidden = lax.dot_general(d_branch, down_low[0], (((1,), (1,)), ((), ())), preferred_element_type=f32)
    sigma = jax.nn.sigmoid(gate[0])
    d_gate = d_hidden * up[0] * sigma * (1.0 + gate[0] * (1.0 - sigma))
    d_up = d_hidden * gate[0] * sigma
    d_gate_up = jnp.concatenate([d_gate, d_up], axis=1).astype(bf16)
    d_a2 = lax.dot_general(d_gate_up, w_gu[0], (((1,), (1,)), ((), ())), preferred_element_type=f32)
    d_attn_all, d_o_all, row_stats_all, d_mid, g_gain_mlp = exchange(
        "rows_attended_back", 10, [d_a2.astype(bf16)[None]], [(late, 0, MODEL_WIDTH)], [from_order, gain_mlp, x1, d_out, o_own, lse],
        attended_back, [(1,) + row + (bf16,), (PAIRS, own_rows, 128, bf16), (1, own_rows, 128, f32)],
        [(row, f32), ((1, MODEL_WIDTH), f32)],
    )
    d_attn_all = d_attn_all[0]

    g_gu = lax.dot_general(a2_all[0], d_gate_up, (((0,), (0,)), ((), ())), preferred_element_type=f32)
    gu_square = jnp.sum(g_gu * g_gu)
    g_gu = g_gu.astype(bf16).reshape(devices, feats_up, 2 * units)
    g_gu, d_o_all = lax.optimization_barrier((g_gu, d_o_all))
    g_gu = lax.all_to_all(g_gu, AXES, split_axis=0, concat_axis=0, tiled=True)
    dq_part, g_kv_part, g_gain_kv, g_bias_kv, dx_tok = attend_back(
        n_one, tile_lo, tile_hi, q_all, d_o_all, row_stats_all[0], x_tok, kv_tok, w_kv, gain_attn[:1],
        freq_wide, frow_wide, flat_of, pos_of, length, rp,
    )
    dq_part, g_gu = lax.optimization_barrier((dq_part, g_gu))
    g_kv_part = jnp.dot(to_exchange, g_kv_part.astype(bf16), preferred_element_type=f32).astype(bf16)
    dq_all, d_row_all, g_kv, g_gain_row, g_bias_q = exchange(
        "rows_queries_back", 12, [dq_part, g_kv_part[None]],
        [(early, 0, MODEL_WIDTH)], [from_order, gain_attn, x0, d_mid, cosine, sine], queries_back,
        [(1,) + row + (bf16,), (1,) + row + (bf16,)],
        [((feats_up, 256), f32), ((1, MODEL_WIDTH), f32), ((1, MODEL_WIDTH), f32)],
    )
    g_kv = g_kv[:feats]
    dq_all = dq_all[0]

    embed_grad, embed_square = table_grad(
        n_one, row_of, d_logits, af_all, d_row_all[0], frow.reshape(1, -1).astype(f32), flat_of, dx_tok, block
    )

    def mine(rows, grads):
        cols = lax.dynamic_slice_in_dim(rows, lin * feats, feats, 1)
        return lax.dot_general(cols, grads, (((0,), (0,)), ((), ())), preferred_element_type=f32)

    g_out = mine(o_all[0], d_attn_all)
    g_q = mine(a1_all[0], dq_all)
    g_qkv = jnp.concatenate([g_q, g_kv], axis=1)

    small_part = jnp.concatenate(
        [
            jnp.sum(g_gain_kv, axis=0) + g_gain_row[0],
            g_gain_mlp[0],
            g_gain_final[0],
            g_bias_q[0],
            jnp.sum(g_bias_kv, axis=0),
        ]
    )
    square_part = (
        jnp.sum(g_qkv * g_qkv) + jnp.sum(g_out * g_out) + gu_square + jnp.sum(g_down * g_down) + jnp.sum(embed_square)
    )
    last = jnp.concatenate([small_part, jnp.full((128,), square_part, f32), jnp.zeros((128,), f32)]).reshape(1, -1, 128)
    (last_all,) = gather([last], 14)
    last_all = jnp.sum(last_all.reshape(devices, -1, 128), axis=0)
    g_small = last_all[:small_rows]
    norm = jnp.sqrt(jnp.sum(g_small * g_small) + last_all[small_rows, 0])
    g_small = lax.dynamic_slice_in_dim(g_small, lin * small_params.shape[1], small_params.shape[1], 1)

    g_gu = join(g_gu, feats, units)
    owned_grads = (g_qkv, g_out, g_gu, g_down, embed_grad, g_small)
    clip = jnp.minimum(1.0, CLIP / (norm + 1e-06))
    new_weights, new_firsts, new_seconds, new_lows, clipped_list = ([], [], [], [], [])
    for w, g, m, v in zip(masters, owned_grads, firsts, seconds):
        w_new, m_new, v_new, g = adam_step(w, g, m, v, clip)
        w_low = w_new.astype(bf16)
        new_weights.append(w_new)
        new_firsts.append(m_new)
        new_seconds.append(v_new)
        clipped_list.append(g)
        new_lows.append(w_low)
    return (
        *new_weights[:5], clipped_list[5], *new_firsts, *new_seconds, *new_lows[:5], norm,
    )


def solution(mesh):
    rows, cols = P(AXES, None), P(None, AXES)
    six = (rows, rows, rows, rows, rows, cols)
    in_specs = (P(), P(), P(), P()) + six * 4
    out_specs = six * 3 + (rows,) * 5 + (P(),)
    return jax.shard_map(body, mesh=mesh, in_specs=in_specs, out_specs=out_specs, check_vma=False)
```

```python
import functools

import jax
import jax.numpy as jnp
from jax import lax
from jax.experimental import pallas as pl
from jax.experimental.pallas import tpu as pltpu
from jax.sharding import PartitionSpec as P

MODEL_WIDTH = 896
QUERY_HEADS = 14
KEY_VALUE_HEADS = 2
HEAD_SIZE = 64
FF = 4864
QKV = 1152
TOK = 256
P_SIZE = 16
MICRO = 2
STEP = 5

EPS_NORM = 1e-06
THETA = 1000000.0
BETA = 0.05
CLIP = 0.1
RATE = 0.03
DECAY = 0.01
MOM1 = 0.5
MOM2 = 0.5
EPS_ADAM = 1e-08

MESH = pl.DeviceIdType.MESH

def places():
    n_mp, n_batch = lax.axis_size("mp"), lax.axis_size("batch")
    return 2, n_mp // 2, n_batch


def coords():
    mp = lax.axis_index("mp")
    return lax.axis_index("half"), mp // 2, lax.rem(mp, 2), lax.axis_index("batch")


def comm_index():
    _, n_y, n_batch = places()
    half, y, core, batch = coords()
    return ((core * 2 + half) * n_y + y) * n_batch + batch


def peers():
    _, n_y, n_batch = places()
    half, y, core, batch = coords()
    line = []
    for k in range(1, n_batch):
        to, frm = lax.rem(batch + k, n_batch), lax.rem(batch + n_batch - k, n_batch)
        line.append(({"half": half, "mp": y * 2 + core, "batch": to}, to, frm))
    plane = []
    n_plane = 2 * n_y
    spot = half * n_y + y
    for k in range(1, n_plane):
        to, frm = lax.rem(spot + k, n_plane), lax.rem(spot + n_plane - k, n_plane)
        plane.append(
            ({"half": to // n_y, "mp": lax.rem(to, n_y) * 2 + core, "batch": batch}, to, frm)
        )
    other = ({"half": half, "mp": y * 2 + (1 - core), "batch": batch}, 1 - core, 1 - core)
    return line, plane, other


def greet(line, plane, other):
    barrier = pltpu.get_barrier_semaphore()
    everyone = line + plane + [other]
    for who, _, _ in everyone:
        pl.semaphore_signal(barrier, inc=1, device_id=who, device_id_type=MESH)
    pl.semaphore_wait(barrier, len(everyone))


def push(src, dst, send_sem, recv_sem, who):
    copy = pltpu.make_async_remote_copy(
        src_ref=src,
        dst_ref=dst,
        send_sem=send_sem,
        recv_sem=recv_sem,
        device_id=who,
        device_id_type=MESH,
    )
    copy.start()
    return copy


def gather_phase(ins, outs, send_sems, recv_sems, own_sem, line, plane, other):
    n_arr = len(ins)
    _, n_y, n_batch = places()
    half, y, core, batch = coords()
    n_plane = 2 * n_y
    spot = half * n_y + y
    slots = iter(range(n_arr * (n_batch - 1 + n_plane * n_batch + (n_plane - 1) * n_batch)))

    def rows(i, where, j):
        size = ins[i].shape[1]
        at = (core * n_plane + where) * n_batch + lax.rem(batch + n_batch - j, n_batch)
        return outs[i].at[:, pl.ds(pl.multiple_of(at * size, size), size), :]

    def send(src, dst, who):
        slot = next(slots)
        return push(src, dst, send_sems.at[slot], recv_sems.at[slot], who)

    local, by_line, by_plane, by_core = [], [], [], []
    for i in range(n_arr):
        by_line.append([send(ins[i], rows(i, spot, 0), who) for who, _, _ in line])
    for i in range(n_arr):
        by_plane.append([[send(ins[i], rows(i, spot, 0), who) for who, _, _ in plane]])
        by_core.append(send(ins[i], rows(i, spot, 0), other[0]))
        copy = pltpu.make_async_copy(ins[i], rows(i, spot, 0), own_sem.at[i])
        copy.start()
        local.append(copy)
    for j in range(1, n_batch):
        for i in range(n_arr):
            by_line[i][j - 1].wait_recv()
            by_plane[i].append([send(rows(i, spot, j), rows(i, spot, j), who) for who, _, _ in plane])
            by_core.append(send(rows(i, spot, j), rows(i, spot, j), other[0]))
    for j in range(n_batch):
        for i in range(n_arr):
            for k, (_, _, frm) in enumerate(plane):
                by_plane[i][j][k].wait_recv()
                by_core.append(send(rows(i, frm, j), rows(i, frm, j), other[0]))
    for copy in local:
        copy.wait()
    for copy in by_core:
        copy.wait_recv()
    for i in range(n_arr):
        for copy in by_line[i] + sum(by_plane[i], []):
            copy.wait_send()
    for copy in by_core:
        copy.wait_send()


def gather_kernel(n_arr, *refs):
    ins, outs = refs[:n_arr], refs[n_arr : 2 * n_arr]
    line, plane, other = peers()
    greet(line, plane, other)
    gather_phase(ins, outs, *refs[2 * n_arr :], line, plane, other)


def gather(arrays, cid, vmem=48):
    _, n_y, n_batch = places()
    n_plane = 2 * n_y
    total = 2 * n_plane * n_batch
    n = len(arrays)
    copies = n * ((n_batch - 1) + (n_plane - 1) * n_batch + n_plane * n_batch)
    return pl.pallas_call(
        functools.partial(gather_kernel, n),
        out_shape=[jax.ShapeDtypeStruct((a.shape[0], a.shape[1] * total, a.shape[2]), a.dtype) for a in arrays],
        in_specs=[pl.BlockSpec(memory_space=pltpu.VMEM)] * n,
        out_specs=[pl.BlockSpec(memory_space=pltpu.VMEM)] * n,
        scratch_shapes=[
            pltpu.SemaphoreType.DMA((copies,)),
            pltpu.SemaphoreType.DMA((copies,)),
            pltpu.SemaphoreType.DMA((n,)),
        ],
        compiler_params=pltpu.CompilerParams(
            collective_id=cid, has_side_effects=True, vmem_limit_bytes=vmem * 2**20
        ),
        name=f"gather_{cid}",
    )(*arrays)


def reduce_phase(ins, outs, scr, send_sems, recv_sems, line, plane, other):
    n_arr = len(ins)
    _, n_y, n_batch = places()
    half, y, core, batch = coords()
    n_plane = 2 * n_y
    spot = half * n_y + y
    f32 = jnp.float32
    slots = iter(range(n_arr * (n_plane * n_batch + (n_plane - 1) * n_batch + n_batch - 1)))
    order = list(range(1, n_batch)) + [0]
    spots = [to for _, to, _ in plane] + [spot]

    def send(src, dst, who):
        slot = next(slots)
        return push(src, dst, send_sems.at[slot], recv_sems.at[slot], who)

    def rows(i, side, where, j):
        size = outs[i].shape[1]
        at = (side * n_plane + where) * n_batch + lax.rem(batch + j, n_batch)
        return pl.ds(pl.multiple_of(at * size, size), size)

    by_core, by_plane, by_line = {}, {}, {}
    for j in order:
        for p in range(n_plane):
            for i in range(n_arr):
                src = ins[i].at[:, rows(i, 1 - core, spots[p], j), :]
                by_core[i, p, j] = send(src, scr[5 * i].at[p, j], other[0])

    def mine(i, p, j):
        by_core[i, p, j].wait_recv()
        return ins[i][:, rows(i, core, spots[p], j), :].astype(f32) + scr[5 * i][p, j].astype(f32)

    for j in order:
        for p in range(n_plane - 1):
            for i in range(n_arr):
                out = scr[5 * i + 1]
                out[p, j] = mine(i, p, j).astype(out.dtype)
                by_plane[i, p, j] = send(out.at[p, j], scr[5 * i + 2].at[p, j], plane[p][0])
    totals = {}
    for j in order:
        for i in range(n_arr):
            total = mine(i, n_plane - 1, j)
            for p in range(n_plane - 1):
                by_plane[i, p, j].wait_recv()
                total = total + scr[5 * i + 2][p, j].astype(f32)
            if j:
                out = scr[5 * i + 3]
                out[j - 1] = total.astype(out.dtype)
                by_line[i, j] = send(out.at[j - 1], scr[5 * i + 4].at[j - 1], line[j - 1][0])
            else:
                outs[i][...] = total
    for i in range(n_arr):
        for j in range(1, n_batch):
            by_line[i, j].wait_recv()
            outs[i][...] += scr[5 * i + 4][j - 1].astype(f32)
    for group in (by_core, by_plane, by_line):
        for copy in group.values():
            copy.wait_send()


def reduce_scratch(arrays):
    _, n_y, n_batch = places()
    n_plane = 2 * n_y
    scratch = []
    for a in arrays:
        m, rows, w = a.shape
        size = rows // (2 * n_plane * n_batch)
        for lead in ((n_plane, n_batch), (n_plane - 1, n_batch), (n_plane - 1, n_batch), (n_batch - 1,), (n_batch - 1,)):
            scratch.append(pltpu.VMEM(lead + (m, size, w), a.dtype))
    return scratch


def exchange_kernel(n_in, columns, n_const, n_out, n_extra, reducer, compute, *refs):
    refs = list(refs)

    def take(n):
        part = refs[:n]
        del refs[:n]
        return part

    n_fetch = len(columns)
    ins, sources, consts, outs, extras = take(n_in), take(n_fetch), take(n_const), take(n_out), take(n_extra)
    totals, staged, fetched = take(n_in), take(n_out), take(n_fetch)
    send_one, recv_one, send_two, recv_two, own_sem, fetch_sem = refs[-6:]
    line, plane, other = peers()
    copies = []
    for k, (first, width) in enumerate(columns):
        copy = pltpu.make_async_copy(sources[k].at[:, pl.ds(first, width)], fetched[k], fetch_sem.at[k])
        copy.start()
        copies.append(copy)
    greet(line, plane, other)
    if ins:
        reducer(ins, totals, refs[:-6], send_one, recv_one, line, plane, other)
    for copy in copies:
        copy.wait()
    compute(totals, fetched + consts, staged, extras)
    if outs:
        gather_phase(staged, outs, send_two, recv_two, own_sem, line, plane, other)


def exchange(name, cid, arrays, fetches, consts, compute, gathered, extras, reducer=reduce_phase):
    _, n_y, n_batch = places()
    n_plane = 2 * n_y
    total = 2 * n_plane * n_batch
    f32 = jnp.float32
    n_in, n_out = len(arrays), len(gathered)
    one = max(1, n_in) * (n_plane * n_batch + (n_plane - 1) * n_batch + n_batch - 1)
    two = max(1, n_out) * (n_batch - 1 + (n_plane - 1) * n_batch + n_plane * n_batch)
    vm = pl.BlockSpec(memory_space=pltpu.VMEM)
    dma = pltpu.SemaphoreType.DMA
    columns = tuple((first, width) for _, first, width in fetches)
    return pl.pallas_call(
        functools.partial(
            exchange_kernel, n_in, columns, len(consts), n_out, len(extras), reducer, compute
        ),
        out_shape=[jax.ShapeDtypeStruct((m, rows * total, w), t) for m, rows, w, t in gathered]
        + [jax.ShapeDtypeStruct(shape, t) for shape, t in extras],
        in_specs=[vm] * n_in + [pl.BlockSpec(memory_space=pl.ANY)] * len(fetches) + [vm] * len(consts),
        out_specs=[vm] * (n_out + len(extras)),
        scratch_shapes=[pltpu.VMEM((a.shape[0], a.shape[1] // total, a.shape[2]), f32) for a in arrays]
        + [pltpu.VMEM((m, rows, w), t) for m, rows, w, t in gathered]
        + [pltpu.VMEM((a.shape[0], width), a.dtype) for a, _, width in fetches]
        + reduce_scratch(arrays)
        + [dma((one,)), dma((one,)), dma((two,)), dma((two,)), dma((max(1, n_out),)), dma((max(1, len(fetches)),))],
        compiler_params=pltpu.CompilerParams(collective_id=cid, has_side_effects=True, vmem_limit_bytes=60 * 2**20),
        name=name,
    )(*arrays, *[a for a, _, _ in fetches], *consts)


def norm_forward(x, gain):
    scale = lax.rsqrt(jnp.mean(x * x, axis=-1, keepdims=True) + EPS_NORM)
    return (x * scale * gain, scale)


def norm_backward(d_out, x, scale, gain):
    d_gain = d_out * x * scale
    d_hat = d_out * gain
    d_x = scale * (d_hat - x * scale * scale * jnp.mean(d_hat * x, axis=-1, keepdims=True))
    return (d_x, d_gain)


HEAD_SLOTS = (0, 2, 4, 6, 1, 3, 5, 8, 10, 12, 7, 9, 11, 13)
COMBOS = ((0, 4, 0), (0, 3, 4), (4, 7, 7), (3, 7, 10))
PAIRS = QUERY_HEADS // 2
TILE = 128


def column(vector):
    return jnp.transpose(jnp.broadcast_to(vector.astype(jnp.float32), (128, 128)))


def last_last(a, b):
    return lax.dot_general(a, b, (((1,), (1,)), ((), ())), preferred_element_type=jnp.float32)


def first_first(a, b):
    return lax.dot_general(a, b, (((0,), (0,)), ((), ())), preferred_element_type=jnp.float32)


def straight(a, b):
    return jnp.dot(a, b, preferred_element_type=jnp.float32)


def lookup_kernel(
    block, span, n_ref, rows_ref, table_ref, frozen_ref, flat_ref, frow_ref,
    low_ref, picked_ref, x_ref, held, rough, staged, sem,
):
    step = pl.program_id(0)
    f32, bf16 = jnp.float32, jnp.bfloat16
    inside = step * span + lax.broadcasted_iota(jnp.int32, (span, 1), 0) < block
    low = jnp.where(inside, table_ref[...], 0.0).astype(bf16)
    low_ref[...] = low
    at = pl.multiple_of(step * span, span)
    held[0, pl.ds(at, span), :] = table_ref[...]
    held[1, pl.ds(at, span), :] = frozen_ref[...].astype(f32)

    @pl.when(step == pl.num_programs(0) - 1)
    def _():
        picked_ref[...] = jnp.zeros_like(picked_ref)
        n_rows = frow_ref.shape[0]

        def tile(i, _):
            def eight(k, _):
                for j in range(8):
                    place = k * 8 + j
                    row = rows_ref[i * TILE + place]
                    for model in range(2):
                        rough[model, pl.ds(place, 1), :] = held[model, pl.ds(row, 1), :]
                return 0

            lax.fori_loop(0, TILE // 8, eight, 0)
            slot = lax.rem(i, 2)
            where = pl.ds(pl.multiple_of(i * TILE, TILE), TILE)
            copy = pltpu.make_async_copy(staged.at[slot], x_ref.at[:, where, :], sem.at[slot])

            @pl.when(i >= 2)
            def _():
                copy.wait()

            staged[slot] = rough[...].astype(bf16)
            copy.start()
            match = frow_ref[...] == jnp.broadcast_to(flat_ref[pl.ds(i, 1), :], (n_rows, TILE))
            match = jnp.where(match, 1.0, 0.0).astype(bf16)
            for model in range(2):
                picked_ref[model] = picked_ref[model] + straight(match, staged[slot, model]).astype(bf16)
            return 0

        tiles = (n_ref[0] + TILE - 1) // TILE
        lax.fori_loop(0, tiles, tile, 0)
        for k in range(2):

            @pl.when(tiles > k)
            def _():
                where = pl.ds(0, TILE)
                pltpu.make_async_copy(staged.at[k], x_ref.at[:, where, :], sem.at[k]).wait()


def lookup(n_local, rows, table, frozen, flat, frow):
    block, width = table.shape
    span = 512
    steps = pl.cdiv(block, span)
    cap = flat.shape[0] * TILE
    n_rows = frow.shape[0]
    bf16 = jnp.bfloat16
    whole = lambda shape: pl.BlockSpec(shape, lambda i: (0,) * len(shape))
    smem = pl.BlockSpec(memory_space=pltpu.SMEM)
    return pl.pallas_call(
        functools.partial(lookup_kernel, block, span),
        grid=(steps,),
        out_shape=[
            jax.ShapeDtypeStruct((steps * span, width), bf16),
            jax.ShapeDtypeStruct((2, n_rows, width), bf16),
            jax.ShapeDtypeStruct((2, cap, width), bf16),
        ],
        in_specs=[
            smem,
            smem,
            pl.BlockSpec((span, width), lambda i: (i, 0)),
            pl.BlockSpec((span, width), lambda i: (i, 0)),
            whole(flat.shape),
            whole(frow.shape),
        ],
        out_specs=[
            pl.BlockSpec((span, width), lambda i: (i, 0)),
            whole((2, n_rows, width)),
            pl.BlockSpec(memory_space=pl.ANY),
        ],
        scratch_shapes=[
            pltpu.VMEM((2, steps * span, width), jnp.float32),
            pltpu.VMEM((2, TILE, width), jnp.float32),
            pltpu.VMEM((2, 2, TILE, width), bf16),
            pltpu.SemaphoreType.DMA((2,)),
        ],
        compiler_params=pltpu.CompilerParams(vmem_limit_bytes=60 * 2**20),
        name="lookup",
    )(n_local, rows, table, frozen, flat, frow)


def head_pieces(both, lane):
    turned = pltpu.roll(both, 64, 1)
    low, high = lane < 64, lane >= 64
    bf16 = jnp.bfloat16
    zero = jnp.zeros_like(both)
    return (
        jnp.where(low, both, zero).astype(bf16),
        jnp.where(high, turned, zero).astype(bf16),
        jnp.where(low, turned, zero).astype(bf16),
        jnp.where(high, both, zero).astype(bf16),
    )


def turn(values, positions, freq, lane, sign):
    angle = positions * freq
    cosine, sine = jnp.cos(angle), jnp.sin(angle)
    first = lax.rem(lane, 64) < 32
    mixed = jnp.where(first, -sign * pltpu.roll(values, 96, 1), sign * pltpu.roll(values, 32, 1))
    return values * cosine + mixed * sine


def allowed_of(frow, flat, r, length):
    flat = jnp.broadcast_to(flat, frow.shape)
    return jnp.where((flat <= frow) & (flat >= r * length), 1.0, 0.0)


def attend_kernel(
    length, rp, n_ref, lo_ref, hi_ref, q_ref, x_ref, w_ref, gain_ref, bias_ref, freq_ref, frow_ref, flat_ref, pos_ref,
    o_ref, st_ref, kv_ref, xbuf, kvbuf, m_scr, l_scr, o_scr, sem,
):
    model = pl.program_id(0)
    f32, bf16 = jnp.float32, jnp.bfloat16
    lane = lax.broadcasted_iota(jnp.int32, (TILE, 128), 1)
    lane_r = lax.broadcasted_iota(jnp.int32, (rp, 128), 1)
    m_scr[...] = jnp.full(m_scr.shape, -1e30, f32)
    l_scr[...] = jnp.zeros_like(l_scr)
    o_scr[...] = jnp.zeros_like(o_scr)

    tiles = (n_ref[0] + TILE - 1) // TILE

    def fetch(i):
        slot = lax.rem(i, 2)
        at = pl.ds(pl.multiple_of(i * TILE, TILE), TILE)
        return pltpu.make_async_copy(x_ref.at[model, at, :], xbuf.at[slot], sem.at[slot])

    @pl.when(tiles > 0)
    def _():
        fetch(0).start()

    def tile(i, _):
        at = pl.ds(pl.multiple_of(i * TILE, TILE), TILE)

        @pl.when(i + 1 < tiles)
        def _():
            fetch(i + 1).start()

        fetch(i).wait()
        x = xbuf[lax.rem(i, 2)].astype(f32)
        scale = lax.rsqrt(jnp.mean(x * x, axis=-1, keepdims=True) + EPS_NORM)
        normed = (x * scale * gain_ref[0]).astype(bf16)
        mixed = straight(normed, w_ref[...]) + bias_ref[0]
        key = turn(mixed[:, :128], column(pos_ref[pl.ds(i, 1), :]), freq_ref[...], lane, 1.0)
        key = key.astype(bf16)
        value = mixed[:, 128:].astype(bf16)
        kvbuf[...] = jnp.concatenate([key, value], axis=1)
        out = pltpu.make_async_copy(kvbuf, kv_ref.at[model, at, :], sem.at[2])
        out.start()
        keys = head_pieces(key.astype(f32), lane)
        values = head_pieces(value.astype(f32), lane)
        one = jnp.ones((TILE, 128), bf16)
        values = tuple(jnp.where((lane < 64) == (c % 2 == 0), v, one) for c, v in enumerate(values))
        flat = flat_ref[pl.ds(i, 1), :]

        def rollout(r, _):
            rows = pl.ds(pl.multiple_of(r * rp, rp), rp)
            ok = allowed_of(frow_ref[rows, :], flat, r, length)[None]
            shift = (ok - 1.0) * 1e30
            falls, adds = {}, {}
            for c, (p0, p1, s0) in enumerate(COMBOS):
                n = p1 - p0
                query = q_ref[p0:p1, rows, :].reshape(n * rp, 128)
                score = last_last(query, keys[c]).reshape(n, rp, TILE) * HEAD_SIZE ** (-0.5)
                score = score * ok + shift
                old = m_scr[s0 : s0 + n, rows, :]
                new = jnp.maximum(old, jnp.max(score, axis=-1, keepdims=True))
                m_scr[s0 : s0 + n, rows, :] = new
                fall = old - new
                prob = jnp.exp(score - new) * ok
                add = straight(prob.astype(bf16).reshape(n * rp, TILE), values[c]).reshape(n, rp, 128)
                for k in range(n):
                    falls[p0 + k, c % 2] = fall[k]
                    adds[p0 + k, c % 2] = add[k]
            for p in range(PAIRS):
                alpha = jnp.exp(jnp.where(lane_r < 64, falls[p, 0], falls[p, 1]))
                turned = pltpu.roll(alpha, 64, 1)
                o_scr[p, rows, :] = o_scr[p, rows, :] * alpha + jnp.where(lane_r < 64, adds[p, 0], adds[p, 1])
                l_scr[p, rows, :] = l_scr[p, rows, :] * turned + jnp.where(lane_r < 64, adds[p, 1], adds[p, 0])
            return 0

        lax.fori_loop(lo_ref[i], hi_ref[i] + 1, rollout, 0)
        out.wait()
        return 0

    lax.fori_loop(0, tiles, tile, 0)

    def leave(r, _):
        rows = pl.ds(pl.multiple_of(r * rp, rp), rp)
        o_ref[:, rows, :] = o_scr[:, rows, :].astype(bf16)
        packed = jnp.where(model == 0, jnp.zeros((rp, 128), f32), st_ref[0, rows, :])
        for slot, head in enumerate(HEAD_SLOTS):
            held = l_scr[head // 2, rows, :]
            held = held[:, 64:65] if head % 2 == 0 else held[:, 0:1]
            packed = jnp.where(lane_r == head + 32 * model, m_scr[slot, rows, :], packed)
            packed = jnp.where(lane_r == 16 + head + 32 * model, held, packed)
        st_ref[0, rows, :] = packed
        return 0

    lax.fori_loop(0, m_scr.shape[1] // rp, leave, 0)


def attend(n_local, lo, hi, q, x, w, gain, bias, freq, frow, flat, pos, length, rp):
    n_rows = q.shape[1]
    width = x.shape[2]
    cap = x.shape[1]
    bf16 = jnp.bfloat16
    whole = lambda shape: pl.BlockSpec(shape, lambda i: (0,) * len(shape))
    smem = pl.BlockSpec(memory_space=pltpu.SMEM)
    anyw = pl.BlockSpec(memory_space=pl.ANY)
    model = lambda shape: pl.BlockSpec(shape, lambda i: (i, 0, 0))
    return pl.pallas_call(
        functools.partial(attend_kernel, length, rp),
        grid=(2,),
        out_shape=[
            jax.ShapeDtypeStruct((2 * PAIRS, n_rows, 128), bf16),
            jax.ShapeDtypeStruct((1, n_rows, 128), jnp.float32),
            jax.ShapeDtypeStruct((2, cap, 256), bf16),
        ],
        in_specs=[
            smem, smem, smem, model((PAIRS, n_rows, 128)), anyw, pl.BlockSpec((width, 256), lambda i: (0, i)), model((1, 1, width)),
            model((1, 1, 256)), whole((1, 128)), whole(frow.shape), whole(flat.shape), whole(pos.shape),
        ],
        out_specs=[model((PAIRS, n_rows, 128)), whole((1, n_rows, 128)), anyw],
        scratch_shapes=[
            pltpu.VMEM((2, TILE, width), bf16),
            pltpu.VMEM((TILE, 256), bf16),
            pltpu.VMEM((QUERY_HEADS, n_rows, 128), jnp.float32),
            pltpu.VMEM((PAIRS, n_rows, 128), jnp.float32),
            pltpu.VMEM((PAIRS, n_rows, 128), jnp.float32),
            pltpu.SemaphoreType.DMA((3,)),
        ],
        compiler_params=pltpu.CompilerParams(vmem_limit_bytes=62 * 2**20),
        name="attend",
    )(n_local, lo, hi, q, x, w, gain, bias, freq, frow, flat, pos)


def attend_back_kernel(
    length, rp, n_ref, lo_ref, hi_ref, q_ref, do_ref, st_ref, x_ref, kv_ref, w_ref, gain_ref, freq_ref, frow_ref, flat_ref,
    pos_ref, dq_ref, gkv_ref, gs_ref, gb_ref, dx_ref, xbuf, kvbuf, dxbuf, dq_scr, dk_scr, dv_scr, sem,
):
    f32, bf16 = jnp.float32, jnp.bfloat16
    lane = lax.broadcasted_iota(jnp.int32, (TILE, 128), 1)
    dq_scr[...] = jnp.zeros_like(dq_scr)
    gkv_ref[...] = jnp.zeros_like(gkv_ref)
    gs_ref[...] = jnp.zeros_like(gs_ref)
    gb_ref[...] = jnp.zeros_like(gb_ref)

    tiles = (n_ref[0] + TILE - 1) // TILE

    def fetch(i):
        slot = lax.rem(i, 2)
        at = pl.ds(pl.multiple_of(i * TILE, TILE), TILE)
        return (
            pltpu.make_async_copy(x_ref.at[0, at, :], xbuf.at[slot], sem.at[slot]),
            pltpu.make_async_copy(kv_ref.at[0, at, :], kvbuf.at[slot], sem.at[2 + slot]),
        )

    def leave(i):
        slot = lax.rem(i, 2)
        at = pl.ds(pl.multiple_of(i * TILE, TILE), TILE)
        return pltpu.make_async_copy(dxbuf.at[slot], dx_ref.at[at, :], sem.at[4 + slot])

    @pl.when(tiles > 0)
    def _():
        for copy in fetch(0):
            copy.start()

    def tile(i, _):
        slot = lax.rem(i, 2)

        @pl.when(i + 1 < tiles)
        def _():
            for copy in fetch(i + 1):
                copy.start()

        for copy in fetch(i):
            copy.wait()
        keys = head_pieces(kvbuf[slot, :, :128].astype(f32), lane)
        values = head_pieces(kvbuf[slot, :, 128:].astype(f32), lane)
        flat = flat_ref[pl.ds(i, 1), :]
        dk_scr[...] = jnp.zeros_like(dk_scr)
        dv_scr[...] = jnp.zeros_like(dv_scr)

        def rollout(r, _):
            rows = pl.ds(pl.multiple_of(r * rp, rp), rp)
            ok = allowed_of(frow_ref[rows, :], flat, r, length)[None]
            shift = (ok - 1.0) * 1e30
            stats = st_ref[rows, :]
            adds = {}
            for c, (p0, p1, s0) in enumerate(COMBOS):
                n = p1 - p0
                heads = HEAD_SLOTS[s0 : s0 + n]
                query = q_ref[p0:p1, rows, :].reshape(n * rp, 128)
                back = do_ref[p0:p1, rows, :].reshape(n * rp, 128)
                lse = jnp.stack([stats[:, h : h + 1] for h in heads])
                delta = jnp.stack([stats[:, 16 + h : 17 + h] for h in heads])
                score = last_last(query, keys[c]).reshape(n, rp, TILE) * HEAD_SIZE ** (-0.5)
                prob = jnp.exp(score * ok + shift - lse)
                d_prob = last_last(back, values[c]).reshape(n, rp, TILE)
                d_score = (prob * (d_prob - delta)).astype(bf16).reshape(n * rp, TILE)
                add = straight(d_score, keys[c]).reshape(n, rp, 128)
                dk_scr[c] += first_first(d_score, query)
                dv_scr[c] += first_first(prob.astype(bf16).reshape(n * rp, TILE), back)
                for k in range(n):
                    adds[p0 + k, c % 2] = add[k]
            for p in range(PAIRS):
                dq_scr[p, rows, :] = dq_scr[p, rows, :] + adds[p, 0] + adds[p, 1]
            return 0

        lax.fori_loop(lo_ref[i], hi_ref[i] + 1, rollout, 0)

        def joined(scr):
            return jnp.where(lane < 64, scr[0] + pltpu.roll(scr[1], 64, 1), scr[3] + pltpu.roll(scr[2], 64, 1))

        d_key = turn(joined(dk_scr) * HEAD_SIZE ** (-0.5), column(pos_ref[pl.ds(i, 1), :]), freq_ref[...], lane, -1.0)
        d_mixed = jnp.concatenate([d_key, joined(dv_scr)], axis=1).astype(bf16)
        x = xbuf[slot].astype(f32)
        scale = lax.rsqrt(jnp.mean(x * x, axis=-1, keepdims=True) + EPS_NORM)
        gain = gain_ref[0]
        normed = (x * scale * gain).astype(bf16)
        gkv_ref[...] += first_first(normed, d_mixed)
        gb_ref[...] += jnp.sum(d_mixed.astype(f32).reshape(TILE // 8, 8, 256), axis=0)
        d_normed = last_last(d_mixed, w_ref[...])
        gs_ref[...] += jnp.sum((d_normed * x * scale).reshape(TILE // 8, 8, x.shape[1]), axis=0)
        d_hat = d_normed * gain
        d_x = scale * (d_hat - x * scale * scale * jnp.mean(d_hat * x, axis=-1, keepdims=True))

        @pl.when(i >= 2)
        def _():
            leave(i - 2).wait()

        dxbuf[slot] = d_x.astype(bf16)
        leave(i).start()
        return 0

    lax.fori_loop(0, tiles, tile, 0)
    for k in range(2):

        @pl.when(tiles > k)
        def _():
            leave(tiles - 1 - k).wait()

    dq_ref[...] = (dq_scr[...] * HEAD_SIZE ** (-0.5)).astype(bf16)


def attend_back(n_local, lo, hi, q, do, stats, x, kv, w, gain, freq, frow, flat, pos, length, rp):
    n_rows = do.shape[1]
    width = x.shape[2]
    cap = x.shape[1]
    bf16, f32 = jnp.bfloat16, jnp.float32
    whole = lambda shape: pl.BlockSpec(shape, lambda i: (0,) * len(shape))
    smem = pl.BlockSpec(memory_space=pltpu.SMEM)
    anyw = pl.BlockSpec(memory_space=pl.ANY)
    return pl.pallas_call(
        functools.partial(attend_back_kernel, length, rp),
        grid=(1,),
        out_shape=[
            jax.ShapeDtypeStruct((PAIRS, n_rows, 128), bf16),
            jax.ShapeDtypeStruct((width, 256), f32),
            jax.ShapeDtypeStruct((8, width), f32),
            jax.ShapeDtypeStruct((8, 256), f32),
            jax.ShapeDtypeStruct((cap, width), bf16),
        ],
        in_specs=[
            smem, smem, smem, whole((PAIRS, n_rows, 128)), whole((PAIRS, n_rows, 128)), whole((n_rows, 128)), anyw, anyw,
            whole((width, 256)), whole((1, 1, width)), whole((1, 128)), whole(frow.shape), whole(flat.shape),
            whole(pos.shape),
        ],
        out_specs=[
            whole((PAIRS, n_rows, 128)), whole((width, 256)), whole((8, width)), whole((8, 256)), anyw,
        ],
        scratch_shapes=[
            pltpu.VMEM((2, TILE, width), bf16),
            pltpu.VMEM((2, TILE, 256), bf16),
            pltpu.VMEM((2, TILE, width), bf16),
            pltpu.VMEM((PAIRS, n_rows, 128), f32),
            pltpu.VMEM((4, TILE, 128), f32),
            pltpu.VMEM((4, TILE, 128), f32),
            pltpu.SemaphoreType.DMA((6,)),
        ],
        compiler_params=pltpu.CompilerParams(vmem_limit_bytes=60 * 2**20),
        name="attend_back",
    )(n_local, lo, hi, q, do, stats, x, kv, w, gain, freq, frow, flat, pos)


def table_grad_kernel(
    span, n_ref, rows_ref, dl_ref, af_ref, drow_ref, frow_ref, flat_ref, dx_ref,
    g_ref, sq_ref, added, moved, rough, sem,
):
    step = pl.program_id(0)
    f32, bf16 = jnp.float32, jnp.bfloat16

    @pl.when(step == 0)
    def _():
        sq_ref[...] = jnp.zeros_like(sq_ref)
        added[...] = jnp.zeros_like(added)
        n_rows = drow_ref.shape[0]

        tiles = (n_ref[0] + TILE - 1) // TILE

        def fetch(i):
            slot = lax.rem(i, 2)
            at = pl.ds(pl.multiple_of(i * TILE, TILE), TILE)
            return pltpu.make_async_copy(dx_ref.at[at, :], moved.at[slot], sem.at[slot])

        @pl.when(tiles > 0)
        def _():
            fetch(0).start()

        def tile(i, _):
            @pl.when(i + 1 < tiles)
            def _():
                fetch(i + 1).start()

            token = column(flat_ref[pl.ds(i, 1), :])
            token = jnp.concatenate([token] * (n_rows // 128), axis=1)
            match = jnp.where(token == jnp.broadcast_to(frow_ref[...], (TILE, n_rows)), 1.0, 0.0).astype(bf16)
            own = straight(match, drow_ref[...])
            fetch(i).wait()
            rough[...] = own + moved[lax.rem(i, 2)].astype(f32)

            def eight(k, _):
                for j in range(8):
                    place = k * 8 + j
                    row = pl.ds(rows_ref[i * TILE + place], 1)
                    added[row, :] = added[row, :] + rough[pl.ds(place, 1), :]
                return 0

            lax.fori_loop(0, TILE // 8, eight, 0)
            return 0

        lax.fori_loop(0, tiles, tile, 0)

    total = straight(dl_ref[...], af_ref[0]) + added[pl.ds(pl.multiple_of(step * span, span), span), :]
    g_ref[...] = total.astype(bf16)
    square = total * total
    sq_ref[...] += jnp.sum(square.reshape(span // 8, 8, square.shape[1]), axis=0)


def table_grad(n_local, rows, dl, af, drow, frow, flat, dx, block):
    _, n_rows, width = af.shape
    span = wide(dl.shape[0])
    steps = dl.shape[0] // span
    whole = lambda shape: pl.BlockSpec(shape, lambda i: (0,) * len(shape))
    smem = pl.BlockSpec(memory_space=pltpu.SMEM)
    return pl.pallas_call(
        functools.partial(table_grad_kernel, span),
        grid=(steps,),
        out_shape=[
            jax.ShapeDtypeStruct((block, width), jnp.bfloat16),
            jax.ShapeDtypeStruct((8, width), jnp.float32),
        ],
        in_specs=[
            smem, smem,
            pl.BlockSpec((span, n_rows), lambda i: (i, 0)),
            whole((1, n_rows, width)), whole(drow.shape), whole(frow.shape), whole(flat.shape),
            pl.BlockSpec(memory_space=pl.ANY),
        ],
        out_specs=[pl.BlockSpec((span, width), lambda i: (i, 0)), whole((8, width))],
        scratch_shapes=[
            pltpu.VMEM((steps * span, width), jnp.float32),
            pltpu.VMEM((2, TILE, width), jnp.bfloat16),
            pltpu.VMEM((TILE, width), jnp.float32),
            pltpu.SemaphoreType.DMA((2,)),
        ],
        compiler_params=pltpu.CompilerParams(vmem_limit_bytes=56 * 2**20),
        name="table_grad",
    )(n_local, rows, dl, af, drow, frow, flat, dx)


def spread_kernel(own_ref, frozen_ref, out_ref):
    devices, _, _, wide = out_ref.shape
    units, rows = wide // 2, own_ref.shape[0]
    bf16 = jnp.bfloat16
    out_ref[...] = jnp.zeros_like(out_ref)
    for side in range(2):
        for d in range(devices):
            at = (side * devices + d) * units
            out_ref[d, 0, :rows, side * units : (side + 1) * units] = own_ref[:, at : at + units].astype(bf16)
            out_ref[d, 1, :rows, side * units : (side + 1) * units] = frozen_ref[:, at : at + units]


def spread(own, frozen, devices, units, rows_up):
    vm = pl.BlockSpec(memory_space=pltpu.VMEM)
    return pl.pallas_call(
        spread_kernel,
        out_shape=jax.ShapeDtypeStruct((devices, 2, rows_up, 2 * units), jnp.bfloat16),
        in_specs=[vm, vm],
        out_specs=vm,
        compiler_params=pltpu.CompilerParams(vmem_limit_bytes=48 * 2**20),
        name="spread",
    )(own, frozen)


def join_kernel(g_ref, out_ref):
    devices, _, wide = g_ref.shape
    units, rows = wide // 2, out_ref.shape[0]
    for side in range(2):
        for d in range(devices):
            at = (side * devices + d) * units
            out_ref[:, at : at + units] = g_ref[d, :rows, side * units : (side + 1) * units].astype(jnp.float32)


def join(g, rows, units):
    vm = pl.BlockSpec(memory_space=pltpu.VMEM)
    return pl.pallas_call(
        join_kernel,
        out_shape=jax.ShapeDtypeStruct((rows, 2 * units * g.shape[0]), jnp.float32),
        in_specs=[vm],
        out_specs=vm,
        compiler_params=pltpu.CompilerParams(vmem_limit_bytes=48 * 2**20),
        name="join",
    )(g)


def wide(rows):
    return 1024 if rows % 1024 == 0 else 512


def head_kernel(block, span, own_ref, frozen_ref, af_ref, aim_ref, st_ref, logit_ref):
    step = pl.program_id(0)
    f32 = jnp.float32
    n_rows = af_ref.shape[1]

    @pl.when(step == 0)
    def _():
        st_ref[...] = jnp.zeros_like(st_ref)
        for model in range(2):
            st_ref[3 * model : 3 * model + 1, :] = jnp.full((1, n_rows), -1e30, f32)

    inside = step * span + lax.broadcasted_iota(jnp.int32, (span, 1), 0) < block
    shift = jnp.where(inside, 0.0, -1e30)
    frozen = frozen_ref[...]
    frozen = jnp.where(jnp.broadcast_to(inside, frozen.shape), frozen, jnp.zeros_like(frozen))
    logits = [last_last(own_ref[...], af_ref[0]) + shift, last_last(frozen, af_ref[1]) + shift]
    logit_ref[...] = logits[0]
    hit = lax.broadcasted_iota(jnp.int32, (span, n_rows), 0) == aim_ref[...] - step * span
    for model, logit in enumerate(logits):
        top, total, found = (pl.ds(3 * model + k, 1) for k in range(3))
        new = jnp.maximum(st_ref[top, :], jnp.max(logit, axis=0, keepdims=True))
        fall = jnp.exp(st_ref[top, :] - new)
        st_ref[total, :] = st_ref[total, :] * fall + jnp.sum(jnp.exp(logit - new), axis=0, keepdims=True)
        st_ref[top, :] = new
        st_ref[found, :] += jnp.sum(jnp.where(hit, logit, 0.0), axis=0, keepdims=True)


def head(own, frozen, af, aim):
    rows, width = own.shape
    n_rows = af.shape[1]
    span = wide(rows)
    whole = lambda shape: pl.BlockSpec(shape, lambda i: (0,) * len(shape))
    return pl.pallas_call(
        functools.partial(head_kernel, frozen.shape[0], span),
        grid=(rows // span,),
        out_shape=[jax.ShapeDtypeStruct((8, n_rows), jnp.float32), jax.ShapeDtypeStruct((rows, n_rows), jnp.float32)],
        in_specs=[
            pl.BlockSpec((span, width), lambda i: (i, 0)), pl.BlockSpec((span, width), lambda i: (i, 0)),
            whole(af.shape), whole(aim.shape),
        ],
        out_specs=[whole((8, n_rows)), pl.BlockSpec((span, n_rows), lambda i: (i, 0))],
        compiler_params=pltpu.CompilerParams(vmem_limit_bytes=56 * 2**20),
        name="head",
    )(own, frozen, af, aim)


def head_back_kernel(logit_ref, own_ref, lse_ref, dlp_ref, aim_ref, dl_ref, d_af_ref, acc):
    step = pl.program_id(0)
    bf16 = jnp.bfloat16

    @pl.when(step == 0)
    def _():
        acc[...] = jnp.zeros_like(acc)

    place = lax.broadcasted_iota(jnp.int32, logit_ref.shape, 0)
    hot = jnp.where(place == aim_ref[...] - step * logit_ref.shape[0], 1.0, 0.0)
    d_logit = (dlp_ref[...] * (hot - jnp.exp(logit_ref[...] - lse_ref[...]))).astype(bf16)
    dl_ref[...] = d_logit
    acc[...] += first_first(d_logit, own_ref[...])

    @pl.when(step == pl.num_programs(0) - 1)
    def _():
        d_af_ref[0] = acc[...].astype(bf16)


def head_back(logits, own, lse, dlp, aim):
    rows, width = own.shape
    n_rows = logits.shape[1]
    span = wide(rows)
    whole = lambda shape: pl.BlockSpec(shape, lambda i: (0,) * len(shape))
    return pl.pallas_call(
        head_back_kernel,
        grid=(rows // span,),
        out_shape=[
            jax.ShapeDtypeStruct((rows, n_rows), jnp.bfloat16),
            jax.ShapeDtypeStruct((1, n_rows, width), jnp.bfloat16),
        ],
        in_specs=[
            pl.BlockSpec((span, n_rows), lambda i: (i, 0)), pl.BlockSpec((span, width), lambda i: (i, 0)),
            whole(lse.shape), whole(dlp.shape), whole(aim.shape),
        ],
        out_specs=[pl.BlockSpec((span, n_rows), lambda i: (i, 0)), whole((1, n_rows, width))],
        scratch_shapes=[pltpu.VMEM((n_rows, width), jnp.float32)],
        compiler_params=pltpu.CompilerParams(vmem_limit_bytes=56 * 2**20),
        name="head_back",
    )(logits, own, lse, dlp, aim)


def adam_step(w, g, m, v, clip):
    g = g.astype(jnp.float32) * clip
    m_new = MOM1 * m + (1.0 - MOM1) * g
    v_new = MOM2 * v + (1.0 - MOM2) * g * g
    update = m_new / (1.0 - MOM1**STEP) / (jnp.sqrt(v_new / (1.0 - MOM2**STEP)) + EPS_ADAM)
    return w - RATE * (update + DECAY * w), m_new, v_new, g


def blend(parts, lane):
    f32 = jnp.float32
    n_models = len(parts[0][0]) // PAIRS
    is_top = lax.rem(lane, 32) < 16
    stats = [p[1][0] for p in parts]
    top = stats[0]
    for s in stats[1:]:
        top = jnp.maximum(top, s)
    weights = [jnp.exp(jnp.where(is_top, s - top, 0.0)) for s in stats]
    total = sum(s * pltpu.roll(w, 16, 1) for s, w in zip(stats, weights))
    planes = []
    for model in range(n_models):
        for pair in range(PAIRS):
            at = 32 * model + 2 * pair
            acc = None
            for p, w in zip(parts, weights):
                each = jnp.where(lane < 64, w[:, at : at + 1], w[:, at + 1 : at + 2])
                term = p[0][model * PAIRS + pair].astype(f32) * each
                acc = term if acc is None else acc + term
            planes.append(acc)
    return planes, [jnp.where(is_top, top, total)]


def mix_phase(ins, outs, scr, send_sems, recv_sems, line, plane, other):
    (o_ref, st_ref), (oo_ref, so_ref) = ins, outs
    core_o, sum_o, plane_o, keep_o, line_o, core_s, sum_s, plane_s, keep_s, line_s = scr
    _, n_y, n_batch = places()
    half, y, core, batch = coords()
    n_plane = 2 * n_y
    spot = half * n_y + y
    size = oo_ref.shape[1]
    lane = lax.broadcasted_iota(jnp.int32, (size, 128), 1)
    order = list(range(1, n_batch)) + [0]
    spots = [to for _, to, _ in plane] + [spot]
    slots = iter(range(2 * (n_plane * n_batch + (n_plane - 1) * n_batch + n_batch - 1)))

    def send(src, dst, who):
        slot = next(slots)
        return push(src, dst, send_sems.at[slot], recv_sems.at[slot], who)

    def rows(side, where, j):
        at = (side * n_plane + where) * n_batch + lax.rem(batch + j, n_batch)
        return pl.ds(pl.multiple_of(at * size, size), size)

    def store(o, s, merged):
        for k, value in enumerate(merged[0]):
            o[k] = value.astype(o.dtype)
        for k, value in enumerate(merged[1]):
            s[k] = value

    by_core, by_plane, by_line = {}, {}, {}
    for j in order:
        for p in range(n_plane):
            at = rows(1 - core, spots[p], j)
            by_core[p, j] = (
                send(o_ref.at[:, at, :], core_o.at[p, j], other[0]), send(st_ref.at[:, at, :], core_s.at[p, j], other[0])
            )

    def mine(p, j):
        at = rows(core, spots[p], j)
        for copy in by_core[p, j]:
            copy.wait_recv()
        return blend([(o_ref[:, at, :], st_ref[:, at, :]), (core_o[p, j], core_s[p, j])], lane)

    for j in order:
        for p in range(n_plane - 1):
            store(sum_o.at[p, j], sum_s.at[p, j], mine(p, j))
            by_plane[p, j] = (
                send(sum_o.at[p, j], plane_o.at[p, j], plane[p][0]), send(sum_s.at[p, j], plane_s.at[p, j], plane[p][0])
            )
    for j in order:
        parts = [mine(n_plane - 1, j)]
        for p in range(n_plane - 1):
            for copy in by_plane[p, j]:
                copy.wait_recv()
            parts.append((plane_o[p, j], plane_s[p, j]))
        merged = blend(parts, lane)
        if j:
            store(keep_o.at[j - 1], keep_s.at[j - 1], merged)
            by_line[j] = (
                send(keep_o.at[j - 1], line_o.at[j - 1], line[j - 1][0]),
                send(keep_s.at[j - 1], line_s.at[j - 1], line[j - 1][0]),
            )
    parts = [merged]
    for j in range(1, n_batch):
        for copy in by_line[j]:
            copy.wait_recv()
        parts.append((line_o[j - 1], line_s[j - 1]))
    store(oo_ref, so_ref, blend(parts, lane))
    for group in (by_core, by_plane, by_line):
        for pair in group.values():
            for copy in pair:
                copy.wait_send()


def low(x):
    return x.astype(jnp.bfloat16)


def split_dot(x, w):
    high = low(x)
    return straight(high, w) + straight(low(x - high.astype(jnp.float32)), w)


def turn_rows(x, cosine, sine, sign):
    lane = lax.broadcasted_iota(jnp.int32, x.shape, 1)
    mixed = jnp.where(lax.rem(lane, 64) < 32, -sign * pltpu.roll(x, 96, 1), sign * pltpu.roll(x, 32, 1))
    return x * cosine + mixed * sine


def queries(totals, consts, staged, extras):
    w_one, w_two, places_ref, gain_ref, bias_ref, cosine_ref, sine_ref, x_ref = consts
    q_ref, a1_ref = staged
    for model, w_ref in enumerate((w_one, w_two)):
        normed, _ = norm_forward(x_ref[model], gain_ref[model])
        normed = low(normed)
        if model == 0:
            a1_ref[0] = normed
        mixed = straight(low(straight(normed, places_ref[...])), w_ref[...]) + bias_ref[model]
        for p in range(PAIRS):
            part = turn_rows(mixed[:, 128 * p : 128 * p + 128], cosine_ref[...], sine_ref[...], 1.0)
            q_ref[model * PAIRS + p] = low(part)


def attended(totals, consts, staged, extras):
    w_one, w_two, places_ref, gain_ref, x_ref = consts
    a2_ref, o_ref = staged
    x1_ref, own_ref, lse_ref = extras
    lane = lax.broadcasted_iota(jnp.int32, (own_ref.shape[0], 128), 1)
    for model, w_ref in enumerate((w_one, w_two)):
        stats = totals[1][0]
        if model == 0:
            total = jnp.where(lane < QUERY_HEADS, pltpu.roll(stats, 112, 1), 1.0)
            lse_ref[...] = stats + jnp.log(total)
        first = 32 * model + 16
        share = 1.0 / jnp.where((lane >= first) & (lane < first + QUERY_HEADS), stats, 1.0)
        parts = []
        for p in range(PAIRS):
            at = first + 2 * p
            each = jnp.where(lane < 64, share[:, at : at + 1], share[:, at + 1 : at + 2])
            parts.append(low(totals[0][model * PAIRS + p] * each))
        o = jnp.concatenate(parts, axis=1)
        if model == 0:
            o_ref[0] = o
            own_ref[...] = o
        x1 = x_ref[model] + straight(low(straight(o, places_ref[...])), w_ref[...])
        x1_ref[model] = x1
        a2, _ = norm_forward(x1, gain_ref[model])
        a2_ref[model] = low(straight(low(a2), places_ref[...]))


def finals(totals, consts, staged, extras):
    gain_ref, x1_ref = consts
    for model in range(2):
        x2 = x1_ref[model] + totals[0][model]
        extras[0][model] = x2
        af, _ = norm_forward(x2, gain_ref[model])
        staged[0][model] = low(af)


def scale_of(x):
    return lax.rsqrt(jnp.mean(x * x, axis=-1, keepdims=True) + EPS_NORM)


def finals_back(totals, consts, staged, extras):
    gain_ref, x2_ref = consts
    x2 = x2_ref[0]
    d_out, d_gain = norm_backward(totals[0][0], x2, scale_of(x2), gain_ref[0])
    staged[0][0] = low(d_out)
    extras[0][...] = d_out
    extras[1][...] = jnp.sum(d_gain, axis=0, keepdims=True)


def attended_back(totals, consts, staged, extras):
    w_ref, from_ref, gain_ref, x1_ref, d_out_ref, o_ref, lse_ref = consts
    d_attn_ref, d_o_ref, stats_ref = staged
    d_mid_ref, d_gain_ref = extras
    x1 = x1_ref[0]
    d_mid, d_gain = norm_backward(split_dot(totals[0][0], from_ref[...]), x1, scale_of(x1), gain_ref[0])
    d_mid = d_mid + d_out_ref[...]
    d_mid_ref[...] = d_mid
    d_gain_ref[...] = jnp.sum(d_gain, axis=0, keepdims=True)
    d_attn = low(d_mid)
    d_attn_ref[0] = d_attn
    d_o = low(straight(low(last_last(d_attn, w_ref[...])), from_ref[...]))
    product = d_o.astype(jnp.float32) * o_ref[...].astype(jnp.float32)
    lane = lax.broadcasted_iota(jnp.int32, (d_o.shape[0], 128), 1)
    stats = jnp.where(lane < QUERY_HEADS, lse_ref[...], 0.0)
    for p in range(PAIRS):
        d_o_ref[p] = d_o[:, 128 * p : 128 * p + 128]
        part = product[:, 128 * p : 128 * p + 128]
        first = jnp.sum(jnp.where(lane < 64, part, 0.0), axis=-1, keepdims=True)
        second = jnp.sum(jnp.where(lane < 64, 0.0, part), axis=-1, keepdims=True)
        stats = jnp.where(lane == 16 + 2 * p, first, stats)
        stats = jnp.where(lane == 17 + 2 * p, second, stats)
    stats_ref[0] = stats


def queries_back(totals, consts, staged, extras):
    w_ref, from_ref, gain_ref, x_ref, d_mid_ref, cosine_ref, sine_ref = consts
    dq_ref, d_row_ref = staged
    g_kv_ref, d_gain_ref, d_bias_ref = extras
    g_kv_ref[...] = totals[1][0]
    parts = [turn_rows(totals[0][p], cosine_ref[...], sine_ref[...], -1.0) for p in range(PAIRS)]
    dq = low(jnp.concatenate(parts, axis=1))
    dq_ref[0] = dq
    d_bias_ref[...] = jnp.sum(dq.astype(jnp.float32), axis=0, keepdims=True)
    x = x_ref[0]
    d_row, d_gain = norm_backward(split_dot(last_last(dq, w_ref[...]), from_ref[...]), x, scale_of(x), gain_ref[0])
    d_row_ref[0] = low(d_row + d_mid_ref[...])
    d_gain_ref[...] = jnp.sum(d_gain, axis=0, keepdims=True)


def keep(totals, consts, staged, extras):
    for total, extra in zip(totals, extras):
        extra[...] = total[...]


AXES = ("half", "mp", "batch")


def frequencies():
    half_size = HEAD_SIZE // 2
    return THETA ** (-(jnp.arange(half_size, dtype=jnp.float32) * 2.0) / HEAD_SIZE)


def bmm(x, w):
    return jnp.stack([jnp.dot(x[i], w[i], preferred_element_type=jnp.float32) for i in range(2)])


def body(
    tokens, lengths, labels, scored, qkv_weight, out_weight, gu_weight, down_weight, embed_weight, small_params,
    moment_qkv, moment_out, moment_gu, moment_down, moment_embed, moment_small,
    square_qkv, square_out, square_gu, square_down, square_embed, square_small,
    ref_qkv, ref_out, ref_gu, ref_down, ref_embed, ref_small,
):
    masters = (qkv_weight, out_weight, gu_weight, down_weight, embed_weight, small_params)
    firsts = (moment_qkv, moment_out, moment_gu, moment_down, moment_embed, moment_small)
    seconds = (square_qkv, square_out, square_gu, square_down, square_embed, square_small)
    bf16, f32, i32 = jnp.bfloat16, jnp.float32, jnp.int32
    n_mp, n_batch = lax.axis_size("mp"), lax.axis_size("batch")
    devices = 2 * n_mp * n_batch
    n_y = n_mp // 2
    block = embed_weight.shape[0]
    feats = qkv_weight.shape[0]
    units = down_weight.shape[0]
    rollouts = MICRO * n_batch
    length = n_mp * TOK
    rp = n_mp * P_SIZE
    n_rows = rollouts * rp
    own_rows = n_rows // devices
    lin = lax.axis_index(AXES)
    com = comm_index()
    base = lin * block

    feats_up = -(-feats // 16) * 16

    def to_up(x):
        return jnp.pad(x, ((0, feats_up - feats), (0, 0)))

    feat = jnp.arange(MODEL_WIDTH, dtype=i32)
    padded = jnp.arange(devices * feats_up, dtype=i32)
    to_order = (padded[None, :] == (feat // feats * feats_up + feat % feats)[:, None]).astype(bf16)
    owner = feat // feats
    mp_of = owner // n_batch % n_mp
    exchanged = ((mp_of % 2 * 2 + owner // (n_mp * n_batch)) * n_y + mp_of // 2) * n_batch + owner % n_batch
    to_exchange = (padded[:, None] == (exchanged * feats_up + feat % feats)[None, :]).astype(bf16)
    from_order = (padded[:, None] == (feat // feats * feats_up + feat % feats)[None, :]).astype(bf16)

    def placed(x):
        x = jnp.pad(x.astype(bf16), ((0, 0), (0, 128 - x.shape[1])))
        x = jnp.roll(x, lin * small_params.shape[1], axis=1)
        return jnp.pad(x, ((0, -x.shape[0] % feats_up), (0, 0)))

    qkv_low = qkv_weight.astype(bf16)
    early = to_up(
        jnp.concatenate(
            [qkv_low[:, :MODEL_WIDTH], ref_qkv[:, :MODEL_WIDTH], qkv_low[:, MODEL_WIDTH:], ref_qkv[:, MODEL_WIDTH:]], axis=1
        )
    )
    smalls = [placed(small_params), placed(ref_small)]
    tall = smalls[0].shape[0] // feats_up
    smalls = [x.reshape(tall, feats_up, 128)[k] for x in smalls for k in range(tall)]
    early = lax.all_gather(jnp.concatenate([early] + smalls, axis=1), AXES, axis=0, tiled=True)
    at_small = 2 * QKV
    down_low = jnp.stack([down_weight.astype(bf16), ref_down])

    ids = tokens.transpose(0, 2, 1, 3).reshape(rollouts, length)
    lens = lengths.reshape(rollouts)
    spots = jnp.arange(length, dtype=i32)
    flat_ids = jnp.arange(rollouts * length, dtype=i32).reshape(rollouts, length)
    bits = max(1, (block - 1).bit_length())
    local = (ids >= base) & (ids < base + block) & (spots[None, :] < lens[:, None])
    key = jnp.where(local, (flat_ids << bits) + (ids - base), jnp.int32(2**31 - 1)).reshape(-1)
    key = lax.sort(key, is_stable=False)
    n_local = jnp.sum(local.astype(i32))
    live = jnp.arange(rollouts * length, dtype=i32) < n_local
    row_of = jnp.where(live, key & ((1 << bits) - 1), 0)
    flat_of = jnp.where(live, key >> bits, 1 << 22).reshape(-1, TILE)
    pos_of = jnp.where(live, (key >> bits) % length, 0).reshape(-1, TILE).astype(f32)
    tile_lo = flat_of[:, 0] // length
    tile_hi = jnp.max(jnp.where(live, (key >> bits) // length, -1).reshape(-1, TILE), axis=1)
    n_one = n_local.reshape(1)

    picks = scored.transpose(0, 2, 1, 3) + (jnp.arange(n_mp, dtype=i32) * TOK)[None, None, :, None]
    picks = picks.reshape(rollouts, rp)
    valid = (picks + 1 < lens[:, None]).astype(f32)
    count = jnp.sum(valid)
    after = picks[:, :, None] + 1 == spots[None, None, :]
    targets = jnp.sum(jnp.where(after, ids[:, None, :], 0), axis=2).reshape(-1)
    frow = (picks + (jnp.arange(rollouts, dtype=i32) * length)[:, None]).reshape(-1)
    frow_wide = jnp.broadcast_to(frow[:, None], (n_rows, 128))

    low_table, picked, x_tok = lookup(n_one, row_of, embed_weight, ref_embed, flat_of, frow_wide)
    out_both = to_up(jnp.concatenate([out_weight.astype(bf16), ref_out], axis=1))
    picked, out_both = lax.optimization_barrier((picked, out_both))
    late = lax.all_gather(out_both, AXES, axis=0, tiled=True)
    row = (own_rows, MODEL_WIDTH)
    (x0,) = exchange("rows_found", 1, [picked], [], [], keep, [], [((2,) + row, f32)])

    x0, tile_lo, tile_hi, targets, valid, to_exchange, from_order, flat_of, pos_of = lax.optimization_barrier(
        (x0, tile_lo, tile_hi, targets, valid, to_exchange, from_order, flat_of, pos_of)
    )

    w_kv = jnp.dot(to_order, early[:, 2 * MODEL_WIDTH : at_small], preferred_element_type=f32).astype(bf16)
    small_rows = small_params.shape[0]
    flat_small = jnp.sum(early[:, at_small:].astype(f32).reshape(devices, feats_up, -1), axis=0)
    flat_small = flat_small.reshape(feats_up, 2, tall, 128).transpose(1, 2, 0, 3).reshape(2, tall * feats_up, 128)
    flat_small = flat_small[:, :small_rows].reshape(2, -1)
    gain_attn = flat_small[:, None, :MODEL_WIDTH]
    gain_mlp = flat_small[:, None, MODEL_WIDTH : 2 * MODEL_WIDTH]
    gain_final = flat_small[:, None, 2 * MODEL_WIDTH : 3 * MODEL_WIDTH]
    bias = flat_small[:, None, 3 * MODEL_WIDTH :]

    freq_wide = jnp.tile(frequencies(), 4).reshape(1, 128)
    my_pos = lax.dynamic_slice_in_dim(picks.reshape(-1), com * own_rows, own_rows)
    angle = my_pos.astype(f32)[:, None] * freq_wide
    cosine, sine = jnp.cos(angle), jnp.sin(angle)
    q_all, a1_all = exchange(
        "rows_queries", 2, [], [(early, 0, MODEL_WIDTH), (early, MODEL_WIDTH, MODEL_WIDTH)],
        [to_order, gain_attn, bias[:, :, :MODEL_WIDTH], cosine, sine, x0], queries,
        [(2 * PAIRS, own_rows, 128, bf16), (1,) + row + (bf16,)], [],
    )
    q_all, gu_sent = lax.optimization_barrier((q_all, spread(gu_weight, ref_gu, devices, units, feats_up)))
    gu_cols = lax.all_to_all(gu_sent, AXES, split_axis=0, concat_axis=0, tiled=True)
    w_gu = tuple(gu_cols[:, model].reshape(devices * feats_up, 2 * units) for model in range(2))

    o_part, st_part, kv_tok = attend(
        n_one, tile_lo, tile_hi, q_all, x_tok, w_kv, gain_attn, bias[:, :, MODEL_WIDTH:], freq_wide, frow_wide, flat_of,
        pos_of, length, rp,
    )
    o_part, late = lax.optimization_barrier((o_part, late))
    a2_all, o_all, x1, o_own, lse = exchange(
        "rows_attended", 3, [o_part, st_part], [(late, 0, MODEL_WIDTH), (late, MODEL_WIDTH, MODEL_WIDTH)],
        [to_order, gain_mlp, x0], attended,
        [(2, own_rows, devices * feats_up, bf16), (1,) + row + (bf16,)],
        [((2,) + row, f32), (row, bf16), ((own_rows, 128), f32)], mix_phase,
    )
    gate_up = bmm(a2_all, w_gu)
    gate, up = gate_up[:, :, :units], gate_up[:, :, units:]
    hidden = (jax.nn.silu(gate) * up).astype(bf16)
    af_all, x2 = exchange(
        "rows_finals", 5, [bmm(hidden, down_low).astype(bf16)], [], [gain_final, x1], finals, [(2,) + row + (bf16,)],
        [((2,) + row, f32)],
    )

    aim = jnp.where((targets >= base) & (targets < base + block), targets - base, -1).reshape(1, -1)
    stats, logits = head(low_table, ref_embed, af_all, aim)
    (stats_all,) = gather([stats[None]], 7)
    stats_all = stats_all.reshape(devices, 8, n_rows)
    lps, lses = [], []
    for i in range(2):
        peaks = stats_all[:, 3 * i]
        peak = jnp.max(peaks, axis=0)
        sums = jnp.sum(stats_all[:, 3 * i + 1] * jnp.exp(peaks - peak[None]), axis=0)
        lses.append(peak + jnp.log(sums))
        lps.append(jnp.sum(stats_all[:, 3 * i + 2], axis=0) - lses[i])
    ratio = (lps[0] - lps[1]).reshape(rollouts, rp)
    factor = BETA * n_rows / count
    reward = factor * jnp.sum(valid * ratio, axis=1)
    d_reward = (jax.nn.sigmoid(reward) - labels.reshape(rollouts).astype(f32)) / rollouts
    d_lp = (valid * (d_reward * factor)[:, None]).reshape(-1)

    d_logits, d_af = head_back(logits, low_table, lses[0].reshape(1, -1), d_lp.reshape(1, -1), aim)
    d_branch, d_out, g_gain_final = exchange(
        "rows_finals_back", 8, [d_af], [], [gain_final, x2], finals_back, [(1,) + row + (bf16,)],
        [(row, f32), ((1, MODEL_WIDTH), f32)],
    )
    d_branch = d_branch[0]
    g_down = lax.dot_general(hidden[0], d_branch, (((0,), (0,)), ((), ())), preferred_element_type=f32)
    d_hidden = lax.dot_general(d_branch, down_low[0], (((1,), (1,)), ((), ())), preferred_element_type=f32)
    sigma = jax.nn.sigmoid(gate[0])
    d_gate = d_hidden * up[0] * sigma * (1.0 + gate[0] * (1.0 - sigma))
    d_up = d_hidden * gate[0] * sigma
    d_gate_up = jnp.concatenate([d_gate, d_up], axis=1).astype(bf16)
    d_a2 = lax.dot_general(d_gate_up, w_gu[0], (((1,), (1,)), ((), ())), preferred_element_type=f32)
    d_attn_all, d_o_all, row_stats_all, d_mid, g_gain_mlp = exchange(
        "rows_attended_back", 10, [d_a2.astype(bf16)[None]], [(late, 0, MODEL_WIDTH)], [from_order, gain_mlp, x1, d_out, o_own, lse],
        attended_back, [(1,) + row + (bf16,), (PAIRS, own_rows, 128, bf16), (1, own_rows, 128, f32)],
        [(row, f32), ((1, MODEL_WIDTH), f32)],
    )
    d_attn_all = d_attn_all[0]

    g_gu = lax.dot_general(a2_all[0], d_gate_up, (((0,), (0,)), ((), ())), preferred_element_type=f32)
    gu_square = jnp.sum(g_gu * g_gu)
    g_gu = g_gu.astype(bf16).reshape(devices, feats_up, 2 * units)
    g_gu, d_o_all = lax.optimization_barrier((g_gu, d_o_all))
    g_gu = lax.all_to_all(g_gu, AXES, split_axis=0, concat_axis=0, tiled=True)
    dq_part, g_kv_part, g_gain_kv, g_bias_kv, dx_tok = attend_back(
        n_one, tile_lo, tile_hi, q_all, d_o_all, row_stats_all[0], x_tok, kv_tok, w_kv, gain_attn[:1],
        freq_wide, frow_wide, flat_of, pos_of, length, rp,
    )
    dq_part, g_gu = lax.optimization_barrier((dq_part, g_gu))
    g_kv_part = jnp.dot(to_exchange, g_kv_part.astype(bf16), preferred_element_type=f32).astype(bf16)
    dq_all, d_row_all, g_kv, g_gain_row, g_bias_q = exchange(
        "rows_queries_back", 12, [dq_part, g_kv_part[None]],
        [(early, 0, MODEL_WIDTH)], [from_order, gain_attn, x0, d_mid, cosine, sine], queries_back,
        [(1,) + row + (bf16,), (1,) + row + (bf16,)],
        [((feats_up, 256), f32), ((1, MODEL_WIDTH), f32), ((1, MODEL_WIDTH), f32)],
    )
    g_kv = g_kv[:feats]
    dq_all = dq_all[0]

    embed_grad, embed_square = table_grad(
        n_one, row_of, d_logits, af_all, d_row_all[0], frow.reshape(1, -1).astype(f32), flat_of, dx_tok, block
    )

    def mine(rows, grads):
        cols = lax.dynamic_slice_in_dim(rows, lin * feats, feats, 1)
        return lax.dot_general(cols, grads, (((0,), (0,)), ((), ())), preferred_element_type=f32)

    g_out = mine(o_all[0], d_attn_all)
    g_q = mine(a1_all[0], dq_all)
    g_qkv = jnp.concatenate([g_q, g_kv], axis=1)

    small_part = jnp.concatenate(
        [
            jnp.sum(g_gain_kv, axis=0) + g_gain_row[0],
            g_gain_mlp[0],
            g_gain_final[0],
            g_bias_q[0],
            jnp.sum(g_bias_kv, axis=0),
        ]
    )
    square_part = (
        jnp.sum(g_qkv * g_qkv) + jnp.sum(g_out * g_out) + gu_square + jnp.sum(g_down * g_down) + jnp.sum(embed_square)
    )
    last = jnp.concatenate([small_part, jnp.full((128,), square_part, f32), jnp.zeros((128,), f32)]).reshape(1, -1, 128)
    (last_all,) = gather([last], 14)
    last_all = jnp.sum(last_all.reshape(devices, -1, 128), axis=0)
    g_small = last_all[:small_rows]
    norm = jnp.sqrt(jnp.sum(g_small * g_small) + last_all[small_rows, 0])
    g_small = lax.dynamic_slice_in_dim(g_small, lin * small_params.shape[1], small_params.shape[1], 1)

    g_gu = join(g_gu, feats, units)
    owned_grads = (g_qkv, g_out, g_gu, g_down, embed_grad, g_small)
    clip = jnp.minimum(1.0, CLIP / (norm + 1e-06))
    new_weights, new_firsts, new_seconds, new_lows, clipped_list = ([], [], [], [], [])
    for w, g, m, v in zip(masters, owned_grads, firsts, seconds):
        w_new, m_new, v_new, g = adam_step(w, g, m, v, clip)
        w_low = w_new.astype(bf16)
        new_weights.append(w_new)
        new_firsts.append(m_new)
        new_seconds.append(v_new)
        clipped_list.append(g)
        new_lows.append(w_low)
    return (
        *new_weights[:5], clipped_list[5], *new_firsts, *new_seconds, *new_lows[:5], norm,
    )


def solution(mesh):
    rows, cols = P(AXES, None), P(None, AXES)
    six = (rows, rows, rows, rows, rows, cols)
    in_specs = (P(), P(), P(), P()) + six * 4
    out_specs = six * 3 + (rows,) * 5 + (P(),)
    return jax.shard_map(body, mesh=mesh, in_specs=in_specs, out_specs=out_specs, check_vma=False)
```
